32 devices in a mesh: pack: 2 (over y), blk: 16 (over z, x, core).
Axes of the slice: x: 2, y: 2, z: 4, core: 2. Of those that a mesh axis runs over, the one named last changes fastest.
Arguments:
- frames: bfloat16 [4096, 1024], P(('pack', 'blk')), may hold values from -6 to 6
- skip_input: bfloat16 [4096, 1024], P(('pack', 'blk')), may hold values from -6 to 6
- lengths: int32 [2, 4], P('pack'), may hold values from 1 to 1856, as said below
- w_skip: bfloat16 [2048, 1024], P('blk')
- b_skip: bfloat16 [1024], P('blk'), may hold values from -3 to 3
- g_attn: bfloat16 [1024], P('blk'), may hold values from 0.5 to 1.5
- w_qkv: bfloat16 [1024, 3072], P('blk'), may hold values from -0.1875 to 0.1875
- w_out: bfloat16 [1024, 1024], P('blk'), may hold values from -1.5 to 1.5
- g_ff: bfloat16 [1024], P('blk'), may hold values from 0.5 to 1.5
- w_up: bfloat16 [1024, 4096], P('blk'), may hold values from -0.1875 to 0.1875
- b_up: bfloat16 [4096], P('blk'), may hold values from -3 to 3
- w_down: bfloat16 [4096, 1024], P('blk'), may hold values from -0.09375 to 0.09375
- b_down: bfloat16 [1024], P('blk'), may hold values from -3 to 3
- out_grad: bfloat16 [4096, 1024], P(('pack', 'blk')), may hold values from -6 to 6
Outputs:
- layer_out: bfloat16 [4096, 1024], P(('pack', 'blk'))
- frames_grad: bfloat16 [4096, 1024], P(('pack', 'blk'))
- skip_grad: bfloat16 [4096, 1024], P(('pack', 'blk'))
- w_skip_grad: float32 [2048, 1024], P('blk')
- b_skip_grad: float32 [1024], P('blk')
- g_attn_grad: float32 [1024], P('blk')
- w_qkv_grad: float32 [1024, 3072], P('blk')
- w_out_grad: float32 [1024, 1024], P('blk')
- g_ff_grad: float32 [1024], P('blk')
- w_up_grad: float32 [1024, 4096], P('blk')
- b_up_grad: float32 [4096], P('blk')
- w_down_grad: float32 [4096, 1024], P('blk')
- b_down_grad: float32 [1024], P('blk')
The draws below stay inside these ranges and needn't reach their ends.
Inputs may be any that keep to these rules, and one draw needn't show every extreme that they name: Each row holds the 4 lengths of one pack in packing order and sums to 2048. One utterance, neither the first nor the last, at a place drawn from the seed, has 1856 frames; it starts within the first 128 frames of the pack and ends within the last 128. The other utterances together hold 192 frames, each fewer than 128.
All inputs are finite; a program needn't handle non-finite values.
Results may differ from the reference program's by a relative error of at most 0.018.
Values may be sent and summed in bfloat16 or wider, within the bound.
No kernel may reach another device: no remote copies, remote signals or barrier semaphores. Data moves between devices by JAX's collectives and lax.ppermute only.
A program may use at most 192 MiB of HBM per device.

```python
import math
import jax
import jax.numpy as jnp
from jax import lax

D = 1024
H = 16
HD = 64
FF = 4096
TOK_DEV = 128
NSEG = 4
FRAMES = 2048
PACKS = 2
TOKENS = 4096


def draw_lengths(key, part):
    key = jax.random.fold_in(key, 9)
    place_key, before_key, weight_key = jax.random.split(key, 3)
    columns = jnp.arange(NSEG, dtype=jnp.int32)[None, :]
    place = jax.random.randint(place_key, (PACKS, 1), 1, NSEG - 1).astype(jnp.int32)
    before_total = jax.random.randint(before_key, (PACKS, 1), TOK_DEV // 2 + 1, TOK_DEV).astype(jnp.int32)
    after_total = (TOK_DEV + TOK_DEV // 2 - before_total).astype(jnp.int32)
    weights = jax.random.randint(weight_key, (PACKS, NSEG), 1, 9).astype(jnp.int32)
    is_before = columns < place
    is_after = columns > place
    weight_before = jnp.where(is_before, weights, 0)
    weight_after = jnp.where(is_after, weights, 0)
    sum_before = jnp.sum(weight_before, 1, keepdims=True)
    sum_after = jnp.sum(weight_after, 1, keepdims=True)
    count_before = place
    count_after = NSEG - 1 - place
    share_before = jnp.where(is_before, 1 + (before_total - count_before) * weight_before // sum_before, 0)
    share_after = jnp.where(is_after, 1 + (after_total - count_after) * weight_after // sum_after, 0)
    rest_before = before_total - jnp.sum(share_before, 1, keepdims=True)
    rest_after = after_total - jnp.sum(share_after, 1, keepdims=True)
    share_before = share_before + jnp.where(columns == 0, rest_before, 0)
    share_after = share_after + jnp.where(columns == NSEG - 1, rest_after, 0)
    longest = FRAMES - 3 * TOK_DEV // 2
    result = share_before + share_after + jnp.where(columns == place, longest, 0)
    return result.astype(jnp.int32)


def draw_w_skip(key, part):
    key = jax.random.fold_in(key, 5)
    entry_key, scale_key = jax.random.split(key)
    entries = jax.random.normal(entry_key, (2 * D, D), jnp.float32)
    column = jnp.exp(jax.random.uniform(scale_key, (1, D), jnp.float32, math.log(0.3), math.log(3.0)))
    return (entries * column / math.sqrt(2 * D)).astype(jnp.bfloat16)


def raised(drawn, rng, source, target, blocks, factor):
    owner, partner = [(jnp.arange(drawn.shape[dim]) // (drawn.shape[dim] // blocks)).reshape([-1 if axis == dim else 1 for axis in range(drawn.ndim)]) for dim in (source, target)]
    chosen = jax.random.permutation(rng, blocks)[partner]
    strong = (owner == chosen) | (owner == (partner + blocks // 2) % blocks)
    return jnp.where(strong, factor * drawn, drawn)


def shard_levels(rng, dims, pieces, least, high):
    def one(dim, shards_of):
        heights = jax.random.uniform(jax.random.fold_in(jax.random.fold_in(rng, 6), dim), (shards_of,), jnp.float32, least / len(pieces), high / len(pieces))
        return jnp.repeat(jnp.exp(heights), dims[dim] // shards_of).reshape((-1,) + (1,) * (len(dims) - dim - 1))

    factor_of = one(*pieces[0])
    for cut in pieces[1:]:
        factor_of = factor_of * one(*cut)
    return factor_of


def bell_draw(rng, dims, spread, bound, pieces=(), kind=jnp.bfloat16):
    level = shard_levels(rng, dims, pieces, -0.22, 0.18) if pieces else 1.0
    values = jax.random.normal(rng, dims, jnp.float32) * spread * level
    return jnp.minimum(jnp.maximum(values, -bound), bound).astype(kind)


def heavy_noise(key, dims, deviation, bound, cuts, heavy, held_as=jnp.bfloat16):
    values = deviation * jax.random.normal(key, dims, jnp.float32)
    if cuts:
        values = values * shard_levels(key, dims, cuts, -0.22, 0.18)
    return jnp.clip(raised(values, jax.random.fold_in(key, 3), *heavy), -bound, bound).astype(held_as)


def setup_inputs(seed: int = 0) -> dict:
    keys = jax.random.split(jax.random.key(seed), 15)
    frames = heavy_noise(keys[0], (TOKENS, D), 1.0, 6.0, ((0, 32),), (0, 1, 32, 2.75))
    skip_input = heavy_noise(keys[1], (TOKENS, D), 1.0, 6.0, ((0, 32),), (0, 1, 32, 2.75))
    lengths = draw_lengths(jax.random.fold_in(keys[14], 71), 0)
    w_skip = draw_w_skip(jax.random.fold_in(keys[14], 71), 0)
    b_skip = bell_draw(keys[4], (D,), 0.5, 3.0, ((0, 16),))
    g_attn = jnp.clip(1.0 + 0.1 * jax.random.normal(keys[5], (D,), jnp.float32), 0.5, 1.5).astype(jnp.bfloat16)
    w_qkv = bell_draw(keys[6], (D, 3 * D), D ** -0.5, 0.1875, ((0, 16),))
    w_out = bell_draw(keys[7], (D, D), (D // 64) ** -0.5, 1.5, ((0, 16),))
    g_ff = jnp.clip(1.0 + 0.1 * jax.random.normal(keys[8], (D,), jnp.float32), 0.5, 1.5).astype(jnp.bfloat16)
    w_up = bell_draw(keys[9], (D, FF), D ** -0.5, 0.1875, ((0, 16),))
    b_up = bell_draw(keys[10], (FF,), 0.5, 3.0, ((0, 16),))
    w_down = bell_draw(keys[11], (FF, D), FF ** -0.5, 0.09375, ((0, 16),))
    b_down = bell_draw(keys[12], (D,), 0.5, 3.0, ((0, 16),))
    out_grad = heavy_noise(keys[13], (TOKENS, D), 1.0, 6.0, ((0, 32),), (0, 1, 32, 2.75))
    return dict(frames=frames, skip_input=skip_input, lengths=lengths, w_skip=w_skip, b_skip=b_skip, g_attn=g_attn, w_qkv=w_qkv, w_out=w_out, g_ff=g_ff, w_up=w_up, b_up=b_up, w_down=w_down, b_down=b_down, out_grad=out_grad)


@jax.custom_vjp
def low(v):
    return lax.optimization_barrier(v.astype(jnp.bfloat16)).astype(jnp.float32)

@jax.custom_vjp
def low_back(v):
    return v

def low_keep(v):
    return (low(v), None)

def low_pass(kept, grad):
    return (grad,)

def back_keep(v):
    return (v, None)

def back_low(kept, grad):
    return (low(grad),)
low.defvjp(low_keep, low_pass)
low_back.defvjp(back_keep, back_low)
EPSILON = 1e-06
MASKED_SCORE = -1e+30

def matmul_high(left, right):
    return jnp.dot(left, right, precision=lax.Precision.HIGHEST)

def normalize(stream, gain_vec):
    return stream * lax.rsqrt(lax.optimization_barrier(jnp.mean(stream * stream, -1, keepdims=True)) + EPSILON) * gain_vec

def rotate(tensor, offset, direction):
    half = tensor.shape[-1] // 2
    freq = 10000.0 ** (-(jnp.arange(half, dtype=jnp.float32) * 2.0 / tensor.shape[-1]))
    angle = offset.astype(jnp.float32)[:, None] * freq[None, :]
    cosine = jnp.cos(angle)[:, None, :]
    sine = direction * jnp.sin(angle)[:, None, :]
    first_half = tensor[..., :half]
    second_half = tensor[..., half:]
    return jnp.concatenate([first_half * cosine - second_half * sine, second_half * cosine + first_half * sine], -1)

def segment_of(position, lengths_row):
    bounds = jnp.cumsum(lengths_row).astype(jnp.int32)
    after = position[:, None] >= bounds[None, :]
    segment = lax.optimization_barrier(jnp.sum(after.astype(jnp.int32), 1, dtype=jnp.int32))
    before = lax.optimization_barrier(jnp.sum(jnp.where(after, lengths_row[None, :], 0), 1, dtype=jnp.int32))
    return (segment, (position - before).astype(jnp.int32))

def activation(value):
    return jax.nn.gelu(value, approximate=True)

def attend_pack(queries, keys_all, values_all, segment):
    query_rows = min(512, FRAMES)
    blocks = FRAMES // query_rows
    score_scale = 1.0 / math.sqrt(HD)

    @jax.checkpoint
    def block_attend(packed):
        query_block, segment_block = packed
        scores = jnp.einsum('qhd,khd->hqk', query_block, keys_all, precision=lax.Precision.HIGHEST) * score_scale
        scores = low_back(scores)
        allowed = (segment_block[:, None] == segment[None, :])[None]
        scores = jnp.where(allowed, scores, MASKED_SCORE)
        row_max = lax.optimization_barrier(jnp.max(scores, -1, keepdims=True))
        exponent = jnp.where(allowed, jnp.exp(scores - row_max), 0.0)
        softmax_w = low(exponent / lax.optimization_barrier(jnp.sum(exponent, -1, keepdims=True)))
        return jnp.einsum('hqk,khd->qhd', softmax_w, values_all, precision=lax.Precision.HIGHEST)
    result = lax.map(block_attend, (queries.reshape(blocks, query_rows, H, HD), segment.reshape(blocks, query_rows)))
    return result.reshape(FRAMES, H * HD)

def pack_layer(pack_frames, pack_skip, lengths_row, weights):
    w_skip, b_skip, g_attn, w_qkv, w_out, g_ff, w_up, b_up, w_down, b_down = weights
    position = jnp.arange(FRAMES, dtype=jnp.int32)
    segment, offset = segment_of(position, lengths_row)
    joined = jnp.concatenate([pack_frames, pack_skip], 1)
    stream_in = low_back(matmul_high(joined, w_skip) + b_skip)
    normed_attn = low(normalize(stream_in, g_attn))
    projected = low_back(matmul_high(normed_attn, w_qkv))
    queries = low(rotate(projected[:, :D].reshape(FRAMES, H, HD), offset, 1.0))
    keys_all = low(rotate(projected[:, D:2 * D].reshape(FRAMES, H, HD), offset, 1.0))
    values_all = low(projected[:, 2 * D:].reshape(FRAMES, H, HD))
    attn_low = low(low_back(attend_pack(queries, keys_all, values_all, segment)))
    stream_mid = stream_in + low_back(matmul_high(attn_low, w_out))
    normed_ff = low(normalize(stream_mid, g_ff))
    hidden_pre = low_back(matmul_high(normed_ff, w_up) + b_up)
    hidden_act = low(activation(hidden_pre))
    return stream_mid + matmul_high(hidden_act, w_down) + b_down

def whole_layer(inputs, lengths):
    frames_all = inputs[0].reshape(PACKS, FRAMES, D)
    skip_all = inputs[1].reshape(PACKS, FRAMES, D)
    weights = tuple(inputs[2:])
    checked = jax.checkpoint(pack_layer)

    def advance(running, packed):
        pack_frames, pack_skip, lengths_row = packed
        return (running, checked(pack_frames, pack_skip, lengths_row, weights))
    _, outputs = lax.scan(advance, jnp.zeros((), jnp.float32), (frames_all, skip_all, lengths))
    return outputs.reshape(TOKENS, D)

def reference(frames, skip_input, lengths, w_skip, b_skip, g_attn, w_qkv, w_out, g_ff, w_up, b_up, w_down, b_down, out_grad):
    floats = [array.astype(jnp.float32) for array in (frames, skip_input, w_skip, b_skip, g_attn, w_qkv, w_out, g_ff, w_up, b_up, w_down, b_down)]

    def forward(*inputs):
        return whole_layer(inputs, lengths)
    result, pullback = jax.vjp(forward, *floats)
    grads = pullback(out_grad.astype(jnp.float32))
    return (result.astype(jnp.bfloat16), grads[0].astype(jnp.bfloat16), grads[1].astype(jnp.bfloat16), grads[2], grads[3], grads[4], grads[5], grads[6], grads[7], grads[8], grads[9], grads[10], grads[11])
```

```python
import functools
import math

import jax
import jax.numpy as jnp
from jax import lax
from jax.experimental import pallas as pl
from jax.experimental.pallas import tpu as pltpu
from jax.sharding import PartitionSpec as P

H = 16
HD = 64
EPSILON = 1e-06
MASKED_SCORE = -1e30
ROWS = 128
VMEM = 56 * 1024 * 1024
BF = jnp.bfloat16
F32 = jnp.float32


def mm(left, right):
    return jnp.dot(left, right, preferred_element_type=F32)


def mm_nt(left, right):
    return lax.dot_general(left, right, (((1,), (1,)), ((), ())), preferred_element_type=F32)


def mm_tn(left, right):
    return lax.dot_general(left, right, (((0,), (0,)), ((), ())), preferred_element_type=F32)


def whole(shape):
    return pl.BlockSpec(shape, lambda *_: (0,) * len(shape))


def segment_of(position, lengths_row):
    bounds = jnp.cumsum(lengths_row)
    after = position[:, None] >= bounds[None, :]
    segment = jnp.sum(after.astype(jnp.int32), 1, dtype=jnp.int32)
    before = jnp.sum(jnp.where(after, lengths_row[None, :], 0), 1, dtype=jnp.int32)
    return segment, position - before


def angles(offset):
    freq = 10000.0 ** (-(jnp.arange(HD // 2, dtype=F32) * 2.0 / HD))
    angle = offset.astype(F32)[:, None] * freq[None, :]
    return jnp.cos(angle), jnp.sin(angle)


def activation(value):
    return jax.nn.gelu(value, approximate=True)


def pack_pair(block, lane_low):
    half = block.shape[0] // 2
    top, bottom = block[:half], block[half:]
    even = jnp.where(lane_low, top, pltpu.roll(bottom, HD, 1))
    odd = jnp.where(lane_low, pltpu.roll(top, HD, 1), bottom)
    return even, odd


def rope_pack_kernel(proj_ref, cos_ref, sin_ref, out_ref):
    rows = proj_ref.shape[0]
    lane = lax.broadcasted_iota(jnp.int32, (rows, 128), 1)
    first = (lane % HD) < HD // 2
    lane_low = lane[: rows // 2] < HD
    cosine, sine = cos_ref[...], sin_ref[...]
    for part in range(3):
        for pair in range(H // 2):
            at = (part * H + 2 * pair) * HD
            block = proj_ref[:, at : at + 128]
            if part < 2:
                swapped = jnp.where(first, pltpu.roll(block, 128 - HD // 2, 1), pltpu.roll(block, HD // 2, 1))
                block = block * cosine + swapped * sine
            block = block.astype(BF).astype(F32)
            if part == 0:
                block = block * (1.0 / math.sqrt(HD))
            even, odd = pack_pair(block, lane_low)
            out_ref[2 * pair, part] = even.astype(BF)
            out_ref[2 * pair + 1, part] = odd.astype(BF)


def rope_pack(proj, cos_pair, sin_pair):
    rows = proj.shape[0]
    return pl.pallas_call(
        rope_pack_kernel,
        out_shape=jax.ShapeDtypeStruct((H, 3, rows // 2, 128), BF),
        compiler_params=pltpu.CompilerParams(vmem_limit_bytes=VMEM),
        name="rope_pack",
    )(proj, cos_pair, sin_pair)


def pack_kernel(in_ref, out_ref):
    rows = in_ref.shape[0]
    lane_low = lax.broadcasted_iota(jnp.int32, (rows // 2, 128), 1) < HD
    for pair in range(H // 2):
        even, odd = pack_pair(in_ref[:, pair * 128 : pair * 128 + 128].astype(F32), lane_low)
        out_ref[2 * pair] = even.astype(BF)
        out_ref[2 * pair + 1] = odd.astype(BF)


def pack_heads(rows_all):
    return pl.pallas_call(
        pack_kernel,
        out_shape=jax.ShapeDtypeStruct((H, rows_all.shape[0] // 2, 128), BF),
        compiler_params=pltpu.CompilerParams(vmem_limit_bytes=VMEM),
        name="pack_heads",
    )(rows_all)


def unpack_kernel(in_ref, out_ref):
    parts, half = in_ref.shape[1], in_ref.shape[2]
    lane_low = lax.broadcasted_iota(jnp.int32, (half, 128), 1) < HD
    for part in range(parts):
        for pair in range(H // 2):
            even = in_ref[2 * pair, part].astype(F32)
            odd = in_ref[2 * pair + 1, part].astype(F32)
            top = jnp.where(lane_low, even, pltpu.roll(odd, HD, 1))
            bottom = jnp.where(lane_low, pltpu.roll(even, HD, 1), odd)
            at = (part * H + 2 * pair) * HD
            out_ref[:half, at : at + 128] = top.astype(BF)
            out_ref[half:, at : at + 128] = bottom.astype(BF)


def unpack_heads(packed):
    _, parts, half, _ = packed.shape
    return pl.pallas_call(
        unpack_kernel,
        out_shape=jax.ShapeDtypeStruct((2 * half, parts * H * HD), BF),
        compiler_params=pltpu.CompilerParams(vmem_limit_bytes=VMEM),
        name="unpack_heads",
    )(packed)


def unpack_all(src_ref, part, dst_ref, steps):
    half = src_ref.shape[-2]
    each = ROWS // half
    for g in range(steps):
        block = src_ref[g * each : (g + 1) * each, part].reshape(ROWS, 128).astype(F32)
        dst_ref[g * 2 * ROWS : g * 2 * ROWS + ROWS] = block[:, :HD].astype(dst_ref.dtype)
        dst_ref[g * 2 * ROWS + ROWS : (g + 1) * 2 * ROWS] = block[:, HD:].astype(dst_ref.dtype)


def attend_kernel(qkv_ref, segc_ref, segr_ref, out_ref, attn_ref, lse_ref, q_s, k_s, v_s, vt_s):
    g = pl.program_id(0)
    steps = pl.num_programs(0)
    half = qkv_ref.shape[-2]
    each = ROWS // half

    @pl.when(g == 0)
    def _():
        total = q_s.shape[0] // (2 * ROWS)
        unpack_all(qkv_ref, 0, q_s, total)
        unpack_all(qkv_ref, 1, k_s, total)
        unpack_all(qkv_ref, 2, v_s, total)
        vt_s[...] = jnp.transpose(v_s[...].astype(F32)).astype(BF)

    at = pl.multiple_of(g * 2 * ROWS, 2 * ROWS)
    scores = mm_nt(k_s[...], q_s[pl.ds(at, 2 * ROWS)])
    allowed = segc_ref[...] == segr_ref[:, pl.ds(at, 2 * ROWS)]
    scores = jnp.where(allowed, scores, MASKED_SCORE)
    top = jnp.max(scores, 0, keepdims=True)
    weight = jnp.exp(scores - top)
    total = jnp.sum(weight, 0, keepdims=True)
    attn_t = mm(vt_s[...], weight.astype(BF)) / total
    attn_ref[:, pl.ds(at, 2 * ROWS)] = attn_t
    lse_ref[:, pl.ds(at, 2 * ROWS)] = top + jnp.log(total)
    rows = jnp.transpose(attn_t)
    joined = jnp.concatenate([rows[:ROWS], rows[ROWS:]], 1).astype(BF)
    out_ref[pl.ds(g * each, each)] = joined.reshape(each, half, 128)


def attend(qkv, seg):
    blocks, _, half, _ = qkv.shape
    total = blocks * half * 2
    steps = total // (2 * ROWS)
    return pl.pallas_call(
        attend_kernel,
        grid=(steps,),
        in_specs=[whole(qkv.shape), whole((total, 1)), whole((1, total))],
        out_specs=[whole((blocks, half, 128)), whole((HD, total)), whole((1, total))],
        out_shape=[
            jax.ShapeDtypeStruct((blocks, half, 128), BF),
            jax.ShapeDtypeStruct((HD, total), F32),
            jax.ShapeDtypeStruct((1, total), F32),
        ],
        scratch_shapes=[
            pltpu.VMEM((total, HD), BF),
            pltpu.VMEM((total, HD), BF),
            pltpu.VMEM((total, HD), BF),
            pltpu.VMEM((HD, total), BF),
        ],
        compiler_params=pltpu.CompilerParams(vmem_limit_bytes=VMEM),
        name="attend",
    )(qkv, seg[:, None], seg[None, :])


def attend_back_kernel(
    qkv_ref, do_ref, attn_ref, lse_ref, segc_ref, segr_ref, cos_ref, sin_ref,
    out_ref, flat_ref,
    q_s, k_s, v_s, do_s, delta_s, dq_s,
):
    g = pl.program_id(0)
    steps = pl.num_programs(0)
    half = qkv_ref.shape[-2]
    each = ROWS // half
    scale = 1.0 / math.sqrt(HD)

    @pl.when(g == 0)
    def _():
        total = q_s.shape[0] // (2 * ROWS)
        unpack_all(qkv_ref, 0, q_s, total)
        unpack_all(qkv_ref, 1, k_s, total)
        unpack_all(qkv_ref, 2, v_s, total)
        unpack_all(do_ref, 0, do_s, total)
        do_t = jnp.transpose(do_s[...].astype(F32))
        delta_s[...] = jnp.sum(do_t * attn_ref[...], 0, keepdims=True)
        dq_s[...] = jnp.zeros_like(dq_s)

    at = pl.multiple_of(g * 2 * ROWS, 2 * ROWS)
    here = pl.ds(at, 2 * ROWS)
    keys = k_s[here]
    scores = mm_nt(keys, q_s[...])
    allowed = segc_ref[here] == segr_ref[...]
    probs = jnp.where(allowed, jnp.exp(scores - lse_ref[...]), 0.0)
    prob_grad = mm_nt(v_s[here], do_s[...])
    score_grad = (probs * (prob_grad - delta_s[...])).astype(BF)
    value_grad = mm(probs.astype(BF), do_s[...])
    key_grad = mm(score_grad, q_s[...])
    keys_t = jnp.transpose(keys.astype(F32)).astype(BF)
    dq_s[...] += mm(keys_t, score_grad)

    def unrotate(rows, where):
        swapped = jnp.concatenate([rows[:, HD // 2 :], rows[:, : HD // 2]], 1)
        return rows * cos_ref[where] + swapped * sin_ref[where]

    def put(part, step, rows):
        low = rows.astype(BF)
        flat_ref[part * HD : (part + 1) * HD, pl.ds(pl.multiple_of(step * 2 * ROWS, 2 * ROWS), 2 * ROWS)] = (
            jnp.transpose(rows).astype(BF)
        )
        joined = jnp.concatenate([low[:ROWS].astype(F32), low[ROWS:].astype(F32)], 1).astype(BF)
        out_ref[pl.ds(step * each, each), part] = joined.reshape(each, half, 128)

    put(1, g, unrotate(key_grad, here))
    put(2, g, value_grad)

    @pl.when(g == steps - 1)
    def _():
        for s in range(q_s.shape[0] // (2 * ROWS)):
            there = slice(s * 2 * ROWS, (s + 1) * 2 * ROWS)
            rows = jnp.transpose(dq_s[:, there]) * scale
            put(0, s, unrotate(rows, there))


def attend_back(qkv, attn_grad, attn_t, lse, seg, cos_rows, sin_rows):
    blocks, _, half, _ = qkv.shape
    total = blocks * half * 2
    steps = total // (2 * ROWS)
    return pl.pallas_call(
        attend_back_kernel,
        grid=(steps,),
        in_specs=[
            whole(qkv.shape), whole((blocks, 1, half, 128)), whole((HD, total)), whole((1, total)),
            whole((total, 1)), whole((1, total)), whole((total, HD)), whole((total, HD)),
        ],
        out_specs=[whole((blocks, 3, half, 128)), whole((3 * HD, total))],
        out_shape=[
            jax.ShapeDtypeStruct((blocks, 3, half, 128), BF),
            jax.ShapeDtypeStruct((3 * HD, total), BF),
        ],
        scratch_shapes=[
            pltpu.VMEM((total, HD), BF),
            pltpu.VMEM((total, HD), BF),
            pltpu.VMEM((total, HD), BF),
            pltpu.VMEM((total, HD), BF),
            pltpu.VMEM((1, total), F32),
            pltpu.VMEM((HD, total), F32),
        ],
        compiler_params=pltpu.CompilerParams(vmem_limit_bytes=VMEM),
        name="attend_back",
    )(qkv, attn_grad[:, None], attn_t, lse, seg[:, None], seg[None, :], cos_rows, sin_rows)


def local(
    frames, skip_input, lengths, w_skip, b_skip, g_attn, w_qkv, w_out, g_ff, w_up, b_up, w_down, b_down, out_grad
):
    tok, width = frames.shape
    blocks = lax.axis_size("blk")
    packs = lax.axis_size("pack")
    me = lax.axis_index("blk")
    mine = lax.axis_index("pack") % 2
    rows = width // blocks
    repeat = blocks // H
    half = tok // 2
    planes = 4
    plane = blocks // planes
    spot = me % plane
    place = me // plane
    plane_groups = [[z * plane + j for j in range(plane)] for z in range(planes)]
    column_groups = [[z * plane + j for z in range(planes)] for j in range(plane)]
    swap = [(i, i ^ 1) for i in range(packs)]

    def to_peer(block):
        return lax.ppermute(block, "pack", swap)

    def over_pairs(block):
        total = block
        for k in range(1, packs // 2):
            total = total + lax.ppermute(block, "pack", [(i, (i + 2 * k) % packs) for i in range(packs)])
        return total

    def all_to_all(block, groups=None):
        return lax.all_to_all(block, "blk", 0, 0, tiled=True, axis_index_groups=groups)

    vectors = jnp.stack([b_skip, g_attn, g_ff, b_down] + list(b_up.reshape(4, rows)), 0)
    vectors = jnp.transpose(jnp.pad(vectors, ((0, 120), (0, 0))))
    first_part = jnp.concatenate([w_skip[:rows], w_skip[rows:], w_qkv, vectors], 1)
    gathered = lax.all_gather(first_part, "blk", axis=0, tiled=True)
    up_cols = jnp.transpose(w_up.reshape(rows, blocks, 4, rows), (0, 2, 1, 3)).reshape(rows, 2, 2 * width)
    up_mine = lax.dynamic_index_in_dim(up_cols, mine, 1, keepdims=False)
    down_mine = lax.dynamic_slice_in_dim(w_down, mine * 2 * rows, 2 * rows, 0)
    second_part = jnp.concatenate([w_out, up_mine, down_mine[:rows], down_mine[rows:]], 1)
    gathered, second_part = lax.optimization_barrier((gathered, second_part))
    gathered_more = lax.all_gather(second_part, "blk", axis=0, tiled=True)
    skip_a, skip_b = gathered[:, :width], gathered[:, width : 2 * width]
    qkv_full = gathered[:, 2 * width : 5 * width]
    small = jnp.transpose(gathered[:, 5 * width :].astype(F32))[:8]
    bias_skip, gain_attn, gain_ff, bias_down = small[0], small[1], small[2], small[3]
    bias_up = lax.dynamic_slice_in_dim(small, 4 + 2 * mine, 2, 0).reshape(2 * width)

    pack_lengths = lengths[0]
    _, offset = segment_of(me * tok + jnp.arange(tok, dtype=jnp.int32), pack_lengths)
    cosine, sine = angles(offset)
    cos_pair = jnp.concatenate([cosine] * 4, 1)
    sin_pair = jnp.concatenate([-sine, sine, -sine, sine], 1)
    index = jnp.arange(tok * blocks, dtype=jnp.int32)
    packed_row = (index // (2 * ROWS)) * ROWS + index % ROWS
    lane_half = (index // ROWS) % 2
    token = (packed_row // half) * tok + lane_half * half + packed_row % half
    seg_all, offset_all = segment_of(token, pack_lengths)
    cos_all, sin_all = angles(offset_all)
    cos_rows = jnp.concatenate([cos_all, cos_all], 1)
    sin_rows = jnp.concatenate([sin_all, -sin_all], 1)

    joined = jnp.concatenate([frames, skip_input], 1)
    joined_split = joined.reshape(tok, planes, plane, 2 * rows)
    joined_share = all_to_all(
        jnp.transpose(joined_split, (2, 0, 1, 3)).reshape(plane, tok, planes * 2 * rows), plane_groups
    )
    grad_peer = to_peer(out_grad)
    out_grad_two = jnp.concatenate([out_grad, grad_peer], 0)

    by_piece = joined.reshape(tok, blocks, 2, rows)
    joined_a = by_piece[:, :, 0].reshape(tok, width)
    joined_b = by_piece[:, :, 1].reshape(tok, width)
    stream_in = mm(joined_a, skip_a) + mm(joined_b, skip_b) + bias_skip
    root_in = lax.rsqrt(jnp.mean(stream_in * stream_in, -1, keepdims=True) + EPSILON)
    unit_in = stream_in * root_in
    normed_attn = (unit_in * gain_attn).astype(BF)
    projected = mm(normed_attn, qkv_full)
    qkv_packed = rope_pack(projected, cos_pair, sin_pair)
    if repeat > 1:
        qkv_packed = jnp.repeat(qkv_packed, repeat, 0)
    qkv_head = all_to_all(qkv_packed)
    attn_packed, attn_t, lse = attend(qkv_head, seg_all)
    attn_back = all_to_all(attn_packed)[::repeat]
    attn_low = unpack_heads(attn_back[:, None])
    out_full = gathered_more[:, :width]
    up_half = gathered_more[:, width : 3 * width]
    down_a, down_b = gathered_more[:, 3 * width : 4 * width], gathered_more[:, 4 * width :]
    stream_mid = stream_in + mm(attn_low, out_full)
    root_mid = lax.rsqrt(jnp.mean(stream_mid * stream_mid, -1, keepdims=True) + EPSILON)
    unit_mid = stream_mid * root_mid
    normed_ff = (unit_mid * gain_ff).astype(BF)
    normed_two = jnp.concatenate([normed_ff, to_peer(normed_ff)], 0)
    hidden_pre = mm(normed_two, up_half) + bias_up
    act_grad = jnp.concatenate([mm_nt(out_grad_two, down_a), mm_nt(out_grad_two, down_b)], 1)
    hidden, gelu_back = jax.vjp(activation, hidden_pre)
    hidden_act = hidden.astype(BF)
    pre_grad = gelu_back(act_grad)[0].astype(BF)
    ff_grad_two = mm_nt(pre_grad, up_half)
    ff_grad = ff_grad_two[:tok] + to_peer(ff_grad_two[tok:].astype(BF)).astype(F32)
    ff_two = mm(hidden_act[:, :width], down_a) + mm(hidden_act[:, width:], down_b)
    layer_out = (
        stream_mid + (ff_two[:tok] + to_peer(ff_two[tok:].astype(BF)).astype(F32)) + bias_down
    ).astype(BF)

    scaled = ff_grad * gain_ff
    grad_gff = jnp.sum(ff_grad * unit_mid, 0)
    mid_grad = out_grad.astype(F32) + root_mid * (scaled - unit_mid * jnp.mean(scaled * unit_mid, -1, keepdims=True))
    branch_grad = mid_grad.astype(BF)
    attn_grad = pack_heads(mm_nt(branch_grad, out_full).astype(BF))
    if repeat > 1:
        attn_grad = jnp.repeat(attn_grad, repeat, 0)
    attn_grad_head = all_to_all(attn_grad)

    grad_up = mm_tn(normed_two, pre_grad)
    grad_down_a = mm_tn(hidden_act[:, :width], out_grad_two)
    grad_down_b = mm_tn(hidden_act[:, width:], out_grad_two)
    grad_out = mm_tn(attn_low, branch_grad)
    vec = jnp.concatenate(
        [
            grad_gff[None],
            jnp.sum(out_grad.astype(F32), 0)[None],
            jnp.sum(pre_grad.astype(F32), 0).reshape(2, width),
        ],
        0,
    )
    vec = jnp.transpose(jnp.pad(vec, ((0, 124), (0, 0)))).astype(BF)
    shares = lax.psum_scatter(
        jnp.concatenate(
            [grad_up.astype(BF), grad_down_a.astype(BF), grad_down_b.astype(BF), grad_out.astype(BF), vec], 1
        ),
        "blk",
        scatter_dimension=0,
        tiled=True,
    )
    if packs > 2:
        shares = over_pairs(shares.astype(F32)).astype(BF)
    others = to_peer(shares).astype(F32)
    shares = shares.astype(F32)

    def both(own, other):
        return jnp.where(mine == 0, jnp.stack([own, other]), jnp.stack([other, own]))

    up_pair = both(shares[:, : 2 * width], others[:, : 2 * width])
    up_pair = jnp.transpose(up_pair, (1, 0, 2)).reshape(rows, 4, blocks, rows)
    w_up_grad = jnp.transpose(up_pair, (0, 2, 1, 3)).reshape(rows, 4 * width)
    down_pair = both(shares[:, 2 * width : 4 * width], others[:, 2 * width : 4 * width])
    w_down_grad = jnp.transpose(down_pair.reshape(2, rows, 2, width), (0, 2, 1, 3)).reshape(4 * rows, width)
    w_out_grad = shares[:, 4 * width : 5 * width] + others[:, 4 * width : 5 * width]
    vec_own, vec_other = jnp.transpose(shares[:, 5 * width :]), jnp.transpose(others[:, 5 * width :])
    g_ff_grad = vec_own[0] + vec_other[0]
    b_down_grad = vec_own[1] + vec_other[1]
    b_up_grad = both(vec_own[2:4], vec_other[2:4]).reshape(4 * rows)

    normed_full = lax.all_gather(normed_attn, "blk", axis=0, tiled=True)
    dqkv_packed, dqkv_t = attend_back(qkv_head, attn_grad_head, attn_t, lse, seg_all, cos_rows, sin_rows)
    dqkv_back = all_to_all(dqkv_packed)[::repeat]
    projected_grad = unpack_heads(dqkv_back)
    normed_grad = mm_nt(projected_grad, qkv_full)
    scaled_in = normed_grad * gain_attn
    grad_gattn = jnp.sum(normed_grad * unit_in, 0)
    in_grad = mid_grad + root_in * (scaled_in - unit_in * jnp.mean(scaled_in * unit_in, -1, keepdims=True))
    in_low = in_grad.astype(BF)
    joined_grad_a = mm_nt(in_low, skip_a).astype(BF).reshape(tok, blocks, 1, rows)
    joined_grad_b = mm_nt(in_low, skip_b).astype(BF).reshape(tok, blocks, 1, rows)
    joined_grad = jnp.concatenate([joined_grad_a, joined_grad_b], 2).reshape(tok, 2 * width)
    frames_grad = joined_grad[:, :width]
    skip_grad = joined_grad[:, width:]

    normed_order = normed_full.reshape(blocks * half // ROWS, ROWS // half, 2, half, width)
    normed_order = jnp.transpose(normed_order, (0, 2, 1, 3, 4)).reshape(blocks * tok, width)
    qkv_grad_t = mm(dqkv_t, normed_order).astype(BF)
    side = 128 // rows
    folded = qkv_grad_t.reshape(side, 3 * HD // side, blocks, rows)
    folded = jnp.transpose(folded, (2, 1, 0, 3)).reshape(blocks, 3 * HD // side, 128)
    folded = all_to_all(folded)[::repeat]
    qkv_share = jnp.transpose(folded.reshape(H, 3 * HD // side, side, rows), (3, 2, 1, 0))
    qkv_share = qkv_share.reshape(rows, 3, HD, H)
    qkv_share = jnp.transpose(qkv_share, (0, 1, 3, 2)).reshape(rows, 3 * width)
    if packs > 2:
        qkv_share = over_pairs(qkv_share.astype(F32)).astype(BF)
    w_qkv_grad = qkv_share.astype(F32) + to_peer(qkv_share).astype(F32)

    extra = jnp.pad(grad_gattn[None].astype(BF), ((0, 15), (0, 0)))
    tail = jnp.concatenate([in_low, extra], 0)
    inner = plane // 2
    pieces = [tail]
    for k in range(1, inner):
        route = [
            (i, (i // plane) * plane + ((i % plane) // 2 + k) % inner * 2 + i % 2) for i in range(blocks)
        ]
        pieces.append(lax.ppermute(tail, "blk", route))
    column = jnp.stack(pieces)
    across = lax.ppermute(column, "blk", [(i, i ^ 1) for i in range(blocks)])
    tails = jnp.concatenate([column, across], 0)
    step = jnp.arange(inner, dtype=jnp.int32)
    from_spot = jnp.concatenate(
        [((spot // 2 - step) % inner) * 2 + spot % 2, ((spot // 2 - step) % inner) * 2 + 1 - spot % 2]
    )
    joined_in_order = jnp.concatenate(
        [lax.dynamic_index_in_dim(joined_share, from_spot[j], 0, keepdims=False) for j in range(plane)], 0
    )
    low_all = tails[:, :tok].reshape(plane * tok, width)
    skip_part = mm_tn(joined_in_order, low_all).astype(BF).reshape(planes, 2 * rows, width)
    vec_tail = jnp.stack(
        [jnp.sum(low_all.astype(F32), 0), jnp.sum(tails[:, tok].astype(F32), 0)] + [jnp.zeros((width,), F32)] * 14
    ).astype(BF)
    payload = jnp.concatenate([skip_part, jnp.broadcast_to(vec_tail[None], (planes, 16, width))], 1)
    arrived = all_to_all(payload, column_groups)
    summed = jnp.sum(arrived.astype(F32), 0)
    if packs > 2:
        summed = over_pairs(summed)
    total = summed + to_peer(summed.astype(BF)).astype(F32)
    w_skip_grad = total[: 2 * rows]
    own = lax.dynamic_slice_in_dim(total[2 * rows : 2 * rows + 2], me * rows, rows, 1)
    return (
        layer_out, frames_grad, skip_grad, w_skip_grad, own[0], own[1], w_qkv_grad, w_out_grad, g_ff_grad,
        w_up_grad, b_up_grad, w_down_grad, b_down_grad,
    )


def solution(mesh):
    token_spec = P(("pack", "blk"), None)
    matrix, vector = P("blk", None), P("blk")
    return jax.shard_map(
        local,
        mesh=mesh,
        in_specs=(
            token_spec, token_spec, P("pack", None), matrix, vector, vector, matrix, matrix, vector, matrix, vector,
            matrix, vector, token_spec,
        ),
        out_specs=(
            token_spec, token_spec, token_spec, matrix, vector, vector, matrix, matrix, vector, matrix, vector, matrix,
            vector,
        ),
        check_vma=False,
    )
```

```python
import functools
import math

import jax
import jax.numpy as jnp
from jax import lax
from jax.experimental import pallas as pl
from jax.experimental.pallas import tpu as pltpu
from jax.sharding import PartitionSpec as P

H = 16
HD = 64
EPSILON = 1e-06
MASKED_SCORE = -1e30
STEP = 256
VMEM = 56 * 1024 * 1024
BF = jnp.bfloat16
F32 = jnp.float32


def mm(left, right):
    return jnp.dot(left, right, preferred_element_type=F32)


def mm_nt(left, right):
    return lax.dot_general(left, right, (((1,), (1,)), ((), ())), preferred_element_type=F32)


def mm_tn(left, right):
    return lax.dot_general(left, right, (((0,), (0,)), ((), ())), preferred_element_type=F32)


def whole(shape):
    return pl.BlockSpec(shape, lambda *_: (0,) * len(shape))


def segment_of(position, lengths_row):
    bounds = jnp.cumsum(lengths_row)
    after = position[:, None] >= bounds[None, :]
    segment = jnp.sum(after.astype(jnp.int32), 1, dtype=jnp.int32)
    before = jnp.sum(jnp.where(after, lengths_row[None, :], 0), 1, dtype=jnp.int32)
    return segment, position - before


def angles(offset):
    freq = 10000.0 ** (-(jnp.arange(HD // 2, dtype=F32) * 2.0 / HD))
    angle = offset.astype(F32)[:, None] * freq[None, :]
    return jnp.cos(angle), jnp.sin(angle)


def activation(value):
    return jax.nn.gelu(value, approximate=True)


def pack_pair(block, lane_low):
    half = block.shape[0] // 2
    top, bottom = block[:half], block[half:]
    even = jnp.where(lane_low, top, pltpu.roll(bottom, HD, 1))
    odd = jnp.where(lane_low, pltpu.roll(top, HD, 1), bottom)
    return even, odd


def rope_pack_kernel(proj_ref, cos_ref, sin_ref, out_ref):
    rows = proj_ref.shape[0]
    lane = lax.broadcasted_iota(jnp.int32, (rows, 128), 1)
    first = (lane % HD) < HD // 2
    lane_low = lane[: rows // 2] < HD
    cosine, sine = cos_ref[...], sin_ref[...]
    for part in range(3):
        for pair in range(H // 2):
            at = (part * H + 2 * pair) * HD
            block = proj_ref[:, at : at + 128]
            if part < 2:
                swapped = jnp.where(first, pltpu.roll(block, 128 - HD // 2, 1), pltpu.roll(block, HD // 2, 1))
                block = block * cosine + swapped * sine
            block = block.astype(BF).astype(F32)
            if part == 0:
                block = block * (1.0 / math.sqrt(HD))
            even, odd = pack_pair(block, lane_low)
            out_ref[2 * pair, part] = even.astype(BF)
            out_ref[2 * pair + 1, part] = odd.astype(BF)


def rope_pack(proj, cos_pair, sin_pair):
    rows = proj.shape[0]
    return pl.pallas_call(
        rope_pack_kernel,
        out_shape=jax.ShapeDtypeStruct((H, 3, rows // 2, 128), BF),
        compiler_params=pltpu.CompilerParams(vmem_limit_bytes=VMEM),
        name="rope_pack",
    )(proj, cos_pair, sin_pair)


def pack_kernel(in_ref, out_ref):
    parts, half = out_ref.shape[1], out_ref.shape[2]
    lane_low = lax.broadcasted_iota(jnp.int32, (half, 128), 1) < HD
    for part in range(parts):
        for pair in range(H // 2):
            at = (part * H + 2 * pair) * HD
            even, odd = pack_pair(in_ref[:, at : at + 128].astype(F32), lane_low)
            out_ref[2 * pair, part] = even.astype(BF)
            out_ref[2 * pair + 1, part] = odd.astype(BF)


def pack_heads(rows_all):
    rows, columns = rows_all.shape
    return pl.pallas_call(
        pack_kernel,
        out_shape=jax.ShapeDtypeStruct((H, columns // (H * HD), rows // 2, 128), BF),
        compiler_params=pltpu.CompilerParams(vmem_limit_bytes=VMEM),
        name="pack_heads",
    )(rows_all)


def unpack_kernel(in_ref, out_ref):
    parts, half = in_ref.shape[1], in_ref.shape[2]
    lane_low = lax.broadcasted_iota(jnp.int32, (half, 128), 1) < HD
    for part in range(parts):
        for pair in range(H // 2):
            even = in_ref[2 * pair, part].astype(F32)
            odd = in_ref[2 * pair + 1, part].astype(F32)
            top = jnp.where(lane_low, even, pltpu.roll(odd, HD, 1))
            bottom = jnp.where(lane_low, pltpu.roll(even, HD, 1), odd)
            at = (part * H + 2 * pair) * HD
            out_ref[:half, at : at + 128] = top.astype(BF)
            out_ref[half:, at : at + 128] = bottom.astype(BF)


def unpack_heads(packed):
    _, parts, half, _ = packed.shape
    return pl.pallas_call(
        unpack_kernel,
        out_shape=jax.ShapeDtypeStruct((2 * half, parts * H * HD), BF),
        compiler_params=pltpu.CompilerParams(vmem_limit_bytes=VMEM),
        name="unpack_heads",
    )(packed)


def lanes(top, bottom):
    low = lax.broadcasted_iota(jnp.int32, top.shape, 1) < HD
    return jnp.where(low, top, pltpu.roll(bottom, HD, 1)), jnp.where(low, pltpu.roll(top, HD, 1), bottom)


def split_kernel(left_ref, right_ref, out_ref):
    pairs = left_ref.shape[1] // 256
    for half, ref in enumerate((left_ref, right_ref)):
        for pair in range(pairs):
            at = pair * 256
            first, second = lanes(ref[:, at : at + 128].astype(F32), ref[:, at + 128 : at + 256].astype(F32))
            there = (half * pairs + pair) * 128
            out_ref[0, :, there : there + 128] = first.astype(out_ref.dtype)
            out_ref[1, :, there : there + 128] = second.astype(out_ref.dtype)


def split_pieces(left, right, blocks):
    tok, width = left.shape
    if width // blocks != HD:
        by_piece = jnp.concatenate([left, right], 1).reshape(tok, blocks, 2, width // blocks)
        return jnp.transpose(by_piece, (2, 0, 1, 3)).reshape(2, tok, width)
    return pl.pallas_call(
        split_kernel,
        out_shape=jax.ShapeDtypeStruct((2, tok, width), left.dtype),
        compiler_params=pltpu.CompilerParams(vmem_limit_bytes=VMEM),
        name="split_pieces",
    )(left, right)


def merge_kernel(first_ref, second_ref, left_ref, right_ref):
    pairs = left_ref.shape[1] // 256
    for half, ref in enumerate((left_ref, right_ref)):
        for pair in range(pairs):
            there = (half * pairs + pair) * 128
            even, odd = lanes(
                first_ref[:, there : there + 128].astype(F32), second_ref[:, there : there + 128].astype(F32)
            )
            at = pair * 256
            ref[:, at : at + 128] = even.astype(ref.dtype)
            ref[:, at + 128 : at + 256] = odd.astype(ref.dtype)


def merge_pieces(first, second, blocks, dtype):
    tok, width = first.shape
    if width // blocks != HD:
        both = jnp.stack([first.reshape(tok, blocks, -1), second.reshape(tok, blocks, -1)], 2)
        both = both.reshape(tok, 2 * width).astype(dtype)
        return both[:, :width], both[:, width:]
    return pl.pallas_call(
        merge_kernel,
        out_shape=[jax.ShapeDtypeStruct((tok, width), dtype)] * 2,
        compiler_params=pltpu.CompilerParams(vmem_limit_bytes=VMEM),
        name="merge_pieces",
    )(first, second)


def up_kernel(mine_ref, own_ref, other_ref, out_ref):
    width = own_ref.shape[1] // 2
    first = mine_ref[0] == 0
    for piece in range(2):
        for pair in range(width // 128):
            at = pair * 128
            tiles = []
            for s in range(2):
                own = own_ref[:, s * width + at : s * width + at + 128].astype(F32)
                other = other_ref[:, s * width + at : s * width + at + 128].astype(F32)
                tiles.append(jnp.where(first, own, other) if piece == 0 else jnp.where(first, other, own))
            even, odd = lanes(*tiles)
            out_ref[:, (4 * pair + piece) * 128 : (4 * pair + piece + 1) * 128] = even
            out_ref[:, (4 * pair + 2 + piece) * 128 : (4 * pair + 3 + piece) * 128] = odd


def up_columns(mine, own, other, blocks):
    rows, half = own.shape
    if half // 2 // blocks != HD:
        pair = jnp.where(mine == 0, jnp.stack([own, other]), jnp.stack([other, own]))
        pair = jnp.transpose(pair, (1, 0, 2)).reshape(rows, 4, blocks, half // 2 // blocks)
        return jnp.transpose(pair, (0, 2, 1, 3)).reshape(rows, 2 * half).astype(F32)
    return pl.pallas_call(
        up_kernel,
        in_specs=[pl.BlockSpec(memory_space=pltpu.SMEM), whole((rows, half)), whole((rows, half))],
        out_specs=whole((rows, 2 * half)),
        out_shape=jax.ShapeDtypeStruct((rows, 2 * half), F32),
        compiler_params=pltpu.CompilerParams(vmem_limit_bytes=VMEM),
        name="up_columns",
    )(mine.astype(jnp.int32).reshape(1), own, other)


def rotated(rows, cosine, sine):
    swapped = jnp.concatenate([rows[:, HD // 2 :], rows[:, : HD // 2]], 1)
    return rows * cosine + swapped * sine


def put_packed(out_ref, step, rows, half, part=None):
    each = rows.shape[0] // (2 * half)
    for i in range(each):
        block = rows[2 * half * i : 2 * half * (i + 1)]
        joined = jnp.concatenate([block[:half], block[half:]], 1).astype(BF)
        if part is None:
            out_ref[step * each + i] = joined
        else:
            out_ref[step * each + i, part] = joined


def attend_kernel(qkv_ref, segc_ref, segr_ref, out_ref, attn_ref, lse_ref, q_ref, k_ref, v_ref, vt_s):
    g = pl.program_id(0)
    half = qkv_ref.shape[-2]
    tok = 2 * half

    @pl.when(g == 0)
    def _():
        for i in range(qkv_ref.shape[0]):
            for part, ref in enumerate((q_ref, k_ref, v_ref)):
                block = qkv_ref[i, part].astype(F32)
                ref[i * tok : i * tok + half] = block[:, :HD].astype(BF)
                ref[i * tok + half : (i + 1) * tok] = block[:, HD:].astype(BF)
        vt_s[...] = jnp.transpose(v_ref[...].astype(F32)).astype(BF)

    here = pl.ds(pl.multiple_of(g * STEP, STEP), STEP)
    scores = mm_nt(k_ref[...], q_ref[here])
    allowed = segc_ref[...] == segr_ref[:, here]
    scores = jnp.where(allowed, scores, MASKED_SCORE)
    top = jnp.max(scores, 0, keepdims=True)
    weight = jnp.exp(scores - top)
    total = jnp.sum(weight, 0, keepdims=True)
    attn_t = mm(vt_s[...], weight.astype(BF)) / total
    attn_ref[:, here] = attn_t
    lse_ref[:, here] = top + jnp.log(total)
    put_packed(out_ref, g, jnp.transpose(attn_t), tok // 2)


def attend(qkv, seg):
    blocks, _, half, _ = qkv.shape
    total = blocks * half * 2
    return pl.pallas_call(
        attend_kernel,
        grid=(total // STEP,),
        in_specs=[whole(qkv.shape), whole((total, 1)), whole((1, total))],
        out_specs=[whole((blocks, half, 128)), whole((HD, total)), whole((1, total))] + [whole((total, HD))] * 3,
        out_shape=[
            jax.ShapeDtypeStruct((blocks, half, 128), BF),
            jax.ShapeDtypeStruct((HD, total), F32),
            jax.ShapeDtypeStruct((1, total), F32),
        ]
        + [jax.ShapeDtypeStruct((total, HD), BF)] * 3,
        scratch_shapes=[pltpu.VMEM((HD, total), BF)],
        compiler_params=pltpu.CompilerParams(vmem_limit_bytes=VMEM),
        cost_estimate=pl.CostEstimate(flops=int(1.6e10), bytes_accessed=8 << 20, transcendentals=0),
        name="attend",
    )(qkv, seg[:, None], seg[None, :])


def attend_back_kernel(
    q_ref, k_ref, v_ref, do_ref, attn_ref, lse_ref, segc_ref, segr_ref, cos_ref, sin_ref, normed_ref,
    out_ref, grad_ref, do_s, delta_s, dq_s, flat_s,
):
    g = pl.program_id(0)
    blocks = do_ref.shape[0]
    half = do_ref.shape[-2]
    tok = 2 * half
    scale = 1.0 / math.sqrt(HD)

    @pl.when(g == 0)
    def _():
        for i in range(blocks):
            block = do_ref[i].astype(F32)
            do_s[i * tok : i * tok + half] = block[:, :HD].astype(BF)
            do_s[i * tok + half : (i + 1) * tok] = block[:, HD:].astype(BF)
        do_t = jnp.transpose(do_s[...].astype(F32))
        delta_s[...] = jnp.sum(do_t * attn_ref[...], 0, keepdims=True)
        dq_s[...] = jnp.zeros_like(dq_s)

    here = pl.ds(pl.multiple_of(g * STEP, STEP), STEP)
    keys = k_ref[here]
    scores = mm_nt(keys, q_ref[...])
    allowed = segc_ref[here] == segr_ref[...]
    probs = jnp.where(allowed, jnp.exp(scores - lse_ref[...]), 0.0)
    prob_grad = mm_nt(v_ref[here], do_s[...])
    score_grad = (probs * (prob_grad - delta_s[...])).astype(BF)
    value_grad = mm(probs.astype(BF), do_s[...])
    key_grad = mm(score_grad, q_ref[...])
    keys_t = jnp.transpose(keys.astype(F32)).astype(BF)
    dq_s[...] += mm(keys_t, score_grad)

    def put(part, step, rows, where):
        flat_s[part * HD : (part + 1) * HD, where] = jnp.transpose(rows).astype(BF)
        put_packed(out_ref, step, rows, half, part)

    put(1, g, rotated(key_grad, cos_ref[here], sin_ref[here]), here)
    put(2, g, value_grad, here)

    @pl.when(g == pl.num_programs(0) - 1)
    def _():
        for step in range(q_ref.shape[0] // STEP):
            there = slice(step * STEP, (step + 1) * STEP)
            rows = jnp.transpose(dq_s[:, there]) * scale
            put(0, step, rotated(rows, cos_ref[there], sin_ref[there]), there)
        grad = jnp.transpose(mm(flat_s[...], normed_ref[...]))
        rows = grad.shape[0] // blocks
        for i in range(blocks):
            for part in range(3):
                block = grad[i * rows : (i + 1) * rows, part * HD : (part + 1) * HD]
                grad_ref[i, part] = jnp.concatenate([block[: rows // 2], block[rows // 2 :]], 1).astype(BF)


def attend_back(normed, q, k, v, attn_grad, attn_t, lse, seg, cos_rows, sin_rows):
    total, width = normed.shape
    blocks, half, _ = attn_grad.shape
    rows = width // blocks
    return pl.pallas_call(
        attend_back_kernel,
        grid=(total // STEP,),
        in_specs=[whole((total, HD))] * 3
        + [whole((blocks, half, 128)), whole((HD, total)), whole((1, total))]
        + [whole((total, 1)), whole((1, total)), whole((total, HD)), whole((total, HD))]
        + [whole((total, width))],
        out_specs=[whole((blocks, 3, half, 128)), whole((blocks, 3, rows // 2, 128))],
        out_shape=[
            jax.ShapeDtypeStruct((blocks, 3, half, 128), BF),
            jax.ShapeDtypeStruct((blocks, 3, rows // 2, 128), BF),
        ],
        scratch_shapes=[
            pltpu.VMEM((total, HD), BF),
            pltpu.VMEM((1, total), F32),
            pltpu.VMEM((HD, total), F32),
            pltpu.VMEM((3 * HD, total), BF),
        ],
        compiler_params=pltpu.CompilerParams(vmem_limit_bytes=VMEM),
        cost_estimate=pl.CostEstimate(flops=int(2.4e10), bytes_accessed=8 << 20, transcendentals=0),
        name="attend_back",
    )(q, k, v, attn_grad, attn_t, lse, seg[:, None], seg[None, :], cos_rows, sin_rows, normed)


def local(
    frames, skip_input, lengths, w_skip, b_skip, g_attn, w_qkv, w_out, g_ff, w_up, b_up, w_down, b_down, out_grad
):
    tok, width = frames.shape
    blocks = lax.axis_size("blk")
    packs = lax.axis_size("pack")
    me = lax.axis_index("blk")
    mine = lax.axis_index("pack") % 2
    rows = width // blocks
    repeat = blocks // H
    half = tok // 2
    planes = 4
    plane = blocks // planes
    spot = me % plane
    place = me // plane
    plane_groups = [[z * plane + j for j in range(plane)] for z in range(planes)]
    column_groups = [[z * plane + j for z in range(planes)] for j in range(plane)]
    swap = [(i, i ^ 1) for i in range(packs)]

    def to_peer(block):
        return lax.ppermute(block, "pack", swap)

    def over_pairs(block):
        total = block
        for k in range(1, packs // 2):
            total = total + lax.ppermute(block, "pack", [(i, (i + 2 * k) % packs) for i in range(packs)])
        return total

    def all_to_all(block, groups=None):
        return lax.all_to_all(block, "blk", 0, 0, tiled=True, axis_index_groups=groups)

    inner = plane // 2
    core = [(i, i ^ 1) for i in range(blocks)]

    def along_z(k):
        return [(i, (i + plane * k) % blocks) for i in range(blocks)]

    def along_x(k):
        return [(i, (i // plane) * plane + ((i % plane) // 2 + k) % inner * 2 + i % 2) for i in range(blocks)]

    def send(block, route):
        return lax.ppermute(block, "blk", route)

    def plane_blocks(block, beside=()):
        column = [block] + [send(block, along_x(k)) for k in range(1, inner)]
        if inner > 1:
            column = jnp.stack(column)
        else:
            column = column[0][None]
        column, beside = lax.optimization_barrier((column, beside))
        return jnp.concatenate([column, send(column, core)], 0), beside

    def spot_order(j):
        return ((j % 2) ^ (spot % 2)) * inner + (spot // 2 - j // 2) % inner

    def own_half(block, axis):
        size = block.shape[axis] // 2
        return lax.dynamic_slice_in_dim(block, mine * size, size, axis)

    def at_index(block, index, axis=0):
        return lax.dynamic_index_in_dim(block, index, axis, keepdims=False)

    vectors = jnp.stack([b_skip, g_attn, g_ff, b_down] + list(b_up.reshape(4, rows)), 0)
    vectors = jnp.transpose(jnp.pad(vectors, ((0, 120), (0, 0))))
    up_cols = jnp.transpose(w_up.reshape(rows, blocks, 4, rows), (0, 2, 1, 3)).reshape(rows, 2, 2 * width)
    up_mine = at_index(up_cols, mine, 1)
    down_mine = own_half(w_down, 0)
    payload = jnp.concatenate(
        [w_skip[:rows], w_skip[rows:], w_qkv, w_out, up_mine, down_mine[:rows], down_mine[rows:], vectors], 1
    )
    gathered = lax.all_gather(payload, "blk", axis=0, tiled=True)

    pack_lengths = lengths[0]
    seg_all, offset_all = segment_of(jnp.arange(tok * blocks, dtype=jnp.int32), pack_lengths)
    cos_all, sin_all = angles(offset_all)
    cos_rows = jnp.concatenate([cos_all, cos_all], 1)
    sin_rows = jnp.concatenate([sin_all, -sin_all], 1)
    cosine = lax.dynamic_slice_in_dim(cos_all, me * tok, tok, 0)
    sine = lax.dynamic_slice_in_dim(sin_all, me * tok, tok, 0)
    cos_pair = jnp.concatenate([cosine] * 4, 1)
    sin_pair = jnp.concatenate([-sine, sine, -sine, sine], 1)
    out_grad_two = jnp.concatenate([out_grad, to_peer(out_grad)], 0)
    pieces = split_pieces(frames, skip_input, blocks)
    gathered, out_grad_two, pieces, cos_rows, sin_rows, cos_pair, sin_pair, seg_all = lax.optimization_barrier(
        (gathered, out_grad_two, pieces, cos_rows, sin_rows, cos_pair, sin_pair, seg_all)
    )
    skip_a, skip_b = gathered[:, :width], gathered[:, width : 2 * width]
    qkv_full = gathered[:, 2 * width : 5 * width]
    gathered_more = gathered[:, 5 * width :]
    small = jnp.transpose(gathered[:, 10 * width :].astype(F32))[:8]
    bias_skip, gain_attn, gain_ff, bias_down = small[0], small[1], small[2], small[3]
    bias_up = lax.dynamic_slice_in_dim(small, 4 + 2 * mine, 2, 0).reshape(2 * width)

    def over_core(grad):
        grad = grad.astype(BF).reshape(planes, inner, 2, rows, grad.shape[-1])
        return (at_index(grad, me % 2, 2).astype(F32) + send(at_index(grad, 1 - me % 2, 2), core).astype(F32)).astype(BF)

    def over_x(grad):
        total = at_index(grad, spot // 2, 1).astype(F32)
        for k in range(1, inner):
            total = total + send(at_index(grad, (spot // 2 + k) % inner, 1), along_x(k)).astype(F32)
        return total.astype(BF)

    def over_z(grad):
        total = lax.psum_scatter(
            grad.reshape(planes * grad.shape[1], grad.shape[2]),
            "blk",
            scatter_dimension=0,
            axis_index_groups=column_groups,
            tiled=True,
        )
        return over_pairs(total.astype(F32)).astype(BF) if packs > 2 else total

    def both(own, other):
        return jnp.where(mine == 0, jnp.stack([own, other]), jnp.stack([other, own]))

    stream_in = mm(pieces[0], skip_a) + mm(pieces[1], skip_b) + bias_skip
    root_in = lax.rsqrt(jnp.mean(stream_in * stream_in, -1, keepdims=True) + EPSILON)
    unit_in = stream_in * root_in
    normed_attn = (unit_in * gain_attn).astype(BF)
    normed_full = lax.all_gather(normed_attn, "blk", axis=0, tiled=True)
    projected = mm(normed_attn, qkv_full)
    qkv_packed = rope_pack(projected, cos_pair, sin_pair)
    if repeat > 1:
        qkv_packed = jnp.repeat(qkv_packed, repeat, 0)
    pieces, qkv_packed = lax.optimization_barrier((pieces, qkv_packed))
    joined, _ = plane_blocks(jnp.concatenate([at_index(pieces, mine), to_peer(at_index(pieces, 1 - mine))], 0))
    joined_mine = at_index(joined.reshape(plane * 2 * tok, planes, plane, rows), spot, 2)
    joined_mine = joined_mine.reshape(plane * 2 * tok, planes * rows)
    attn_packed, attn_t, lse, q_all, k_all, v_all = attend(all_to_all(qkv_packed), seg_all)
    attn_back = all_to_all(attn_packed)[::repeat]
    attn_back, joined_mine = lax.optimization_barrier((attn_back, joined_mine))
    attn_low = unpack_heads(attn_back[:, None])
    out_full = gathered_more[:, :width]
    up_half = gathered_more[:, width : 3 * width]
    down_a, down_b = gathered_more[:, 3 * width : 4 * width], gathered_more[:, 4 * width : 5 * width]
    stream_mid = stream_in + mm(attn_low, out_full)
    root_mid = lax.rsqrt(jnp.mean(stream_mid * stream_mid, -1, keepdims=True) + EPSILON)
    unit_mid = stream_mid * root_mid
    normed_ff = (unit_mid * gain_ff).astype(BF)
    normed_two = jnp.concatenate([normed_ff, to_peer(normed_ff)], 0)
    hidden_pre = mm(normed_two, up_half) + bias_up
    act_grad = jnp.concatenate([mm_nt(out_grad_two, down_a), mm_nt(out_grad_two, down_b)], 1)
    hidden, gelu_back = jax.vjp(activation, hidden_pre)
    hidden_act = hidden.astype(BF)
    pre_grad = gelu_back(act_grad)[0].astype(BF)
    ff_grad_two = mm_nt(pre_grad, up_half)
    ff_came = to_peer(ff_grad_two[tok:].astype(BF))
    down_low = [
        over_core(mm_tn(hidden_act[:, :width], out_grad_two)), over_core(mm_tn(hidden_act[:, width:], out_grad_two))
    ]
    ff_came, down_low = lax.optimization_barrier((ff_came, down_low))
    ff_grad = ff_grad_two[:tok] + ff_came.astype(F32)

    scaled = ff_grad * gain_ff
    grad_gff = jnp.sum(ff_grad * unit_mid, 0)
    mid_grad = out_grad.astype(F32) + root_mid * (scaled - unit_mid * jnp.mean(scaled * unit_mid, -1, keepdims=True))
    branch_grad = mid_grad.astype(BF)
    attn_grad = pack_heads(mm_nt(branch_grad, out_full).astype(BF))
    if repeat > 1:
        attn_grad = jnp.repeat(attn_grad, repeat, 0)

    hidden_act, normed_two, pre_grad, attn_grad = lax.optimization_barrier(
        (hidden_act, normed_two, pre_grad, attn_grad)
    )
    attn_grad_head = all_to_all(attn_grad[:, 0])
    grad_bup = jnp.sum(pre_grad.astype(F32), 0)
    up_low, out_low = over_core(mm_tn(normed_two, pre_grad)), over_core(mm_tn(attn_low, branch_grad))
    ff_two = mm(hidden_act[:, :width], down_a) + mm(hidden_act[:, width:], down_b)
    layer_out = (
        stream_mid + (ff_two[:tok] + to_peer(ff_two[tok:].astype(BF)).astype(F32)) + bias_down
    ).astype(BF)
    down_sum = jnp.concatenate([over_x(d) for d in down_low], 1)
    attn_grad_head, down_sum, up_low, out_low, normed_full = lax.optimization_barrier(
        (attn_grad_head, down_sum, up_low, out_low, normed_full)
    )
    down_share = over_z(down_sum)
    up_sum, out_sum = over_x(up_low), over_x(out_low)

    dqkv_packed, folded = attend_back(
        normed_full, q_all, k_all, v_all, attn_grad_head, attn_t, lse, seg_all, cos_rows, sin_rows
    )
    dqkv_packed, up_sum = lax.optimization_barrier((dqkv_packed, up_sum))
    dqkv_back, out_sum, down_share, layer_out = lax.optimization_barrier(
        (all_to_all(dqkv_packed)[::repeat], out_sum, down_share, layer_out)
    )
    projected_grad = unpack_heads(dqkv_back)
    shares = over_z(jnp.concatenate([up_sum, out_sum], 2))
    normed_grad = mm_nt(projected_grad, qkv_full)
    scaled_in = normed_grad * gain_attn
    grad_gattn = jnp.sum(normed_grad * unit_in, 0)
    in_grad = mid_grad + root_in * (scaled_in - unit_in * jnp.mean(scaled_in * unit_in, -1, keepdims=True))
    in_low = in_grad.astype(BF)
    folded, in_low = lax.optimization_barrier((folded, in_low))
    folded = all_to_all(folded)[::repeat]
    frames_grad, skip_grad = merge_pieces(mm_nt(in_low, skip_a), mm_nt(in_low, skip_b), blocks, BF)
    extra = [grad_gattn, grad_gff, jnp.sum(out_grad.astype(F32), 0)] + list(grad_bup.reshape(2, width))
    extra = jnp.pad(jnp.stack(extra).astype(BF), ((0, 11), (0, 0)))
    tail = jnp.concatenate([in_low, extra], 0)
    tails = jnp.concatenate([tail, to_peer(tail)], 0)
    tails, folded = lax.optimization_barrier((tails, folded))
    tails, (frames_grad, skip_grad) = plane_blocks(tails, (frames_grad, skip_grad))
    tails = tails.reshape(2 * plane, tok + 16, width)
    low_all = tails[:, :tok].reshape(2 * plane * tok, width)
    skip_part = mm_tn(joined_mine, low_all).astype(BF).reshape(planes, rows, width)
    vec = jnp.sum(tails[:, tok : tok + 5].astype(F32).reshape(plane, 2, 5, width), 0)
    vec = jnp.concatenate([jnp.sum(low_all.astype(F32), 0)[None], vec[0, :3] + vec[1, :3], vec[0, 3:], vec[1, 3:]], 0)
    vec = jnp.pad(vec.astype(BF), ((0, 8), (0, 0)))
    payload = jnp.concatenate([skip_part, jnp.broadcast_to(vec[None], (planes, 16, width))], 1)
    payload, shares = lax.optimization_barrier((payload, shares))
    summed = jnp.sum(all_to_all(payload, column_groups).astype(F32), 0)
    if packs > 2:
        summed = over_pairs(summed)
    skip_share = summed[:rows].astype(BF)
    w_skip_grad = both(skip_share, to_peer(skip_share)).reshape(2 * rows, width).astype(F32)
    own = lax.dynamic_slice_in_dim(summed[rows : rows + 8], me * rows, rows, 1)
    b_up_grad = both(own[4:6], own[6:8]).reshape(4 * rows)
    qkv_share = unpack_heads(folded)
    if packs > 2:
        qkv_share = over_pairs(qkv_share.astype(F32)).astype(BF)
    w_qkv_grad = qkv_share.astype(F32) + to_peer(qkv_share).astype(F32)

    others = to_peer(shares)
    w_up_grad = up_columns(mine, shares[:, : 2 * width], others[:, : 2 * width], blocks)
    shares, others = shares[:, 2 * width :].astype(F32), others[:, 2 * width :].astype(F32)
    w_out_grad = shares + others
    w_down_grad = both(down_share, to_peer(down_share)).reshape(4 * rows, width).astype(F32)
    return (
        layer_out, frames_grad, skip_grad, w_skip_grad, own[0], own[1], w_qkv_grad, w_out_grad, own[2],
        w_up_grad, b_up_grad, w_down_grad, own[3],
    )


def solution(mesh):
    token_spec = P(("pack", "blk"), None)
    matrix, vector = P("blk", None), P("blk")
    return jax.shard_map(
        local,
        mesh=mesh,
        in_specs=(
            token_spec, token_spec, P("pack", None), matrix, vector, vector, matrix, matrix, vector, matrix, vector,
            matrix, vector, token_spec,
        ),
        out_specs=(
            token_spec, token_spec, token_spec, matrix, vector, vector, matrix, matrix, vector, matrix, vector, matrix,
            vector,
        ),
        check_vma=False,
    )
```

```python
import functools
import math

import jax
import jax.numpy as jnp
from jax import lax
from jax.experimental import pallas as pl
from jax.experimental.pallas import tpu as pltpu
from jax.sharding import PartitionSpec as P

H = 16
HD = 64
EPSILON = 1e-06
MASKED_SCORE = -1e30
STEP = 256
VMEM = 56 * 1024 * 1024
BF = jnp.bfloat16
F32 = jnp.float32


def mm(left, right):
    return jnp.dot(left, right, preferred_element_type=F32)


def mm_nt(left, right):
    return lax.dot_general(left, right, (((1,), (1,)), ((), ())), preferred_element_type=F32)


def mm_tn(left, right):
    return lax.dot_general(left, right, (((0,), (0,)), ((), ())), preferred_element_type=F32)


def whole(shape):
    return pl.BlockSpec(shape, lambda *_: (0,) * len(shape))


def segment_of(position, lengths_row):
    bounds = jnp.cumsum(lengths_row)
    after = position[:, None] >= bounds[None, :]
    segment = jnp.sum(after.astype(jnp.int32), 1, dtype=jnp.int32)
    before = jnp.sum(jnp.where(after, lengths_row[None, :], 0), 1, dtype=jnp.int32)
    return segment, position - before


def angles(offset):
    freq = 10000.0 ** (-(jnp.arange(HD // 2, dtype=F32) * 2.0 / HD))
    angle = offset.astype(F32)[:, None] * freq[None, :]
    return jnp.cos(angle), jnp.sin(angle)


def activation(value):
    return jax.nn.gelu(value, approximate=True)


def pack_pair(block, lane_low):
    half = block.shape[0] // 2
    top, bottom = block[:half], block[half:]
    even = jnp.where(lane_low, top, pltpu.roll(bottom, HD, 1))
    odd = jnp.where(lane_low, pltpu.roll(top, HD, 1), bottom)
    return even, odd


def rope_pack_kernel(proj_ref, cos_ref, sin_ref, out_ref):
    rows = proj_ref.shape[0]
    lane = lax.broadcasted_iota(jnp.int32, (rows, 128), 1)
    first = (lane % HD) < HD // 2
    lane_low = lane[: rows // 2] < HD
    cosine, sine = cos_ref[...], sin_ref[...]
    for part in range(3):
        for pair in range(H // 2):
            at = (part * H + 2 * pair) * HD
            block = proj_ref[:, at : at + 128]
            if part < 2:
                swapped = jnp.where(first, pltpu.roll(block, 128 - HD // 2, 1), pltpu.roll(block, HD // 2, 1))
                block = block * cosine + swapped * sine
            block = block.astype(BF).astype(F32)
            if part == 0:
                block = block * (1.0 / math.sqrt(HD))
            even, odd = pack_pair(block, lane_low)
            out_ref[2 * pair, part] = even.astype(BF)
            out_ref[2 * pair + 1, part] = odd.astype(BF)


def rope_pack(proj, cos_pair, sin_pair):
    rows = proj.shape[0]
    return pl.pallas_call(
        rope_pack_kernel,
        out_shape=jax.ShapeDtypeStruct((H, 3, rows // 2, 128), BF),
        compiler_params=pltpu.CompilerParams(vmem_limit_bytes=VMEM),
        name="rope_pack",
    )(proj, cos_pair, sin_pair)


def pack_kernel(in_ref, out_ref):
    parts, half = out_ref.shape[1], out_ref.shape[2]
    lane_low = lax.broadcasted_iota(jnp.int32, (half, 128), 1) < HD
    for part in range(parts):
        for pair in range(H // 2):
            at = (part * H + 2 * pair) * HD
            even, odd = pack_pair(in_ref[:, at : at + 128].astype(F32), lane_low)
            out_ref[2 * pair, part] = even.astype(BF)
            out_ref[2 * pair + 1, part] = odd.astype(BF)


def pack_heads(rows_all):
    rows, columns = rows_all.shape
    return pl.pallas_call(
        pack_kernel,
        out_shape=jax.ShapeDtypeStruct((H, columns // (H * HD), rows // 2, 128), BF),
        compiler_params=pltpu.CompilerParams(vmem_limit_bytes=VMEM),
        name="pack_heads",
    )(rows_all)


def unpack_kernel(in_ref, out_ref):
    parts, half = in_ref.shape[1], in_ref.shape[2]
    lane_low = lax.broadcasted_iota(jnp.int32, (half, 128), 1) < HD
    for part in range(parts):
        for pair in range(H // 2):
            even = in_ref[2 * pair, part].astype(F32)
            odd = in_ref[2 * pair + 1, part].astype(F32)
            top = jnp.where(lane_low, even, pltpu.roll(odd, HD, 1))
            bottom = jnp.where(lane_low, pltpu.roll(even, HD, 1), odd)
            at = (part * H + 2 * pair) * HD
            out_ref[:half, at : at + 128] = top.astype(BF)
            out_ref[half:, at : at + 128] = bottom.astype(BF)


def unpack_heads(packed):
    _, parts, half, _ = packed.shape
    return pl.pallas_call(
        unpack_kernel,
        out_shape=jax.ShapeDtypeStruct((2 * half, parts * H * HD), BF),
        compiler_params=pltpu.CompilerParams(vmem_limit_bytes=VMEM),
        name="unpack_heads",
    )(packed)


def lanes(top, bottom):
    low = lax.broadcasted_iota(jnp.int32, top.shape, 1) < HD
    return jnp.where(low, top, pltpu.roll(bottom, HD, 1)), jnp.where(low, pltpu.roll(top, HD, 1), bottom)


def split_kernel(left_ref, right_ref, out_ref):
    pairs = left_ref.shape[1] // 256
    for half, ref in enumerate((left_ref, right_ref)):
        for pair in range(pairs):
            at = pair * 256
            first, second = lanes(ref[:, at : at + 128].astype(F32), ref[:, at + 128 : at + 256].astype(F32))
            there = (half * pairs + pair) * 128
            out_ref[0, :, there : there + 128] = first.astype(out_ref.dtype)
            out_ref[1, :, there : there + 128] = second.astype(out_ref.dtype)


def split_pieces(left, right, blocks):
    tok, width = left.shape
    if width // blocks != HD:
        by_piece = jnp.concatenate([left, right], 1).reshape(tok, blocks, 2, width // blocks)
        return jnp.transpose(by_piece, (2, 0, 1, 3)).reshape(2, tok, width)
    return pl.pallas_call(
        split_kernel,
        out_shape=jax.ShapeDtypeStruct((2, tok, width), left.dtype),
        compiler_params=pltpu.CompilerParams(vmem_limit_bytes=VMEM),
        name="split_pieces",
    )(left, right)


def merge_kernel(first_ref, second_ref, left_ref, right_ref):
    pairs = left_ref.shape[1] // 256
    for half, ref in enumerate((left_ref, right_ref)):
        for pair in range(pairs):
            there = (half * pairs + pair) * 128
            even, odd = lanes(
                first_ref[:, there : there + 128].astype(F32), second_ref[:, there : there + 128].astype(F32)
            )
            at = pair * 256
            ref[:, at : at + 128] = even.astype(ref.dtype)
            ref[:, at + 128 : at + 256] = odd.astype(ref.dtype)


def merge_pieces(first, second, blocks, dtype):
    tok, width = first.shape
    if width // blocks != HD:
        both = jnp.stack([first.reshape(tok, blocks, -1), second.reshape(tok, blocks, -1)], 2)
        both = both.reshape(tok, 2 * width).astype(dtype)
        return both[:, :width], both[:, width:]
    return pl.pallas_call(
        merge_kernel,
        out_shape=[jax.ShapeDtypeStruct((tok, width), dtype)] * 2,
        compiler_params=pltpu.CompilerParams(vmem_limit_bytes=VMEM),
        name="merge_pieces",
    )(first, second)


def up_kernel(mine_ref, own_ref, other_ref, out_ref):
    width = own_ref.shape[1] // 2
    first = mine_ref[0] == 0
    for piece in range(2):
        for pair in range(width // 128):
            at = pair * 128
            tiles = []
            for s in range(2):
                own = own_ref[:, s * width + at : s * width + at + 128].astype(F32)
                other = other_ref[:, s * width + at : s * width + at + 128].astype(F32)
                tiles.append(jnp.where(first, own, other) if piece == 0 else jnp.where(first, other, own))
            even, odd = lanes(*tiles)
            out_ref[:, (4 * pair + piece) * 128 : (4 * pair + piece + 1) * 128] = even
            out_ref[:, (4 * pair + 2 + piece) * 128 : (4 * pair + 3 + piece) * 128] = odd


def up_columns(mine, own, other, blocks):
    rows, half = own.shape
    if half // 2 // blocks != HD:
        pair = jnp.where(mine == 0, jnp.stack([own, other]), jnp.stack([other, own]))
        pair = jnp.transpose(pair, (1, 0, 2)).reshape(rows, 4, blocks, half // 2 // blocks)
        return jnp.transpose(pair, (0, 2, 1, 3)).reshape(rows, 2 * half).astype(F32)
    return pl.pallas_call(
        up_kernel,
        in_specs=[pl.BlockSpec(memory_space=pltpu.SMEM), whole((rows, half)), whole((rows, half))],
        out_specs=whole((rows, 2 * half)),
        out_shape=jax.ShapeDtypeStruct((rows, 2 * half), F32),
        compiler_params=pltpu.CompilerParams(vmem_limit_bytes=VMEM),
        name="up_columns",
    )(mine.astype(jnp.int32).reshape(1), own, other)


def parts_kernel(planes, inner, core_ref, left_ref, right_ref, keep_ref, send_ref):
    first = core_ref[0] == 0
    step = pl.program_id(0)
    for z in range(planes):
        at = (step // inner * planes * inner + z * inner + step % inner) * 2 * HD
        grad = mm_tn(left_ref[:, pl.ds(pl.multiple_of(at, 2 * HD), 2 * HD)], right_ref[...])
        top, bottom = grad[:HD], grad[HD:]
        keep_ref[0, z] = jnp.where(first, top, bottom).astype(BF)
        send_ref[0, z] = jnp.where(first, bottom, top).astype(BF)


def grad_parts(left, right, me, planes, inner, rows):
    frames, columns = right.shape
    pieces = left.shape[1] // (planes * inner * 2 * rows)
    core, x = me % 2, me // 2 % inner
    if rows != HD:
        grad = mm_tn(left, right).astype(BF).reshape(pieces, planes, inner, 2, rows, columns)
        grad = jnp.stack([lax.dynamic_index_in_dim(grad, (x + k) % inner, 2, keepdims=False) for k in range(inner)])
        both = [lax.dynamic_index_in_dim(grad, c, 3, keepdims=False) for c in (core, 1 - core)]
        return [jnp.transpose(g, (0, 2, 1, 3, 4)).reshape(inner, planes, pieces * rows, columns) for g in both]

    def place(i, scalars):
        return (i % inner - scalars[1] + inner) % inner, 0, i // inner, 0

    shape = (inner, planes, pieces * rows, columns)
    return pl.pallas_call(
        functools.partial(parts_kernel, planes, inner),
        grid_spec=pltpu.PrefetchScalarGridSpec(
            num_scalar_prefetch=1,
            grid=(pieces * inner,),
            in_specs=[whole(left.shape), whole(right.shape)],
            out_specs=[pl.BlockSpec((1, planes, rows, columns), place)] * 2,
        ),
        out_shape=[jax.ShapeDtypeStruct(shape, BF)] * 2,
        compiler_params=pltpu.CompilerParams(vmem_limit_bytes=VMEM),
        name="grad_parts",
    )(jnp.stack([core, x]).astype(jnp.int32), left, right)


def rotated(rows, cosine, sine):
    swapped = jnp.concatenate([rows[:, HD // 2 :], rows[:, : HD // 2]], 1)
    return rows * cosine + swapped * sine


def put_packed(out_ref, step, rows, half, part=None):
    each = rows.shape[0] // (2 * half)
    for i in range(each):
        block = rows[2 * half * i : 2 * half * (i + 1)]
        joined = jnp.concatenate([block[:half], block[half:]], 1).astype(BF)
        if part is None:
            out_ref[step * each + i] = joined
        else:
            out_ref[step * each + i, part] = joined


def attend_kernel(qkv_ref, segc_ref, segr_ref, out_ref, attn_ref, lse_ref, q_ref, k_ref, v_ref, vt_s):
    g = pl.program_id(0)
    half = qkv_ref.shape[-2]
    tok = 2 * half

    @pl.when(g == 0)
    def _():
        for i in range(qkv_ref.shape[0]):
            for part, ref in enumerate((q_ref, k_ref, v_ref)):
                block = qkv_ref[i, part].astype(F32)
                ref[i * tok : i * tok + half] = block[:, :HD].astype(BF)
                ref[i * tok + half : (i + 1) * tok] = block[:, HD:].astype(BF)
        vt_s[...] = jnp.transpose(v_ref[...].astype(F32)).astype(BF)

    here = pl.ds(pl.multiple_of(g * STEP, STEP), STEP)
    scores = mm_nt(k_ref[...], q_ref[here])
    allowed = segc_ref[...] == segr_ref[:, here]
    scores = jnp.where(allowed, scores, MASKED_SCORE)
    top = jnp.max(scores, 0, keepdims=True)
    weight = jnp.exp(scores - top)
    total = jnp.sum(weight, 0, keepdims=True)
    attn_t = mm(vt_s[...], weight.astype(BF)) / total
    attn_ref[:, here] = attn_t
    lse_ref[:, here] = top + jnp.log(total)
    put_packed(out_ref, g, jnp.transpose(attn_t), tok // 2)


def attend(qkv, seg):
    blocks, _, half, _ = qkv.shape
    total = blocks * half * 2
    return pl.pallas_call(
        attend_kernel,
        grid=(total // STEP,),
        in_specs=[whole(qkv.shape), whole((total, 1)), whole((1, total))],
        out_specs=[whole((blocks, half, 128)), whole((HD, total)), whole((1, total))] + [whole((total, HD))] * 3,
        out_shape=[
            jax.ShapeDtypeStruct((blocks, half, 128), BF),
            jax.ShapeDtypeStruct((HD, total), F32),
            jax.ShapeDtypeStruct((1, total), F32),
        ]
        + [jax.ShapeDtypeStruct((total, HD), BF)] * 3,
        scratch_shapes=[pltpu.VMEM((HD, total), BF)],
        compiler_params=pltpu.CompilerParams(vmem_limit_bytes=VMEM),
        cost_estimate=pl.CostEstimate(flops=int(1.6e10), bytes_accessed=8 << 20, transcendentals=0),
        name="attend",
    )(qkv, seg[:, None], seg[None, :])


def attend_back_kernel(
    q_ref, k_ref, v_ref, do_ref, attn_ref, lse_ref, segc_ref, segr_ref, cos_ref, sin_ref, normed_ref,
    out_ref, grad_ref, do_s, delta_s, dq_s, flat_s,
):
    g = pl.program_id(0)
    blocks = do_ref.shape[0]
    half = do_ref.shape[-2]
    tok = 2 * half
    scale = 1.0 / math.sqrt(HD)

    @pl.when(g == 0)
    def _():
        for i in range(blocks):
            block = do_ref[i].astype(F32)
            do_s[i * tok : i * tok + half] = block[:, :HD].astype(BF)
            do_s[i * tok + half : (i + 1) * tok] = block[:, HD:].astype(BF)
        do_t = jnp.transpose(do_s[...].astype(F32))
        delta_s[...] = jnp.sum(do_t * attn_ref[...], 0, keepdims=True)
        dq_s[...] = jnp.zeros_like(dq_s)

    here = pl.ds(pl.multiple_of(g * STEP, STEP), STEP)
    keys = k_ref[here]
    scores = mm_nt(keys, q_ref[...])
    allowed = segc_ref[here] == segr_ref[...]
    probs = jnp.where(allowed, jnp.exp(scores - lse_ref[...]), 0.0)
    prob_grad = mm_nt(v_ref[here], do_s[...])
    score_grad = (probs * (prob_grad - delta_s[...])).astype(BF)
    value_grad = mm(probs.astype(BF), do_s[...])
    key_grad = mm(score_grad, q_ref[...])
    keys_t = jnp.transpose(keys.astype(F32)).astype(BF)
    dq_s[...] += mm(keys_t, score_grad)

    def put(part, step, rows, where):
        flat_s[part * HD : (part + 1) * HD, where] = jnp.transpose(rows).astype(BF)
        put_packed(out_ref, step, rows, half, part)

    put(1, g, rotated(key_grad, cos_ref[here], sin_ref[here]), here)
    put(2, g, value_grad, here)

    @pl.when(g == pl.num_programs(0) - 1)
    def _():
        for step in range(q_ref.shape[0] // STEP):
            there = slice(step * STEP, (step + 1) * STEP)
            rows = jnp.transpose(dq_s[:, there]) * scale
            put(0, step, rotated(rows, cos_ref[there], sin_ref[there]), there)
        grad = jnp.transpose(mm(flat_s[...], normed_ref[...]))
        rows = grad.shape[0] // blocks
        for i in range(blocks):
            for part in range(3):
                block = grad[i * rows : (i + 1) * rows, part * HD : (part + 1) * HD]
                grad_ref[i, part] = jnp.concatenate([block[: rows // 2], block[rows // 2 :]], 1).astype(BF)


def attend_back(normed, q, k, v, attn_grad, attn_t, lse, seg, cos_rows, sin_rows):
    total, width = normed.shape
    blocks, half, _ = attn_grad.shape
    rows = width // blocks
    return pl.pallas_call(
        attend_back_kernel,
        grid=(total // STEP,),
        in_specs=[whole((total, HD))] * 3
        + [whole((blocks, half, 128)), whole((HD, total)), whole((1, total))]
        + [whole((total, 1)), whole((1, total)), whole((total, HD)), whole((total, HD))]
        + [whole((total, width))],
        out_specs=[whole((blocks, 3, half, 128)), whole((blocks, 3, rows // 2, 128))],
        out_shape=[
            jax.ShapeDtypeStruct((blocks, 3, half, 128), BF),
            jax.ShapeDtypeStruct((blocks, 3, rows // 2, 128), BF),
        ],
        scratch_shapes=[
            pltpu.VMEM((total, HD), BF),
            pltpu.VMEM((1, total), F32),
            pltpu.VMEM((HD, total), F32),
            pltpu.VMEM((3 * HD, total), BF),
        ],
        compiler_params=pltpu.CompilerParams(vmem_limit_bytes=VMEM),
        cost_estimate=pl.CostEstimate(flops=int(2.4e10), bytes_accessed=8 << 20, transcendentals=0),
        name="attend_back",
    )(q, k, v, attn_grad, attn_t, lse, seg[:, None], seg[None, :], cos_rows, sin_rows, normed)


def local(
    frames, skip_input, lengths, w_skip, b_skip, g_attn, w_qkv, w_out, g_ff, w_up, b_up, w_down, b_down, out_grad
):
    tok, width = frames.shape
    blocks = lax.axis_size("blk")
    packs = lax.axis_size("pack")
    me = lax.axis_index("blk")
    mine = lax.axis_index("pack") % 2
    rows = width // blocks
    repeat = blocks // H
    half = tok // 2
    planes = 4
    plane = blocks // planes
    spot = me % plane
    place = me // plane
    plane_groups = [[z * plane + j for j in range(plane)] for z in range(planes)]
    column_groups = [[z * plane + j for z in range(planes)] for j in range(plane)]
    swap = [(i, i ^ 1) for i in range(packs)]

    def to_peer(block):
        return lax.ppermute(block, "pack", swap)

    def over_pairs(block):
        total = block
        for k in range(1, packs // 2):
            total = total + lax.ppermute(block, "pack", [(i, (i + 2 * k) % packs) for i in range(packs)])
        return total

    def all_to_all(block, groups=None):
        return lax.all_to_all(block, "blk", 0, 0, tiled=True, axis_index_groups=groups)

    inner = plane // 2
    core = [(i, i ^ 1) for i in range(blocks)]

    def along_z(k):
        return [(i, (i + plane * k) % blocks) for i in range(blocks)]

    def along_x(k):
        return [(i, (i // plane) * plane + ((i % plane) // 2 + k) % inner * 2 + i % 2) for i in range(blocks)]

    def send(block, route):
        return lax.ppermute(block, "blk", route)

    def plane_blocks(block, beside=()):
        column = [block] + [send(block, along_x(k)) for k in range(1, inner)]
        if inner > 1:
            column = jnp.stack(column)
        else:
            column = column[0][None]
        column, beside = lax.optimization_barrier((column, beside))
        return jnp.concatenate([column, send(column, core)], 0), beside

    def plane_sources():
        return [(spot // 2 - k) % inner * 2 + ((spot % 2) ^ c) for c in range(2) for k in range(inner)]

    def own_half(block, axis):
        size = block.shape[axis] // 2
        return lax.dynamic_slice_in_dim(block, mine * size, size, axis)

    def at_index(block, index, axis=0):
        return lax.dynamic_index_in_dim(block, index, axis, keepdims=False)

    vectors = jnp.stack([b_skip, g_attn, g_ff, b_down] + list(b_up.reshape(4, rows)), 0)
    vectors = jnp.transpose(jnp.pad(vectors, ((0, 120), (0, 0))))
    up_cols = jnp.transpose(w_up.reshape(rows, blocks, 4, rows), (0, 2, 1, 3)).reshape(rows, 2, 2 * width)
    up_mine = at_index(up_cols, mine, 1)
    down_mine = own_half(w_down, 0)
    payload = jnp.concatenate(
        [w_skip[:rows], w_skip[rows:], w_qkv, w_out, up_mine, down_mine[:rows], down_mine[rows:], vectors], 1
    )
    gathered = lax.all_gather(payload, "blk", axis=0, tiled=True)

    pack_lengths = lengths[0]
    seg_all, offset_all = segment_of(jnp.arange(tok * blocks, dtype=jnp.int32), pack_lengths)
    cos_all, sin_all = angles(offset_all)
    cos_rows = jnp.concatenate([cos_all, cos_all], 1)
    sin_rows = jnp.concatenate([sin_all, -sin_all], 1)
    cosine = lax.dynamic_slice_in_dim(cos_all, me * tok, tok, 0)
    sine = lax.dynamic_slice_in_dim(sin_all, me * tok, tok, 0)
    cos_pair = jnp.concatenate([cosine] * 4, 1)
    sin_pair = jnp.concatenate([-sine, sine, -sine, sine], 1)
    pieces = split_pieces(frames, skip_input, blocks)
    gathered, pieces, cos_rows, sin_rows, cos_pair, sin_pair, seg_all = lax.optimization_barrier(
        (gathered, pieces, cos_rows, sin_rows, cos_pair, sin_pair, seg_all)
    )
    skip_a, skip_b = gathered[:, :width], gathered[:, width : 2 * width]
    qkv_full = gathered[:, 2 * width : 5 * width]
    gathered_more = gathered[:, 5 * width :]
    small = jnp.transpose(gathered[:, 10 * width :].astype(F32))[:8]
    bias_skip, gain_attn, gain_ff, bias_down = small[0], small[1], small[2], small[3]
    bias_up = lax.dynamic_slice_in_dim(small, 4 + 2 * mine, 2, 0).reshape(2 * width)

    def over_core(left, right):
        keep, other = grad_parts(left, right, me, planes, inner, rows)
        return (keep.astype(F32) + send(other, core).astype(F32)).astype(BF)

    def over_x(grad):
        total = grad[0].astype(F32)
        for k in range(1, inner):
            total = total + send(grad[k], along_x(k)).astype(F32)
        return total.astype(BF)

    def over_z(grad):
        total = lax.psum_scatter(
            grad.reshape(planes * grad.shape[1], grad.shape[2]),
            "blk",
            scatter_dimension=0,
            axis_index_groups=column_groups,
            tiled=True,
        )
        return over_pairs(total.astype(F32)).astype(BF) if packs > 2 else total

    def both(own, other):
        return jnp.where(mine == 0, jnp.stack([own, other]), jnp.stack([other, own]))

    stream_in = mm(pieces[0], skip_a) + mm(pieces[1], skip_b) + bias_skip
    root_in = lax.rsqrt(jnp.mean(stream_in * stream_in, -1, keepdims=True) + EPSILON)
    unit_in = stream_in * root_in
    normed_attn = (unit_in * gain_attn).astype(BF)
    projected = mm(normed_attn, qkv_full)
    qkv_packed = rope_pack(projected, cos_pair, sin_pair)
    if repeat > 1:
        qkv_packed = jnp.repeat(qkv_packed, repeat, 0)
    qkv_packed, grad_sent = lax.optimization_barrier((qkv_packed, out_grad))
    out_grad_two = jnp.concatenate([out_grad, to_peer(grad_sent)], 0)
    qkv_head, frames_late, skip_late = lax.optimization_barrier((all_to_all(qkv_packed), frames, skip_input))
    joined = jnp.concatenate([frames_late, skip_late], 1).reshape(tok, planes, plane, 2 * rows)
    joined = all_to_all(jnp.transpose(joined, (2, 0, 1, 3)).reshape(plane, tok, planes * 2 * rows), plane_groups)
    joined = jnp.concatenate([at_index(joined, source) for source in plane_sources()], 0)
    attn_packed, attn_t, lse, q_all, k_all, v_all = attend(qkv_head, seg_all)
    attn_packed, joined = lax.optimization_barrier((attn_packed, joined))
    attn_back = all_to_all(attn_packed)[::repeat]
    attn_back, normed_late, out_grad_two = lax.optimization_barrier((attn_back, normed_attn, out_grad_two))
    normed_full = lax.all_gather(normed_late, "blk", axis=0, tiled=True)
    attn_low = unpack_heads(attn_back[:, None])
    out_full = gathered_more[:, :width]
    up_half = gathered_more[:, width : 3 * width]
    down_a, down_b = gathered_more[:, 3 * width : 4 * width], gathered_more[:, 4 * width : 5 * width]
    stream_mid = stream_in + mm(attn_low, out_full)
    root_mid = lax.rsqrt(jnp.mean(stream_mid * stream_mid, -1, keepdims=True) + EPSILON)
    unit_mid = stream_mid * root_mid
    normed_ff = (unit_mid * gain_ff).astype(BF)
    normed_two = jnp.concatenate([normed_ff, to_peer(normed_ff)], 0)
    hidden_pre = mm(normed_two, up_half) + bias_up
    act_grad = jnp.concatenate([mm_nt(out_grad_two, down_a), mm_nt(out_grad_two, down_b)], 1)
    hidden, gelu_back = jax.vjp(activation, hidden_pre)
    hidden_act = hidden.astype(BF)
    pre_grad = gelu_back(act_grad)[0].astype(BF)
    ff_grad_two = mm_nt(pre_grad, up_half)
    ff_came = to_peer(ff_grad_two[tok:].astype(BF))
    down_low = over_core(hidden_act, out_grad_two)
    ff_came, down_low = lax.optimization_barrier((ff_came, down_low))
    ff_grad = ff_grad_two[:tok] + ff_came.astype(F32)

    scaled = ff_grad * gain_ff
    grad_gff = jnp.sum(ff_grad * unit_mid, 0)
    mid_grad = out_grad.astype(F32) + root_mid * (scaled - unit_mid * jnp.mean(scaled * unit_mid, -1, keepdims=True))
    branch_grad = mid_grad.astype(BF)
    attn_grad = pack_heads(mm_nt(branch_grad, out_full).astype(BF))
    if repeat > 1:
        attn_grad = jnp.repeat(attn_grad, repeat, 0)

    hidden_act, normed_two, pre_grad, attn_grad = lax.optimization_barrier(
        (hidden_act, normed_two, pre_grad, attn_grad)
    )
    attn_grad_head = all_to_all(attn_grad[:, 0])
    grad_bup = jnp.sum(pre_grad.astype(F32), 0)
    up_low, out_low = over_core(normed_two, pre_grad), over_core(attn_low, branch_grad)
    ff_two = mm(hidden_act[:, :width], down_a) + mm(hidden_act[:, width:], down_b)
    layer_out = (
        stream_mid + (ff_two[:tok] + to_peer(ff_two[tok:].astype(BF)).astype(F32)) + bias_down
    ).astype(BF)
    down_sum = over_x(down_low)
    attn_grad_head, down_sum, up_low, out_low, normed_full = lax.optimization_barrier(
        (attn_grad_head, down_sum, up_low, out_low, normed_full)
    )
    down_share = over_z(down_sum)
    up_sum, out_sum = over_x(up_low), over_x(out_low)

    dqkv_packed, folded = attend_back(
        normed_full, q_all, k_all, v_all, attn_grad_head, attn_t, lse, seg_all, cos_rows, sin_rows
    )
    dqkv_packed, up_sum = lax.optimization_barrier((dqkv_packed, up_sum))
    down_peer = to_peer(down_share)
    dqkv_back, up_sum, down_share, down_peer, layer_out = lax.optimization_barrier(
        (all_to_all(dqkv_packed)[::repeat], up_sum, down_share, down_peer, layer_out)
    )
    projected_grad = unpack_heads(dqkv_back)
    shares = over_z(jnp.concatenate([up_sum, out_sum], 2))
    normed_grad = mm_nt(projected_grad, qkv_full)
    scaled_in = normed_grad * gain_attn
    grad_gattn = jnp.sum(normed_grad * unit_in, 0)
    in_grad = mid_grad + root_in * (scaled_in - unit_in * jnp.mean(scaled_in * unit_in, -1, keepdims=True))
    in_low = in_grad.astype(BF)
    folded, in_low = lax.optimization_barrier((folded, in_low))
    folded = all_to_all(folded)[::repeat]
    frames_grad, skip_grad = merge_pieces(mm_nt(in_low, skip_a), mm_nt(in_low, skip_b), blocks, BF)
    extra = [grad_gattn, grad_gff, jnp.sum(out_grad.astype(F32), 0)] + list(grad_bup.reshape(2, width))
    extra = jnp.pad(jnp.stack(extra).astype(BF), ((0, 11), (0, 0)))
    tail = jnp.concatenate([in_low, extra], 0)
    tails, (frames_grad, skip_grad, folded) = plane_blocks(tail[None], (frames_grad, skip_grad, folded))
    qkv_share = unpack_heads(folded)
    if packs > 2:
        qkv_share = over_pairs(qkv_share.astype(F32)).astype(BF)
    qkv_peer = to_peer(qkv_share)
    tails = tails.reshape(plane, tok + 16, width)
    low_all = tails[:, :tok].reshape(plane * tok, width)
    skip_part = mm_tn(joined, low_all).astype(BF).reshape(planes, 2 * rows, width)
    vec = jnp.sum(tails[:, tok : tok + 5].astype(F32), 0)
    vec = jnp.concatenate([jnp.sum(low_all.astype(F32), 0)[None], vec], 0)
    vec = jnp.pad(vec.astype(BF), ((0, 10), (0, 0)))
    payload = jnp.concatenate([skip_part, jnp.broadcast_to(vec[None], (planes, 16, width))], 1)
    payload, shares = lax.optimization_barrier((payload, shares))
    others = to_peer(shares)
    summed = at_index(payload, place).astype(F32)
    came = [send(at_index(payload, (place + k) % planes), along_z(k)) for k in range(1, planes)]
    came, qkv_peer, others = lax.optimization_barrier((came, qkv_peer, others))
    for block in came:
        summed = summed + block.astype(F32)
    if packs > 2:
        summed = over_pairs(summed)
    summed_peer = to_peer(summed.astype(BF)).astype(F32)
    total = summed + summed_peer
    w_skip_grad = total[: 2 * rows]
    own = lax.dynamic_slice_in_dim(total[2 * rows :], me * rows, rows, 1)
    b_up_grad = both(
        lax.dynamic_slice_in_dim(summed[2 * rows + 4 : 2 * rows + 6], me * rows, rows, 1),
        lax.dynamic_slice_in_dim(summed_peer[2 * rows + 4 : 2 * rows + 6], me * rows, rows, 1),
    ).reshape(4 * rows)
    w_qkv_grad = qkv_share.astype(F32) + qkv_peer.astype(F32)

    w_up_grad = up_columns(mine, shares[:, : 2 * width], others[:, : 2 * width], blocks)
    shares, others = shares[:, 2 * width :].astype(F32), others[:, 2 * width :].astype(F32)
    w_out_grad = shares + others
    w_down_grad = both(down_share, down_peer).reshape(4 * rows, width).astype(F32)
    return (
        layer_out, frames_grad, skip_grad, w_skip_grad, own[0], own[1], w_qkv_grad, w_out_grad, own[2],
        w_up_grad, b_up_grad, w_down_grad, own[3],
    )


def solution(mesh):
    token_spec = P(("pack", "blk"), None)
    matrix, vector = P("blk", None), P("blk")
    return jax.shard_map(
        local,
        mesh=mesh,
        in_specs=(
            token_spec, token_spec, P("pack", None), matrix, vector, vector, matrix, matrix, vector, matrix, vector,
            matrix, vector, token_spec,
        ),
        out_specs=(
            token_spec, token_spec, token_spec, matrix, vector, vector, matrix, matrix, vector, matrix, vector, matrix,
            vector,
        ),
        check_vma=False,
    )
```

```python
import functools
import math

import jax
import jax.numpy as jnp
from jax import lax
from jax.experimental import pallas as pl
from jax.experimental.pallas import tpu as pltpu
from jax.sharding import PartitionSpec as P

H = 16
HD = 64
EPSILON = 1e-06
MASKED_SCORE = -1e30
SCORES = 2048 * 2048
QKV = 1024
VMEM = 56 * 1024 * 1024
BF = jnp.bfloat16
F32 = jnp.float32


def mm(left, right):
    return jnp.dot(left, right, preferred_element_type=F32)


def mm_nt(left, right):
    return lax.dot_general(left, right, (((1,), (1,)), ((), ())), preferred_element_type=F32)


def mm_tn(left, right):
    return lax.dot_general(left, right, (((0,), (0,)), ((), ())), preferred_element_type=F32)


def whole(shape):
    return pl.BlockSpec(shape, lambda *_: (0,) * len(shape))


def segment_of(position, lengths_row):
    bounds = jnp.cumsum(lengths_row)
    after = position[:, None] >= bounds[None, :]
    segment = jnp.sum(after.astype(jnp.int32), 1, dtype=jnp.int32)
    before = jnp.sum(jnp.where(after, lengths_row[None, :], 0), 1, dtype=jnp.int32)
    return segment, position - before


def angles(offset):
    freq = 10000.0 ** (-(jnp.arange(HD // 2, dtype=F32) * 2.0 / HD))
    angle = offset.astype(F32)[:, None] * freq[None, :]
    return jnp.cos(angle), jnp.sin(angle)


def activation(value):
    return jax.nn.gelu(value, approximate=True)


def pack_pair(block, lane_low):
    half = block.shape[0] // 2
    top, bottom = block[:half], block[half:]
    even = jnp.where(lane_low, top, pltpu.roll(bottom, HD, 1))
    odd = jnp.where(lane_low, pltpu.roll(top, HD, 1), bottom)
    return even, odd


def qkv_kernel(normed_ref, weight_ref, cos_ref, sin_ref, out_ref):
    step = pl.program_id(0)
    projected = mm(normed_ref[...], weight_ref[...])
    rows = projected.shape[0]
    lane = lax.broadcasted_iota(jnp.int32, (rows, 128), 1)
    first = (lane % HD) < HD // 2
    lane_low = lane[: rows // 2] < HD
    per_part = normed_ref.shape[1] // QKV
    scale = jnp.where(step < per_part, 1.0 / math.sqrt(HD), 1.0)
    for pair in range(QKV // 128):
        block = projected[:, pair * 128 : pair * 128 + 128]
        swapped = jnp.where(first, pltpu.roll(block, 128 - HD // 2, 1), pltpu.roll(block, HD // 2, 1))
        block = jnp.where(step < 2 * per_part, block * cos_ref[...] + swapped * sin_ref[...], block)
        even, odd = pack_pair(block.astype(BF).astype(F32) * scale, lane_low)
        out_ref[2 * pair, 0] = even.astype(BF)
        out_ref[2 * pair + 1, 0] = odd.astype(BF)


def qkv_rows(normed, gathered, at, cos_pair, sin_pair):
    rows, width = normed.shape
    return pl.pallas_call(
        qkv_kernel,
        grid=(3 * width // QKV,),
        in_specs=[
            whole(normed.shape), pl.BlockSpec((width, QKV), lambda i: (0, at // QKV + i)), whole((rows, 128)),
            whole((rows, 128)),
        ],
        out_specs=pl.BlockSpec((QKV // HD, 1, rows // 2, 128), lambda i: (i % (width // QKV), i // (width // QKV), 0, 0)),
        out_shape=jax.ShapeDtypeStruct((H, 3, rows // 2, 128), BF),
        compiler_params=pltpu.CompilerParams(vmem_limit_bytes=VMEM),
        name="qkv_rows",
    )(normed, gathered, cos_pair, sin_pair)


def qkv_back_kernel(grad_ref, weight_ref, out_ref, rows_s, total_s):
    half = grad_ref.shape[2]
    lane_low = lax.broadcasted_iota(jnp.int32, (half, 128), 1) < HD
    for pair in range(QKV // 128):
        even, odd = grad_ref[2 * pair, 0].astype(F32), grad_ref[2 * pair + 1, 0].astype(F32)
        at = pair * 128
        rows_s[:half, at : at + 128] = jnp.where(lane_low, even, pltpu.roll(odd, HD, 1)).astype(BF)
        rows_s[half:, at : at + 128] = jnp.where(lane_low, pltpu.roll(even, HD, 1), odd).astype(BF)
    product = mm_nt(weight_ref[...], rows_s[...])

    @pl.when(pl.program_id(0) == 0)
    def _():
        total_s[...] = product

    @pl.when(pl.program_id(0) > 0)
    def _():
        total_s[...] += product

    @pl.when(pl.program_id(0) == pl.num_programs(0) - 1)
    def _():
        out_ref[...] = jnp.transpose(total_s[...])


def qkv_back(grads, gathered, at):
    half = grads.shape[2]
    width = gathered.shape[0]
    return pl.pallas_call(
        qkv_back_kernel,
        grid=(3 * width // QKV,),
        in_specs=[
            pl.BlockSpec((QKV // HD, 1, half, 128), lambda i: (i % (width // QKV), i // (width // QKV), 0, 0)),
            pl.BlockSpec((width, QKV), lambda i: (0, at // QKV + i)),
        ],
        out_specs=whole((2 * half, width)),
        out_shape=jax.ShapeDtypeStruct((2 * half, width), F32),
        scratch_shapes=[pltpu.VMEM((2 * half, QKV), BF), pltpu.VMEM((width, 2 * half), F32)],
        compiler_params=pltpu.CompilerParams(vmem_limit_bytes=VMEM),
        name="qkv_back",
    )(grads, gathered)


def head_grad_kernel(branch_ref, weight_ref, out_ref):
    grad = jnp.transpose(mm_nt(weight_ref[...], branch_ref[...])).astype(BF).astype(F32)
    lane_low = lax.broadcasted_iota(jnp.int32, (grad.shape[0] // 2, 128), 1) < HD
    for pair in range(grad.shape[1] // 128):
        even, odd = pack_pair(grad[:, pair * 128 : pair * 128 + 128], lane_low)
        out_ref[2 * pair] = even.astype(BF)
        out_ref[2 * pair + 1] = odd.astype(BF)


def head_grads(branch, gathered, at):
    rows, width = branch.shape
    step = 4 * HD
    return pl.pallas_call(
        head_grad_kernel,
        grid=(width // step,),
        in_specs=[whole(branch.shape), pl.BlockSpec((step, width), lambda i: (i, at // width))],
        out_specs=pl.BlockSpec((4, rows // 2, 128), lambda i: (i, 0, 0)),
        out_shape=jax.ShapeDtypeStruct((H, rows // 2, 128), BF),
        compiler_params=pltpu.CompilerParams(vmem_limit_bytes=VMEM),
        name="head_grads",
    )(branch, gathered)


def unpack_kernel(in_ref, out_ref):
    parts, half = in_ref.shape[1], in_ref.shape[2]
    lane_low = lax.broadcasted_iota(jnp.int32, (half, 128), 1) < HD
    for part in range(parts):
        for pair in range(H // 2):
            even = in_ref[2 * pair, part].astype(F32)
            odd = in_ref[2 * pair + 1, part].astype(F32)
            top = jnp.where(lane_low, even, pltpu.roll(odd, HD, 1))
            bottom = jnp.where(lane_low, pltpu.roll(even, HD, 1), odd)
            at = (part * H + 2 * pair) * HD
            out_ref[:half, at : at + 128] = top.astype(BF)
            out_ref[half:, at : at + 128] = bottom.astype(BF)


def unpack_heads(packed):
    _, parts, half, _ = packed.shape
    return pl.pallas_call(
        unpack_kernel,
        out_shape=jax.ShapeDtypeStruct((2 * half, parts * H * HD), BF),
        compiler_params=pltpu.CompilerParams(vmem_limit_bytes=VMEM),
        name="unpack_heads",
    )(packed)


def lanes(top, bottom):
    low = lax.broadcasted_iota(jnp.int32, top.shape, 1) < HD
    return jnp.where(low, top, pltpu.roll(bottom, HD, 1)), jnp.where(low, pltpu.roll(top, HD, 1), bottom)


def split_kernel(left_ref, right_ref, out_ref):
    pairs = left_ref.shape[1] // 256
    for half, ref in enumerate((left_ref, right_ref)):
        for pair in range(pairs):
            at = pair * 256
            first, second = lanes(ref[:, at : at + 128].astype(F32), ref[:, at + 128 : at + 256].astype(F32))
            there = (half * pairs + pair) * 128
            out_ref[0, :, there : there + 128] = first.astype(out_ref.dtype)
            out_ref[1, :, there : there + 128] = second.astype(out_ref.dtype)


def split_pieces(left, right, blocks):
    tok, width = left.shape
    if width // blocks != HD:
        by_piece = jnp.concatenate([left, right], 1).reshape(tok, blocks, 2, width // blocks)
        return jnp.transpose(by_piece, (2, 0, 1, 3)).reshape(2, tok, width)
    return pl.pallas_call(
        split_kernel,
        out_shape=jax.ShapeDtypeStruct((2, tok, width), left.dtype),
        compiler_params=pltpu.CompilerParams(vmem_limit_bytes=VMEM),
        name="split_pieces",
    )(left, right)


def merge_kernel(first_ref, second_ref, left_ref, right_ref):
    pairs = left_ref.shape[1] // 256
    for half, ref in enumerate((left_ref, right_ref)):
        for pair in range(pairs):
            there = (half * pairs + pair) * 128
            even, odd = lanes(
                first_ref[:, there : there + 128].astype(F32), second_ref[:, there : there + 128].astype(F32)
            )
            at = pair * 256
            ref[:, at : at + 128] = even.astype(ref.dtype)
            ref[:, at + 128 : at + 256] = odd.astype(ref.dtype)


def merge_pieces(first, second, blocks, dtype):
    tok, width = first.shape
    if width // blocks != HD:
        both = jnp.stack([first.reshape(tok, blocks, -1), second.reshape(tok, blocks, -1)], 2)
        both = both.reshape(tok, 2 * width).astype(dtype)
        return both[:, :width], both[:, width:]
    return pl.pallas_call(
        merge_kernel,
        out_shape=[jax.ShapeDtypeStruct((tok, width), dtype)] * 2,
        compiler_params=pltpu.CompilerParams(vmem_limit_bytes=VMEM),
        name="merge_pieces",
    )(first, second)


def up_kernel(mine_ref, own_ref, other_ref, out_ref):
    width = own_ref.shape[1] // 2
    first = mine_ref[0] == 0
    for piece in range(2):
        for pair in range(width // 128):
            at = pair * 128
            tiles = []
            for s in range(2):
                own = own_ref[:, s * width + at : s * width + at + 128].astype(F32)
                other = other_ref[:, s * width + at : s * width + at + 128].astype(F32)
                tiles.append(jnp.where(first, own, other) if piece == 0 else jnp.where(first, other, own))
            even, odd = lanes(*tiles)
            out_ref[:, (4 * pair + piece) * 128 : (4 * pair + piece + 1) * 128] = even
            out_ref[:, (4 * pair + 2 + piece) * 128 : (4 * pair + 3 + piece) * 128] = odd


def up_columns(mine, own, other, blocks):
    rows, half = own.shape
    if half // 2 // blocks != HD:
        pair = jnp.where(mine == 0, jnp.stack([own, other]), jnp.stack([other, own]))
        pair = jnp.transpose(pair, (1, 0, 2)).reshape(rows, 4, blocks, half // 2 // blocks)
        return jnp.transpose(pair, (0, 2, 1, 3)).reshape(rows, 2 * half).astype(F32)
    return pl.pallas_call(
        up_kernel,
        in_specs=[pl.BlockSpec(memory_space=pltpu.SMEM), whole((rows, half)), whole((rows, half))],
        out_specs=whole((rows, 2 * half)),
        out_shape=jax.ShapeDtypeStruct((rows, 2 * half), F32),
        compiler_params=pltpu.CompilerParams(vmem_limit_bytes=VMEM),
        name="up_columns",
    )(mine.astype(jnp.int32).reshape(1), own, other)


def parts_kernel(planes, inner, core_ref, left_ref, right_ref, keep_ref, send_ref):
    first = core_ref[0] == 0
    step = pl.program_id(0)
    for z in range(planes):
        at = (step // inner * planes * inner + z * inner + step % inner) * 2 * HD
        grad = mm_tn(left_ref[:, pl.ds(pl.multiple_of(at, 2 * HD), 2 * HD)], right_ref[...])
        top, bottom = grad[:HD], grad[HD:]
        keep_ref[0, z] = jnp.where(first, top, bottom).astype(BF)
        send_ref[0, z] = jnp.where(first, bottom, top).astype(BF)


def grad_parts(left, right, me, planes, inner, rows):
    frames, columns = right.shape
    pieces = left.shape[1] // (planes * inner * 2 * rows)
    core, x = me % 2, me // 2 % inner
    if rows != HD:
        grad = mm_tn(left, right).astype(BF).reshape(pieces, planes, inner, 2, rows, columns)
        grad = jnp.stack([lax.dynamic_index_in_dim(grad, (x + k) % inner, 2, keepdims=False) for k in range(inner)])
        both = [lax.dynamic_index_in_dim(grad, c, 3, keepdims=False) for c in (core, 1 - core)]
        return [jnp.transpose(g, (0, 2, 1, 3, 4)).reshape(inner, planes, pieces * rows, columns) for g in both]

    def place(i, scalars):
        return (i % inner - scalars[1] + inner) % inner, 0, i // inner, 0

    shape = (inner, planes, pieces * rows, columns)
    return pl.pallas_call(
        functools.partial(parts_kernel, planes, inner),
        grid_spec=pltpu.PrefetchScalarGridSpec(
            num_scalar_prefetch=1,
            grid=(pieces * inner,),
            in_specs=[whole(left.shape), whole(right.shape)],
            out_specs=[pl.BlockSpec((1, planes, rows, columns), place)] * 2,
        ),
        out_shape=[jax.ShapeDtypeStruct(shape, BF)] * 2,
        compiler_params=pltpu.CompilerParams(vmem_limit_bytes=VMEM),
        name="grad_parts",
    )(jnp.stack([core, x]).astype(jnp.int32), left, right)


def rotated(rows, cosine, sine):
    swapped = jnp.concatenate([rows[:, HD // 2 :], rows[:, : HD // 2]], 1)
    return rows * cosine + swapped * sine


def put_packed(out_ref, step, rows, half, part=None):
    each = rows.shape[0] // (2 * half)
    for i in range(each):
        block = rows[2 * half * i : 2 * half * (i + 1)]
        joined = jnp.concatenate([block[:half], block[half:]], 1).astype(BF)
        if part is None:
            out_ref[step * each + i] = joined
        else:
            out_ref[step * each + i, part] = joined


def attend_kernel(qkv_ref, segc_ref, segr_ref, out_ref, attn_ref, lse_ref, q_ref, k_ref, v_ref, vt_s):
    g = pl.program_id(0)
    step_rows = SCORES // q_ref.shape[0]
    half = qkv_ref.shape[-2]
    tok = 2 * half

    @pl.when(g == 0)
    def _():
        for i in range(qkv_ref.shape[0]):
            for part, ref in enumerate((q_ref, k_ref, v_ref)):
                block = qkv_ref[i, part].astype(F32)
                ref[i * tok : i * tok + half] = block[:, :HD].astype(BF)
                ref[i * tok + half : (i + 1) * tok] = block[:, HD:].astype(BF)
        vt_s[...] = jnp.transpose(v_ref[...].astype(F32)).astype(BF)

    here = pl.ds(pl.multiple_of(g * step_rows, step_rows), step_rows)
    scores = mm_nt(k_ref[...], q_ref[here])
    allowed = segc_ref[...] == segr_ref[:, here]
    scores = jnp.where(allowed, scores, MASKED_SCORE)
    top = jnp.max(scores, 0, keepdims=True)
    weight = jnp.exp(scores - top)
    total = jnp.sum(weight, 0, keepdims=True)
    attn_t = mm(vt_s[...], weight.astype(BF)) / total
    attn_ref[:, here] = attn_t
    lse_ref[:, here] = top + jnp.log(total)
    put_packed(out_ref, g, jnp.transpose(attn_t), tok // 2)


def attend(qkv, seg):
    blocks, _, half, _ = qkv.shape
    total = blocks * half * 2
    return pl.pallas_call(
        attend_kernel,
        grid=(total // (SCORES // total),),
        in_specs=[whole(qkv.shape), whole((total, 1)), whole((1, total))],
        out_specs=[whole((blocks, half, 128)), whole((HD, total)), whole((1, total))] + [whole((total, HD))] * 3,
        out_shape=[
            jax.ShapeDtypeStruct((blocks, half, 128), BF),
            jax.ShapeDtypeStruct((HD, total), F32),
            jax.ShapeDtypeStruct((1, total), F32),
        ]
        + [jax.ShapeDtypeStruct((total, HD), BF)] * 3,
        scratch_shapes=[pltpu.VMEM((HD, total), BF)],
        compiler_params=pltpu.CompilerParams(vmem_limit_bytes=VMEM),
        cost_estimate=pl.CostEstimate(flops=int(1.6e10), bytes_accessed=8 << 20, transcendentals=0),
        name="attend",
    )(qkv, seg[:, None], seg[None, :])


def attend_back_kernel(
    q_ref, k_ref, v_ref, do_ref, attn_ref, lse_ref, segc_ref, segr_ref, cos_ref, sin_ref, normed_ref,
    out_ref, grad_ref, do_s, delta_s, dq_s, flat_s,
):
    g = pl.program_id(0)
    step_rows = SCORES // q_ref.shape[0]
    blocks = do_ref.shape[0]
    half = do_ref.shape[-2]
    tok = 2 * half
    scale = 1.0 / math.sqrt(HD)

    @pl.when(g == 0)
    def _():
        for i in range(blocks):
            block = do_ref[i].astype(F32)
            do_s[i * tok : i * tok + half] = block[:, :HD].astype(BF)
            do_s[i * tok + half : (i + 1) * tok] = block[:, HD:].astype(BF)
        do_t = jnp.transpose(do_s[...].astype(F32))
        delta_s[...] = jnp.sum(do_t * attn_ref[...], 0, keepdims=True)
        dq_s[...] = jnp.zeros_like(dq_s)

    here = pl.ds(pl.multiple_of(g * step_rows, step_rows), step_rows)
    keys = k_ref[here]
    scores = mm_nt(keys, q_ref[...])
    allowed = segc_ref[here] == segr_ref[...]
    probs = jnp.where(allowed, jnp.exp(scores - lse_ref[...]), 0.0)
    prob_grad = mm_nt(v_ref[here], do_s[...])
    score_grad = (probs * (prob_grad - delta_s[...])).astype(BF)
    value_grad = mm(probs.astype(BF), do_s[...])
    key_grad = mm(score_grad, q_ref[...])
    keys_t = jnp.transpose(keys.astype(F32)).astype(BF)
    dq_s[...] += mm(keys_t, score_grad)

    def put(part, step, rows, where):
        flat_s[part * HD : (part + 1) * HD, where] = jnp.transpose(rows).astype(BF)
        put_packed(out_ref, step, rows, half, part)

    put(1, g, rotated(key_grad, cos_ref[here], sin_ref[here]), here)
    put(2, g, value_grad, here)

    @pl.when(g == pl.num_programs(0) - 1)
    def _():
        for step in range(q_ref.shape[0] // step_rows):
            there = slice(step * step_rows, (step + 1) * step_rows)
            rows = jnp.transpose(dq_s[:, there]) * scale
            put(0, step, rotated(rows, cos_ref[there], sin_ref[there]), there)
        grad = jnp.transpose(mm(flat_s[...], normed_ref[...]))
        rows = grad.shape[0] // blocks
        for i in range(blocks):
            for part in range(3):
                block = grad[i * rows : (i + 1) * rows, part * HD : (part + 1) * HD]
                grad_ref[i, part] = jnp.concatenate([block[: rows // 2], block[rows // 2 :]], 1).astype(BF)


def attend_back(normed, q, k, v, attn_grad, attn_t, lse, seg, cos_rows, sin_rows):
    total, width = normed.shape
    blocks, half, _ = attn_grad.shape
    rows = width // blocks
    return pl.pallas_call(
        attend_back_kernel,
        grid=(total // (SCORES // total),),
        in_specs=[whole((total, HD))] * 3
        + [whole((blocks, half, 128)), whole((HD, total)), whole((1, total))]
        + [whole((total, 1)), whole((1, total)), whole((total, HD)), whole((total, HD))]
        + [whole((total, width))],
        out_specs=[whole((blocks, 3, half, 128)), whole((blocks, 3, rows // 2, 128))],
        out_shape=[
            jax.ShapeDtypeStruct((blocks, 3, half, 128), BF),
            jax.ShapeDtypeStruct((blocks, 3, rows // 2, 128), BF),
        ],
        scratch_shapes=[
            pltpu.VMEM((total, HD), BF),
            pltpu.VMEM((1, total), F32),
            pltpu.VMEM((HD, total), F32),
            pltpu.VMEM((3 * HD, total), BF),
        ],
        compiler_params=pltpu.CompilerParams(vmem_limit_bytes=VMEM),
        cost_estimate=pl.CostEstimate(flops=int(2.4e10), bytes_accessed=8 << 20, transcendentals=0),
        name="attend_back",
    )(q, k, v, attn_grad, attn_t, lse, seg[:, None], seg[None, :], cos_rows, sin_rows, normed)


def local(
    frames, skip_input, lengths, w_skip, b_skip, g_attn, w_qkv, w_out, g_ff, w_up, b_up, w_down, b_down, out_grad
):
    tok, width = frames.shape
    blocks = lax.axis_size("blk")
    packs = lax.axis_size("pack")
    me = lax.axis_index("blk")
    mine = lax.axis_index("pack") % 2
    rows = width // blocks
    repeat = blocks // H
    half = tok // 2
    planes = 4
    plane = blocks // planes
    spot = me % plane
    place = me // plane
    plane_groups = [[z * plane + j for j in range(plane)] for z in range(planes)]
    column_groups = [[z * plane + j for z in range(planes)] for j in range(plane)]
    swap = [(i, i ^ 1) for i in range(packs)]

    def to_peer(block):
        return lax.ppermute(block, "pack", swap)

    def over_pairs(block):
        total = block
        for k in range(1, packs // 2):
            total = total + lax.ppermute(block, "pack", [(i, (i + 2 * k) % packs) for i in range(packs)])
        return total

    def all_to_all(block, groups=None):
        return lax.all_to_all(block, "blk", 0, 0, tiled=True, axis_index_groups=groups)

    inner = plane // 2
    core = [(i, i ^ 1) for i in range(blocks)]

    def along_z(k):
        return [(i, (i + plane * k) % blocks) for i in range(blocks)]

    def along_x(k):
        return [(i, (i // plane) * plane + ((i % plane) // 2 + k) % inner * 2 + i % 2) for i in range(blocks)]

    def send(block, route):
        return lax.ppermute(block, "blk", route)

    def plane_blocks(block, beside=()):
        column = [block] + [send(block, along_x(k)) for k in range(1, inner)]
        if inner > 1:
            column = jnp.stack(column)
        else:
            column = column[0][None]
        column, beside = lax.optimization_barrier((column, beside))
        return jnp.concatenate([column, send(column, core)], 0), beside

    def plane_sources():
        return [(spot // 2 - k) % inner * 2 + ((spot % 2) ^ c) for c in range(2) for k in range(inner)]

    def own_half(block, axis):
        size = block.shape[axis] // 2
        return lax.dynamic_slice_in_dim(block, mine * size, size, axis)

    def at_index(block, index, axis=0):
        return lax.dynamic_index_in_dim(block, index, axis, keepdims=False)

    vectors = jnp.stack([b_skip, g_attn, g_ff, b_down] + list(b_up.reshape(4, rows)), 0)
    vectors = jnp.transpose(jnp.pad(vectors, ((0, 120), (0, 0))))
    up_cols = jnp.transpose(w_up.reshape(rows, blocks, 4, rows), (0, 2, 1, 3)).reshape(rows, 2, 2 * width)
    up_mine = at_index(up_cols, mine, 1)
    down_mine = own_half(w_down, 0)
    payload = jnp.concatenate(
        [w_skip[:rows], w_skip[rows:], w_qkv, w_out, up_mine, down_mine[:rows], down_mine[rows:], vectors], 1
    )
    gathered = lax.all_gather(payload, "blk", axis=0, tiled=True)

    pack_lengths = lengths[0]
    seg_all, offset_all = segment_of(jnp.arange(tok * blocks, dtype=jnp.int32), pack_lengths)
    cos_all, sin_all = angles(offset_all)
    cos_rows = jnp.concatenate([cos_all, cos_all], 1)
    sin_rows = jnp.concatenate([sin_all, -sin_all], 1)
    cosine = lax.dynamic_slice_in_dim(cos_all, me * tok, tok, 0)
    sine = lax.dynamic_slice_in_dim(sin_all, me * tok, tok, 0)
    cos_pair = jnp.concatenate([cosine] * 4, 1)
    sin_pair = jnp.concatenate([-sine, sine, -sine, sine], 1)
    pieces = split_pieces(frames, skip_input, blocks)
    gathered, pieces, cos_rows, sin_rows, cos_pair, sin_pair, seg_all = lax.optimization_barrier(
        (gathered, pieces, cos_rows, sin_rows, cos_pair, sin_pair, seg_all)
    )
    skip_a, skip_b = gathered[:, :width], gathered[:, width : 2 * width]
    gathered_more = gathered[:, 5 * width :]
    small = jnp.transpose(gathered[:, 10 * width :].astype(F32))[:8]
    bias_skip, gain_attn, gain_ff, bias_down = small[0], small[1], small[2], small[3]
    bias_up = lax.dynamic_slice_in_dim(small, 4 + 2 * mine, 2, 0).reshape(2 * width)

    def over_core(left, right):
        keep, other = grad_parts(left, right, me, planes, inner, rows)
        return (keep.astype(F32) + send(other, core).astype(F32)).astype(BF)

    def over_x(grad):
        total = grad[0].astype(F32)
        for k in range(1, inner):
            total = total + send(grad[k], along_x(k)).astype(F32)
        return total.astype(BF)

    def over_z(grad):
        total = lax.psum_scatter(
            grad.reshape(planes * grad.shape[1], grad.shape[2]),
            "blk",
            scatter_dimension=0,
            axis_index_groups=column_groups,
            tiled=True,
        )
        return over_pairs(total.astype(F32)).astype(BF) if packs > 2 else total

    def both(own, other):
        return jnp.where(mine == 0, jnp.stack([own, other]), jnp.stack([other, own]))

    stream_in = mm(pieces[0], skip_a) + mm(pieces[1], skip_b) + bias_skip
    root_in = lax.rsqrt(jnp.mean(stream_in * stream_in, -1, keepdims=True) + EPSILON)
    unit_in = stream_in * root_in
    normed_attn = (unit_in * gain_attn).astype(BF)
    qkv_packed = qkv_rows(normed_attn, gathered, 2 * width, cos_pair, sin_pair)
    if repeat > 1:
        qkv_packed = jnp.repeat(qkv_packed, repeat, 0)
    qkv_packed, grad_sent = lax.optimization_barrier((qkv_packed, out_grad))
    out_grad_two = jnp.concatenate([out_grad, to_peer(grad_sent)], 0)
    qkv_head, frames_late, skip_late = lax.optimization_barrier((all_to_all(qkv_packed), frames, skip_input))
    joined = jnp.concatenate([frames_late, skip_late], 1).reshape(tok, planes, plane, 2 * rows)
    joined = all_to_all(jnp.transpose(joined, (2, 0, 1, 3)).reshape(plane, tok, planes * 2 * rows), plane_groups)
    joined = jnp.concatenate([at_index(joined, source) for source in plane_sources()], 0)
    attn_packed, attn_t, lse, q_all, k_all, v_all = attend(qkv_head, seg_all)
    attn_packed, joined = lax.optimization_barrier((attn_packed, joined))
    attn_back = all_to_all(attn_packed)[::repeat]
    attn_back, normed_late, out_grad_two = lax.optimization_barrier((attn_back, normed_attn, out_grad_two))
    normed_full = lax.all_gather(normed_late, "blk", axis=0, tiled=True)
    attn_low = unpack_heads(attn_back[:, None])
    out_full = gathered_more[:, :width]
    up_half = gathered_more[:, width : 3 * width]
    down_a, down_b = gathered_more[:, 3 * width : 4 * width], gathered_more[:, 4 * width : 5 * width]
    stream_mid = stream_in + mm(attn_low, out_full)
    root_mid = lax.rsqrt(jnp.mean(stream_mid * stream_mid, -1, keepdims=True) + EPSILON)
    unit_mid = stream_mid * root_mid
    normed_ff = (unit_mid * gain_ff).astype(BF)
    normed_two = jnp.concatenate([normed_ff, to_peer(normed_ff)], 0)
    hidden_pre = mm(normed_two, up_half) + bias_up
    act_grad = jnp.concatenate([mm_nt(out_grad_two, down_a), mm_nt(out_grad_two, down_b)], 1)
    hidden, gelu_back = jax.vjp(activation, hidden_pre)
    hidden_act = hidden.astype(BF)
    pre_grad = gelu_back(act_grad)[0].astype(BF)
    ff_grad_two = mm_nt(pre_grad, up_half)
    ff_came = to_peer(ff_grad_two[tok:].astype(BF))
    down_low = [mm_tn(hidden_act[:, i * width : (i + 1) * width], out_grad_two).astype(BF) for i in range(2)]
    down_low = [low.reshape(planes, inner, 2, rows, width) for low in down_low]
    down_low = [
        (at_index(low, me % 2, 2).astype(F32) + send(at_index(low, 1 - me % 2, 2), core).astype(F32)).astype(BF)
        for low in down_low
    ]
    ff_came, down_low = lax.optimization_barrier((ff_came, down_low))
    ff_grad = ff_grad_two[:tok] + ff_came.astype(F32)

    scaled = ff_grad * gain_ff
    grad_gff = jnp.sum(ff_grad * unit_mid, 0)
    mid_grad = out_grad.astype(F32) + root_mid * (scaled - unit_mid * jnp.mean(scaled * unit_mid, -1, keepdims=True))
    branch_grad = mid_grad.astype(BF)
    attn_grad = head_grads(branch_grad, gathered, 5 * width)
    if repeat > 1:
        attn_grad = jnp.repeat(attn_grad, repeat, 0)

    hidden_act, normed_two, pre_grad, attn_grad = lax.optimization_barrier(
        (hidden_act, normed_two, pre_grad, attn_grad)
    )
    attn_grad_head = all_to_all(attn_grad)
    grad_bup = jnp.sum(pre_grad.astype(F32), 0)
    up_low, out_low = over_core(normed_two, pre_grad), over_core(attn_low, branch_grad)
    ff_two = mm(hidden_act[:, :width], down_a) + mm(hidden_act[:, width:], down_b)
    layer_out = (
        stream_mid + (ff_two[:tok] + to_peer(ff_two[tok:].astype(BF)).astype(F32)) + bias_down
    ).astype(BF)
    down_low = jnp.concatenate(down_low, 2)
    down_sum = over_x(jnp.stack([at_index(down_low, (spot // 2 + k) % inner, 1) for k in range(inner)]))
    attn_grad_head, down_sum, up_low, out_low, normed_full = lax.optimization_barrier(
        (attn_grad_head, down_sum, up_low, out_low, normed_full)
    )
    down_share = over_z(down_sum)
    up_sum, out_sum = over_x(up_low), over_x(out_low)

    dqkv_packed, folded = attend_back(
        normed_full, q_all, k_all, v_all, attn_grad_head, attn_t, lse, seg_all, cos_rows, sin_rows
    )
    dqkv_packed, up_sum = lax.optimization_barrier((dqkv_packed, up_sum))
    down_peer = to_peer(down_share)
    dqkv_back, up_sum, down_share, down_peer, layer_out = lax.optimization_barrier(
        (all_to_all(dqkv_packed)[::repeat], up_sum, down_share, down_peer, layer_out)
    )
    shares = over_z(jnp.concatenate([up_sum, out_sum], 2))
    normed_grad = qkv_back(dqkv_back, gathered, 2 * width)
    scaled_in = normed_grad * gain_attn
    grad_gattn = jnp.sum(normed_grad * unit_in, 0)
    in_grad = mid_grad + root_in * (scaled_in - unit_in * jnp.mean(scaled_in * unit_in, -1, keepdims=True))
    in_low = in_grad.astype(BF)
    folded, in_low = lax.optimization_barrier((folded, in_low))
    folded = all_to_all(folded)[::repeat]
    frames_grad, skip_grad = merge_pieces(mm_nt(in_low, skip_a), mm_nt(in_low, skip_b), blocks, BF)
    extra = [grad_gattn, grad_gff, jnp.sum(out_grad.astype(F32), 0)] + list(grad_bup.reshape(2, width))
    extra = jnp.pad(jnp.stack(extra).astype(BF), ((0, 11), (0, 0)))
    tail = jnp.concatenate([in_low, extra], 0)
    tails, (frames_grad, skip_grad, folded) = plane_blocks(tail[None], (frames_grad, skip_grad, folded))
    qkv_share = unpack_heads(folded)
    if packs > 2:
        qkv_share = over_pairs(qkv_share.astype(F32)).astype(BF)
    qkv_peer = to_peer(qkv_share)
    tails = tails.reshape(plane, tok + 16, width)
    low_all = tails[:, :tok].reshape(plane * tok, width)
    skip_part = mm_tn(joined, low_all).astype(BF).reshape(planes, 2 * rows, width)
    vec = jnp.sum(tails[:, tok : tok + 5].astype(F32), 0)
    vec = jnp.concatenate([jnp.sum(low_all.astype(F32), 0)[None], vec], 0)
    vec = jnp.pad(vec.astype(BF), ((0, 10), (0, 0)))
    payload = jnp.concatenate([skip_part, jnp.broadcast_to(vec[None], (planes, 16, width))], 1)
    payload, shares = lax.optimization_barrier((payload, shares))
    others = to_peer(shares)
    summed = at_index(payload, place).astype(F32)
    came = [send(at_index(payload, (place + k) % planes), along_z(k)) for k in range(1, planes)]
    came, qkv_peer, others = lax.optimization_barrier((came, qkv_peer, others))
    for block in came:
        summed = summed + block.astype(F32)
    if packs > 2:
        summed = over_pairs(summed)
    summed_peer = to_peer(summed.astype(BF)).astype(F32)
    total = summed + summed_peer
    w_skip_grad = total[: 2 * rows]
    own = lax.dynamic_slice_in_dim(total[2 * rows :], me * rows, rows, 1)
    b_up_grad = both(
        lax.dynamic_slice_in_dim(summed[2 * rows + 4 : 2 * rows + 6], me * rows, rows, 1),
        lax.dynamic_slice_in_dim(summed_peer[2 * rows + 4 : 2 * rows + 6], me * rows, rows, 1),
    ).reshape(4 * rows)
    w_qkv_grad = qkv_share.astype(F32) + qkv_peer.astype(F32)

    w_up_grad = up_columns(mine, shares[:, : 2 * width], others[:, : 2 * width], blocks)
    shares, others = shares[:, 2 * width :].astype(F32), others[:, 2 * width :].astype(F32)
    w_out_grad = shares + others
    w_down_grad = both(down_share, down_peer).reshape(4 * rows, width).astype(F32)
    return (
        layer_out, frames_grad, skip_grad, w_skip_grad, own[0], own[1], w_qkv_grad, w_out_grad, own[2],
        w_up_grad, b_up_grad, w_down_grad, own[3],
    )


def solution(mesh):
    token_spec = P(("pack", "blk"), None)
    matrix, vector = P("blk", None), P("blk")
    return jax.shard_map(
        local,
        mesh=mesh,
        in_specs=(
            token_spec, token_spec, P("pack", None), matrix, vector, vector, matrix, matrix, vector, matrix, vector,
            matrix, vector, token_spec,
        ),
        out_specs=(
            token_spec, token_spec, token_spec, matrix, vector, vector, matrix, matrix, vector, matrix, vector, matrix,
            vector,
        ),
        check_vma=False,
    )
```

```python
import functools
import math

import jax
import jax.numpy as jnp
from jax import lax
from jax.experimental import pallas as pl
from jax.experimental.pallas import tpu as pltpu
from jax.sharding import PartitionSpec as P

H = 16
HD = 64
EPSILON = 1e-06
MASKED_SCORE = -1e30
SCORES = 2048 * 2048
QKV = 1024
VMEM = 56 * 1024 * 1024
BF = jnp.bfloat16
F32 = jnp.float32


def mm(left, right):
    return jnp.dot(left, right, preferred_element_type=F32)


def mm_nt(left, right):
    return lax.dot_general(left, right, (((1,), (1,)), ((), ())), preferred_element_type=F32)


def mm_tn(left, right):
    return lax.dot_general(left, right, (((0,), (0,)), ((), ())), preferred_element_type=F32)


def whole(shape):
    return pl.BlockSpec(shape, lambda *_: (0,) * len(shape))


def segment_of(position, lengths_row):
    bounds = jnp.cumsum(lengths_row)
    after = position[:, None] >= bounds[None, :]
    segment = jnp.sum(after.astype(jnp.int32), 1, dtype=jnp.int32)
    before = jnp.sum(jnp.where(after, lengths_row[None, :], 0), 1, dtype=jnp.int32)
    return segment, position - before


def angles(offset):
    freq = 10000.0 ** (-(jnp.arange(HD // 2, dtype=F32) * 2.0 / HD))
    angle = offset.astype(F32)[:, None] * freq[None, :]
    return jnp.cos(angle), jnp.sin(angle)


def activation(value):
    return jax.nn.gelu(value, approximate=True)


def pack_pair(block, lane_low):
    half = block.shape[0] // 2
    top, bottom = block[:half], block[half:]
    even = jnp.where(lane_low, top, pltpu.roll(bottom, HD, 1))
    odd = jnp.where(lane_low, pltpu.roll(top, HD, 1), bottom)
    return even, odd


def qkv_kernel(normed_ref, weight_ref, cos_ref, sin_ref, out_ref):
    step = pl.program_id(0)
    projected = mm(normed_ref[...], weight_ref[...])
    rows = projected.shape[0]
    lane = lax.broadcasted_iota(jnp.int32, (rows, 128), 1)
    first = (lane % HD) < HD // 2
    lane_low = lane[: rows // 2] < HD
    per_part = normed_ref.shape[1] // QKV
    scale = jnp.where(step < per_part, 1.0 / math.sqrt(HD), 1.0)
    for pair in range(QKV // 128):
        block = projected[:, pair * 128 : pair * 128 + 128]
        swapped = jnp.where(first, pltpu.roll(block, 128 - HD // 2, 1), pltpu.roll(block, HD // 2, 1))
        block = jnp.where(step < 2 * per_part, block * cos_ref[...] + swapped * sin_ref[...], block)
        even, odd = pack_pair(block.astype(BF).astype(F32) * scale, lane_low)
        out_ref[2 * pair, 0] = even.astype(BF)
        out_ref[2 * pair + 1, 0] = odd.astype(BF)


def qkv_rows(normed, gathered, at, cos_pair, sin_pair):
    rows, width = normed.shape
    return pl.pallas_call(
        qkv_kernel,
        grid=(3 * width // QKV,),
        in_specs=[
            whole(normed.shape), pl.BlockSpec((width, QKV), lambda i: (0, at // QKV + i)), whole((rows, 128)),
            whole((rows, 128)),
        ],
        out_specs=pl.BlockSpec((QKV // HD, 1, rows // 2, 128), lambda i: (i % (width // QKV), i // (width // QKV), 0, 0)),
        out_shape=jax.ShapeDtypeStruct((H, 3, rows // 2, 128), BF),
        compiler_params=pltpu.CompilerParams(vmem_limit_bytes=VMEM),
        name="qkv_rows",
    )(normed, gathered, cos_pair, sin_pair)


def qkv_back_kernel(grad_ref, weight_ref, out_ref, rows_s, total_s):
    half = grad_ref.shape[2]
    lane_low = lax.broadcasted_iota(jnp.int32, (half, 128), 1) < HD
    for pair in range(QKV // 128):
        even, odd = grad_ref[2 * pair, 0].astype(F32), grad_ref[2 * pair + 1, 0].astype(F32)
        at = pair * 128
        rows_s[:half, at : at + 128] = jnp.where(lane_low, even, pltpu.roll(odd, HD, 1)).astype(BF)
        rows_s[half:, at : at + 128] = jnp.where(lane_low, pltpu.roll(even, HD, 1), odd).astype(BF)
    product = mm_nt(weight_ref[...], rows_s[...])

    @pl.when(pl.program_id(0) == 0)
    def _():
        total_s[...] = product

    @pl.when(pl.program_id(0) > 0)
    def _():
        total_s[...] += product

    @pl.when(pl.program_id(0) == pl.num_programs(0) - 1)
    def _():
        out_ref[...] = jnp.transpose(total_s[...])


def qkv_back(grads, gathered, at):
    half = grads.shape[2]
    width = gathered.shape[0]
    return pl.pallas_call(
        qkv_back_kernel,
        grid=(3 * width // QKV,),
        in_specs=[
            pl.BlockSpec((QKV // HD, 1, half, 128), lambda i: (i % (width // QKV), i // (width // QKV), 0, 0)),
            pl.BlockSpec((width, QKV), lambda i: (0, at // QKV + i)),
        ],
        out_specs=whole((2 * half, width)),
        out_shape=jax.ShapeDtypeStruct((2 * half, width), F32),
        scratch_shapes=[pltpu.VMEM((2 * half, QKV), BF), pltpu.VMEM((width, 2 * half), F32)],
        compiler_params=pltpu.CompilerParams(vmem_limit_bytes=VMEM),
        name="qkv_back",
    )(grads, gathered)


def head_grad_kernel(branch_ref, weight_ref, out_ref):
    grad = jnp.transpose(mm_nt(weight_ref[...], branch_ref[...])).astype(BF).astype(F32)
    lane_low = lax.broadcasted_iota(jnp.int32, (grad.shape[0] // 2, 128), 1) < HD
    for pair in range(grad.shape[1] // 128):
        even, odd = pack_pair(grad[:, pair * 128 : pair * 128 + 128], lane_low)
        out_ref[2 * pair] = even.astype(BF)
        out_ref[2 * pair + 1] = odd.astype(BF)


def head_grads(branch, gathered, at):
    rows, width = branch.shape
    step = 4 * HD
    return pl.pallas_call(
        head_grad_kernel,
        grid=(width // step,),
        in_specs=[whole(branch.shape), pl.BlockSpec((step, width), lambda i: (i, at // width))],
        out_specs=pl.BlockSpec((4, rows // 2, 128), lambda i: (i, 0, 0)),
        out_shape=jax.ShapeDtypeStruct((H, rows // 2, 128), BF),
        compiler_params=pltpu.CompilerParams(vmem_limit_bytes=VMEM),
        name="head_grads",
    )(branch, gathered)


def unpack_kernel(in_ref, out_ref):
    parts, half = in_ref.shape[1], in_ref.shape[2]
    lane_low = lax.broadcasted_iota(jnp.int32, (half, 128), 1) < HD
    for part in range(parts):
        for pair in range(H // 2):
            even = in_ref[2 * pair, part].astype(F32)
            odd = in_ref[2 * pair + 1, part].astype(F32)
            top = jnp.where(lane_low, even, pltpu.roll(odd, HD, 1))
            bottom = jnp.where(lane_low, pltpu.roll(even, HD, 1), odd)
            at = (part * H + 2 * pair) * HD
            out_ref[:half, at : at + 128] = top.astype(BF)
            out_ref[half:, at : at + 128] = bottom.astype(BF)


def unpack_heads(packed):
    _, parts, half, _ = packed.shape
    return pl.pallas_call(
        unpack_kernel,
        out_shape=jax.ShapeDtypeStruct((2 * half, parts * H * HD), BF),
        compiler_params=pltpu.CompilerParams(vmem_limit_bytes=VMEM),
        name="unpack_heads",
    )(packed)


def lanes(top, bottom):
    low = lax.broadcasted_iota(jnp.int32, top.shape, 1) < HD
    return jnp.where(low, top, pltpu.roll(bottom, HD, 1)), jnp.where(low, pltpu.roll(top, HD, 1), bottom)


def split_kernel(left_ref, right_ref, out_ref):
    pairs = left_ref.shape[1] // 256
    for half, ref in enumerate((left_ref, right_ref)):
        for pair in range(pairs):
            at = pair * 256
            first, second = lanes(ref[:, at : at + 128].astype(F32), ref[:, at + 128 : at + 256].astype(F32))
            there = (half * pairs + pair) * 128
            out_ref[0, :, there : there + 128] = first.astype(out_ref.dtype)
            out_ref[1, :, there : there + 128] = second.astype(out_ref.dtype)


def split_pieces(left, right, blocks):
    tok, width = left.shape
    if width // blocks != HD:
        by_piece = jnp.concatenate([left, right], 1).reshape(tok, blocks, 2, width // blocks)
        return jnp.transpose(by_piece, (2, 0, 1, 3)).reshape(2, tok, width)
    return pl.pallas_call(
        split_kernel,
        out_shape=jax.ShapeDtypeStruct((2, tok, width), left.dtype),
        compiler_params=pltpu.CompilerParams(vmem_limit_bytes=VMEM),
        name="split_pieces",
    )(left, right)


def merge_kernel(first_ref, second_ref, left_ref, right_ref):
    pairs = left_ref.shape[1] // 256
    for half, ref in enumerate((left_ref, right_ref)):
        for pair in range(pairs):
            there = (half * pairs + pair) * 128
            even, odd = lanes(
                first_ref[:, there : there + 128].astype(F32), second_ref[:, there : there + 128].astype(F32)
            )
            at = pair * 256
            ref[:, at : at + 128] = even.astype(ref.dtype)
            ref[:, at + 128 : at + 256] = odd.astype(ref.dtype)


def merge_pieces(first, second, blocks, dtype):
    tok, width = first.shape
    if width // blocks != HD:
        both = jnp.stack([first.reshape(tok, blocks, -1), second.reshape(tok, blocks, -1)], 2)
        both = both.reshape(tok, 2 * width).astype(dtype)
        return both[:, :width], both[:, width:]
    return pl.pallas_call(
        merge_kernel,
        out_shape=[jax.ShapeDtypeStruct((tok, width), dtype)] * 2,
        compiler_params=pltpu.CompilerParams(vmem_limit_bytes=VMEM),
        name="merge_pieces",
    )(first, second)


def up_kernel(mine_ref, own_ref, other_ref, out_ref):
    width = own_ref.shape[1] // 2
    first = mine_ref[0] == 0
    for piece in range(2):
        for pair in range(width // 128):
            at = pair * 128
            tiles = []
            for s in range(2):
                own = own_ref[:, s * width + at : s * width + at + 128].astype(F32)
                other = other_ref[:, s * width + at : s * width + at + 128].astype(F32)
                tiles.append(jnp.where(first, own, other) if piece == 0 else jnp.where(first, other, own))
            even, odd = lanes(*tiles)
            out_ref[:, (4 * pair + piece) * 128 : (4 * pair + piece + 1) * 128] = even
            out_ref[:, (4 * pair + 2 + piece) * 128 : (4 * pair + 3 + piece) * 128] = odd


def up_columns(mine, own, other, blocks):
    rows, half = own.shape
    if half // 2 // blocks != HD:
        pair = jnp.where(mine == 0, jnp.stack([own, other]), jnp.stack([other, own]))
        pair = jnp.transpose(pair, (1, 0, 2)).reshape(rows, 4, blocks, half // 2 // blocks)
        return jnp.transpose(pair, (0, 2, 1, 3)).reshape(rows, 2 * half).astype(F32)
    return pl.pallas_call(
        up_kernel,
        in_specs=[pl.BlockSpec(memory_space=pltpu.SMEM), whole((rows, half)), whole((rows, half))],
        out_specs=whole((rows, 2 * half)),
        out_shape=jax.ShapeDtypeStruct((rows, 2 * half), F32),
        compiler_params=pltpu.CompilerParams(vmem_limit_bytes=VMEM),
        name="up_columns",
    )(mine.astype(jnp.int32).reshape(1), own, other)


def parts_kernel(planes, inner, core_ref, left_ref, right_ref, keep_ref, send_ref):
    first = core_ref[0] == 0
    step = pl.program_id(0)
    for z in range(planes):
        at = (step // inner * planes * inner + z * inner + step % inner) * 2 * HD
        grad = mm_tn(left_ref[:, pl.ds(pl.multiple_of(at, 2 * HD), 2 * HD)], right_ref[...])
        top, bottom = grad[:HD], grad[HD:]
        keep_ref[0, z] = jnp.where(first, top, bottom).astype(BF)
        send_ref[0, z] = jnp.where(first, bottom, top).astype(BF)


def grad_parts(left, right, me, planes, inner, rows):
    frames, columns = right.shape
    pieces = left.shape[1] // (planes * inner * 2 * rows)
    core, x = me % 2, me // 2 % inner
    if rows != HD:
        grad = mm_tn(left, right).astype(BF).reshape(pieces, planes, inner, 2, rows, columns)
        grad = jnp.stack([lax.dynamic_index_in_dim(grad, (x + k) % inner, 2, keepdims=False) for k in range(inner)])
        both = [lax.dynamic_index_in_dim(grad, c, 3, keepdims=False) for c in (core, 1 - core)]
        return [jnp.transpose(g, (0, 2, 1, 3, 4)).reshape(inner, planes, pieces * rows, columns) for g in both]

    def place(i, scalars):
        return (i % inner - scalars[1] + inner) % inner, 0, i // inner, 0

    shape = (inner, planes, pieces * rows, columns)
    return pl.pallas_call(
        functools.partial(parts_kernel, planes, inner),
        grid_spec=pltpu.PrefetchScalarGridSpec(
            num_scalar_prefetch=1,
            grid=(pieces * inner,),
            in_specs=[whole(left.shape), whole(right.shape)],
            out_specs=[pl.BlockSpec((1, planes, rows, columns), place)] * 2,
        ),
        out_shape=[jax.ShapeDtypeStruct(shape, BF)] * 2,
        compiler_params=pltpu.CompilerParams(vmem_limit_bytes=VMEM),
        name="grad_parts",
    )(jnp.stack([core, x]).astype(jnp.int32), left, right)


def rotated(rows, cosine, sine):
    swapped = jnp.concatenate([rows[:, HD // 2 :], rows[:, : HD // 2]], 1)
    return rows * cosine + swapped * sine


def put_packed(out_ref, step, rows, half, part=None):
    each = rows.shape[0] // (2 * half)
    for i in range(each):
        block = rows[2 * half * i : 2 * half * (i + 1)]
        joined = jnp.concatenate([block[:half], block[half:]], 1).astype(BF)
        if part is None:
            out_ref[step * each + i] = joined
        else:
            out_ref[step * each + i, part] = joined


def attend_kernel(qkv_ref, segc_ref, segr_ref, out_ref, attn_ref, lse_ref, q_ref, k_ref, v_ref, vt_s):
    g = pl.program_id(0)
    step_rows = SCORES // q_ref.shape[0]
    half = qkv_ref.shape[-2]
    tok = 2 * half

    @pl.when(g == 0)
    def _():
        for i in range(qkv_ref.shape[0]):
            for part, ref in enumerate((q_ref, k_ref, v_ref)):
                block = qkv_ref[i, part].astype(F32)
                ref[i * tok : i * tok + half] = block[:, :HD].astype(BF)
                ref[i * tok + half : (i + 1) * tok] = block[:, HD:].astype(BF)
        vt_s[...] = jnp.transpose(v_ref[...].astype(F32)).astype(BF)

    here = pl.ds(pl.multiple_of(g * step_rows, step_rows), step_rows)
    scores = mm_nt(k_ref[...], q_ref[here])
    allowed = segc_ref[...] == segr_ref[:, here]
    scores = jnp.where(allowed, scores, MASKED_SCORE)
    top = jnp.max(scores, 0, keepdims=True)
    weight = jnp.exp(scores - top)
    total = jnp.sum(weight, 0, keepdims=True)
    attn_t = mm(vt_s[...], weight.astype(BF)) / total
    attn_ref[:, here] = attn_t
    lse_ref[:, here] = top + jnp.log(total)
    put_packed(out_ref, g, jnp.transpose(attn_t), tok // 2)


def attend(qkv, seg):
    blocks, _, half, _ = qkv.shape
    total = blocks * half * 2
    return pl.pallas_call(
        attend_kernel,
        grid=(total // (SCORES // total),),
        in_specs=[whole(qkv.shape), whole((total, 1)), whole((1, total))],
        out_specs=[whole((blocks, half, 128)), whole((HD, total)), whole((1, total))] + [whole((total, HD))] * 3,
        out_shape=[
            jax.ShapeDtypeStruct((blocks, half, 128), BF),
            jax.ShapeDtypeStruct((HD, total), F32),
            jax.ShapeDtypeStruct((1, total), F32),
        ]
        + [jax.ShapeDtypeStruct((total, HD), BF)] * 3,
        scratch_shapes=[pltpu.VMEM((HD, total), BF)],
        compiler_params=pltpu.CompilerParams(vmem_limit_bytes=VMEM),
        cost_estimate=pl.CostEstimate(flops=int(1.6e10), bytes_accessed=8 << 20, transcendentals=0),
        name="attend",
    )(qkv, seg[:, None], seg[None, :])


def attend_back_kernel(
    q_ref, k_ref, v_ref, do_ref, attn_ref, lse_ref, segc_ref, segr_ref, cos_ref, sin_ref,
    out_ref, flat_s, do_s, delta_s, dq_s,
):
    g = pl.program_id(0)
    step_rows = SCORES // q_ref.shape[0]
    blocks = do_ref.shape[0]
    half = do_ref.shape[-2]
    tok = 2 * half
    scale = 1.0 / math.sqrt(HD)

    @pl.when(g == 0)
    def _():
        for i in range(blocks):
            block = do_ref[i].astype(F32)
            do_s[i * tok : i * tok + half] = block[:, :HD].astype(BF)
            do_s[i * tok + half : (i + 1) * tok] = block[:, HD:].astype(BF)
        do_t = jnp.transpose(do_s[...].astype(F32))
        delta_s[...] = jnp.sum(do_t * attn_ref[...], 0, keepdims=True)
        dq_s[...] = jnp.zeros_like(dq_s)

    here = pl.ds(pl.multiple_of(g * step_rows, step_rows), step_rows)
    keys = k_ref[here]
    scores = mm_nt(keys, q_ref[...])
    allowed = segc_ref[here] == segr_ref[...]
    probs = jnp.where(allowed, jnp.exp(scores - lse_ref[...]), 0.0)
    prob_grad = mm_nt(v_ref[here], do_s[...])
    score_grad = (probs * (prob_grad - delta_s[...])).astype(BF)
    value_grad = mm(probs.astype(BF), do_s[...])
    key_grad = mm(score_grad, q_ref[...])
    keys_t = jnp.transpose(keys.astype(F32)).astype(BF)
    dq_s[...] += mm(keys_t, score_grad)

    def put(part, step, rows, where):
        flat_s[part * HD : (part + 1) * HD, where] = jnp.transpose(rows).astype(BF)
        put_packed(out_ref, step, rows, half, part)

    put(1, g, rotated(key_grad, cos_ref[here], sin_ref[here]), here)
    put(2, g, value_grad, here)

    @pl.when(g == pl.num_programs(0) - 1)
    def _():
        for step in range(q_ref.shape[0] // step_rows):
            there = slice(step * step_rows, (step + 1) * step_rows)
            rows = jnp.transpose(dq_s[:, there]) * scale
            put(0, step, rotated(rows, cos_ref[there], sin_ref[there]), there)


def qkv_grad_kernel(flat_ref, normed_ref, grad_ref):
    blocks = grad_ref.shape[0]
    grad = jnp.transpose(mm(flat_ref[...], normed_ref[...]))
    rows = grad.shape[0] // blocks
    for i in range(blocks):
        for part in range(3):
            block = grad[i * rows : (i + 1) * rows, part * HD : (part + 1) * HD]
            grad_ref[i, part] = jnp.concatenate([block[: rows // 2], block[rows // 2 :]], 1).astype(BF)


def qkv_grads(flat, normed, blocks):
    rows = normed.shape[1] // blocks
    return pl.pallas_call(
        qkv_grad_kernel,
        out_shape=jax.ShapeDtypeStruct((blocks, 3, rows // 2, 128), BF),
        compiler_params=pltpu.CompilerParams(vmem_limit_bytes=VMEM),
        name="qkv_grads",
    )(flat, normed)


def attend_back(q, k, v, attn_grad, attn_t, lse, seg, cos_rows, sin_rows):
    total = q.shape[0]
    blocks, half, _ = attn_grad.shape
    return pl.pallas_call(
        attend_back_kernel,
        grid=(total // (SCORES // total),),
        in_specs=[whole((total, HD))] * 3
        + [whole((blocks, half, 128)), whole((HD, total)), whole((1, total))]
        + [whole((total, 1)), whole((1, total)), whole((total, HD)), whole((total, HD))],
        out_specs=[whole((blocks, 3, half, 128)), whole((3 * HD, total))],
        out_shape=[
            jax.ShapeDtypeStruct((blocks, 3, half, 128), BF),
            jax.ShapeDtypeStruct((3 * HD, total), BF),
        ],
        scratch_shapes=[
            pltpu.VMEM((total, HD), BF),
            pltpu.VMEM((1, total), F32),
            pltpu.VMEM((HD, total), F32),
        ],
        compiler_params=pltpu.CompilerParams(vmem_limit_bytes=VMEM),
        cost_estimate=pl.CostEstimate(flops=int(2.4e10), bytes_accessed=8 << 20, transcendentals=0),
        name="attend_back",
    )(q, k, v, attn_grad, attn_t, lse, seg[:, None], seg[None, :], cos_rows, sin_rows)


def local(
    frames, skip_input, lengths, w_skip, b_skip, g_attn, w_qkv, w_out, g_ff, w_up, b_up, w_down, b_down, out_grad
):
    tok, width = frames.shape
    blocks = lax.axis_size("blk")
    packs = lax.axis_size("pack")
    me = lax.axis_index("blk")
    mine = lax.axis_index("pack") % 2
    rows = width // blocks
    repeat = blocks // H
    half = tok // 2
    planes = 4
    plane = blocks // planes
    spot = me % plane
    place = me // plane
    plane_groups = [[z * plane + j for j in range(plane)] for z in range(planes)]
    column_groups = [[z * plane + j for z in range(planes)] for j in range(plane)]
    swap = [(i, i ^ 1) for i in range(packs)]

    def to_peer(block):
        return lax.ppermute(block, "pack", swap)

    def over_pairs(block):
        total = block
        for k in range(1, packs // 2):
            total = total + lax.ppermute(block, "pack", [(i, (i + 2 * k) % packs) for i in range(packs)])
        return total

    def all_to_all(block, groups=None):
        return lax.all_to_all(block, "blk", 0, 0, tiled=True, axis_index_groups=groups)

    inner = plane // 2
    core = [(i, i ^ 1) for i in range(blocks)]

    def along_z(k):
        return [(i, (i + plane * k) % blocks) for i in range(blocks)]

    def along_x(k):
        return [(i, (i // plane) * plane + ((i % plane) // 2 + k) % inner * 2 + i % 2) for i in range(blocks)]

    def send(block, route):
        return lax.ppermute(block, "blk", route)

    def plane_blocks(block, beside=()):
        column = [block] + [send(block, along_x(k)) for k in range(1, inner)]
        if inner > 1:
            column = jnp.stack(column)
        else:
            column = column[0][None]
        column, beside = lax.optimization_barrier((column, beside))
        return jnp.concatenate([column, send(column, core)], 0), beside

    def plane_sources():
        return [(spot // 2 - k) % inner * 2 + ((spot % 2) ^ c) for c in range(2) for k in range(inner)]

    def own_half(block, axis):
        size = block.shape[axis] // 2
        return lax.dynamic_slice_in_dim(block, mine * size, size, axis)

    def at_index(block, index, axis=0):
        return lax.dynamic_index_in_dim(block, index, axis, keepdims=False)

    vectors = jnp.stack([b_skip, g_attn, g_ff, b_down] + list(b_up.reshape(4, rows)), 0)
    vectors = jnp.transpose(jnp.pad(vectors, ((0, 120), (0, 0))))
    up_cols = jnp.transpose(w_up.reshape(rows, blocks, 4, rows), (0, 2, 1, 3)).reshape(rows, 2, 2 * width)
    up_mine = at_index(up_cols, mine, 1)
    down_mine = own_half(w_down, 0)
    payload = jnp.concatenate(
        [w_skip[:rows], w_skip[rows:], w_qkv, w_out, up_mine, down_mine[:rows], down_mine[rows:], vectors], 1
    )
    gathered = lax.all_gather(payload, "blk", axis=0, tiled=True)

    pack_lengths = lengths[0]
    seg_all, offset_all = segment_of(jnp.arange(tok * blocks, dtype=jnp.int32), pack_lengths)
    cos_all, sin_all = angles(offset_all)
    cos_rows = jnp.concatenate([cos_all, cos_all], 1)
    sin_rows = jnp.concatenate([sin_all, -sin_all], 1)
    cosine = lax.dynamic_slice_in_dim(cos_all, me * tok, tok, 0)
    sine = lax.dynamic_slice_in_dim(sin_all, me * tok, tok, 0)
    cos_pair = jnp.concatenate([cosine] * 4, 1)
    sin_pair = jnp.concatenate([-sine, sine, -sine, sine], 1)
    pieces = split_pieces(frames, skip_input, blocks)
    gathered, pieces, cos_rows, sin_rows, cos_pair, sin_pair, seg_all = lax.optimization_barrier(
        (gathered, pieces, cos_rows, sin_rows, cos_pair, sin_pair, seg_all)
    )
    skip_a, skip_b = gathered[:, :width], gathered[:, width : 2 * width]
    gathered_more = gathered[:, 5 * width :]
    small = jnp.transpose(gathered[:, 10 * width :].astype(F32))[:8]
    bias_skip, gain_attn, gain_ff, bias_down = small[0], small[1], small[2], small[3]
    bias_up = lax.dynamic_slice_in_dim(small, 4 + 2 * mine, 2, 0).reshape(2 * width)

    def over_core(left, right):
        keep, other = grad_parts(left, right, me, planes, inner, rows)
        return (keep.astype(F32) + send(other, core).astype(F32)).astype(BF)

    def over_x(grad):
        total = grad[0].astype(F32)
        for k in range(1, inner):
            total = total + send(grad[k], along_x(k)).astype(F32)
        return total.astype(BF)

    def x_parts(grad):
        return [grad[0]] + [send(grad[k], along_x(k)) for k in range(1, inner)]

    def added(parts):
        return sum(part.astype(F32) for part in parts).astype(BF)

    def over_z(grad):
        total = lax.psum_scatter(
            grad.reshape(planes * grad.shape[1], grad.shape[2]),
            "blk",
            scatter_dimension=0,
            axis_index_groups=column_groups,
            tiled=True,
        )
        return over_pairs(total.astype(F32)).astype(BF) if packs > 2 else total

    def both(own, other):
        return jnp.where(mine == 0, jnp.stack([own, other]), jnp.stack([other, own]))

    stream_in = mm(pieces[0], skip_a) + mm(pieces[1], skip_b) + bias_skip
    root_in = lax.rsqrt(jnp.mean(stream_in * stream_in, -1, keepdims=True) + EPSILON)
    unit_in = stream_in * root_in
    normed_attn = (unit_in * gain_attn).astype(BF)
    qkv_packed = qkv_rows(normed_attn, gathered, 2 * width, cos_pair, sin_pair)
    if repeat > 1:
        qkv_packed = jnp.repeat(qkv_packed, repeat, 0)
    qkv_packed, grad_sent = lax.optimization_barrier((qkv_packed, out_grad))
    out_grad_two = jnp.concatenate([out_grad, to_peer(grad_sent)], 0)
    qkv_head, frames_late, skip_late = lax.optimization_barrier((all_to_all(qkv_packed), frames, skip_input))
    joined = jnp.concatenate([frames_late, skip_late], 1).reshape(tok, planes, plane, 2 * rows)
    joined = all_to_all(jnp.transpose(joined, (2, 0, 1, 3)).reshape(plane, tok, planes * 2 * rows), plane_groups)
    joined = jnp.concatenate([at_index(joined, source) for source in plane_sources()], 0)
    attn_packed, attn_t, lse, q_all, k_all, v_all = attend(qkv_head, seg_all)
    attn_packed, joined = lax.optimization_barrier((attn_packed, joined))
    attn_back = all_to_all(attn_packed)[::repeat]
    attn_back, normed_late, out_grad_two = lax.optimization_barrier((attn_back, normed_attn, out_grad_two))
    normed_full = lax.all_gather(normed_late, "blk", axis=0, tiled=True)
    attn_low = unpack_heads(attn_back[:, None])
    out_full = gathered_more[:, :width]
    up_half = gathered_more[:, width : 3 * width]
    down_a, down_b = gathered_more[:, 3 * width : 4 * width], gathered_more[:, 4 * width : 5 * width]
    stream_mid = stream_in + mm(attn_low, out_full)
    root_mid = lax.rsqrt(jnp.mean(stream_mid * stream_mid, -1, keepdims=True) + EPSILON)
    unit_mid = stream_mid * root_mid
    normed_ff = (unit_mid * gain_ff).astype(BF)
    normed_two = jnp.concatenate([normed_ff, to_peer(normed_ff)], 0)
    hidden_pre = mm(normed_two, up_half) + bias_up
    act_grad = jnp.concatenate([mm_nt(out_grad_two, down_a), mm_nt(out_grad_two, down_b)], 1)
    hidden, gelu_back = jax.vjp(activation, hidden_pre)
    hidden_act = hidden.astype(BF)
    pre_grad = gelu_back(act_grad)[0].astype(BF)
    ff_grad_two = mm_nt(pre_grad, up_half)
    ff_came = to_peer(ff_grad_two[tok:].astype(BF))
    down_low = [mm_tn(hidden_act[:, i * width : (i + 1) * width], out_grad_two).astype(BF) for i in range(2)]
    down_low = [low.reshape(planes, inner, 2, rows, width) for low in down_low]
    down_low = [
        (at_index(low, me % 2, 2).astype(F32) + send(at_index(low, 1 - me % 2, 2), core).astype(F32)).astype(BF)
        for low in down_low
    ]
    ff_came, down_low = lax.optimization_barrier((ff_came, down_low))
    ff_grad = ff_grad_two[:tok] + ff_came.astype(F32)

    scaled = ff_grad * gain_ff
    grad_gff = jnp.sum(ff_grad * unit_mid, 0)
    mid_grad = out_grad.astype(F32) + root_mid * (scaled - unit_mid * jnp.mean(scaled * unit_mid, -1, keepdims=True))
    branch_grad = mid_grad.astype(BF)
    attn_grad = head_grads(branch_grad, gathered, 5 * width)
    if repeat > 1:
        attn_grad = jnp.repeat(attn_grad, repeat, 0)

    hidden_act, normed_two, pre_grad, attn_grad = lax.optimization_barrier(
        (hidden_act, normed_two, pre_grad, attn_grad)
    )
    attn_grad_head = all_to_all(attn_grad)
    grad_bup = jnp.sum(pre_grad.astype(F32), 0)
    up_low, out_low = over_core(normed_two, pre_grad), over_core(attn_low, branch_grad)
    ff_two = mm(hidden_act[:, :width], down_a) + mm(hidden_act[:, width:], down_b)
    layer_out = (
        stream_mid + (ff_two[:tok] + to_peer(ff_two[tok:].astype(BF)).astype(F32)) + bias_down
    ).astype(BF)
    down_low = jnp.concatenate(down_low, 2)
    down_sum = over_x(jnp.stack([at_index(down_low, (spot // 2 + k) % inner, 1) for k in range(inner)]))
    attn_grad_head, down_sum, up_low, out_low, normed_full = lax.optimization_barrier(
        (attn_grad_head, down_sum, up_low, out_low, normed_full)
    )
    down_share = over_z(down_sum)
    up_came, out_came = x_parts(up_low), x_parts(out_low)

    dqkv_packed, flat = attend_back(
        q_all, k_all, v_all, attn_grad_head, attn_t, lse, seg_all, cos_rows, sin_rows
    )
    dqkv_packed, out_came = lax.optimization_barrier((dqkv_packed, out_came))
    down_peer = to_peer(down_share)
    dqkv_back, up_came, down_share, down_peer, layer_out, folded = lax.optimization_barrier(
        (all_to_all(dqkv_packed)[::repeat], up_came, down_share, down_peer, layer_out, qkv_grads(flat, normed_full, blocks))
    )
    shares = over_z(jnp.concatenate([added(up_came), added(out_came)], 2))
    normed_grad = qkv_back(dqkv_back, gathered, 2 * width)
    scaled_in = normed_grad * gain_attn
    grad_gattn = jnp.sum(normed_grad * unit_in, 0)
    in_grad = mid_grad + root_in * (scaled_in - unit_in * jnp.mean(scaled_in * unit_in, -1, keepdims=True))
    in_low = in_grad.astype(BF)
    folded, in_low = lax.optimization_barrier((all_to_all(folded)[::repeat], in_low))
    frames_grad, skip_grad = merge_pieces(mm_nt(in_low, skip_a), mm_nt(in_low, skip_b), blocks, BF)
    extra = [grad_gattn, grad_gff, jnp.sum(out_grad.astype(F32), 0)] + list(grad_bup.reshape(2, width))
    extra = jnp.pad(jnp.stack(extra).astype(BF), ((0, 11), (0, 0)))
    tail = jnp.concatenate([in_low, extra], 0)
    tails, (frames_grad, skip_grad, folded) = plane_blocks(tail[None], (frames_grad, skip_grad, folded))
    qkv_share = unpack_heads(folded)
    if packs > 2:
        qkv_share = over_pairs(qkv_share.astype(F32)).astype(BF)
    qkv_peer = to_peer(qkv_share)
    tails = tails.reshape(plane, tok + 16, width)
    low_all = tails[:, :tok].reshape(plane * tok, width)
    skip_part = mm_tn(joined, low_all).astype(BF).reshape(planes, 2 * rows, width)
    vec = jnp.sum(tails[:, tok : tok + 5].astype(F32), 0)
    vec = jnp.concatenate([jnp.sum(low_all.astype(F32), 0)[None], vec], 0)
    vec = jnp.pad(vec.astype(BF), ((0, 10), (0, 0)))
    payload = jnp.concatenate([skip_part, jnp.broadcast_to(vec[None], (planes, 16, width))], 1)
    payload, shares = lax.optimization_barrier((payload, shares))
    others = to_peer(shares)
    summed = at_index(payload, place).astype(F32)
    came = [send(at_index(payload, (place + k) % planes), along_z(k)) for k in range(1, planes)]
    came, qkv_peer, others = lax.optimization_barrier((came, qkv_peer, others))
    for block in came:
        summed = summed + block.astype(F32)
    if packs > 2:
        summed = over_pairs(summed)
    summed_peer = to_peer(summed.astype(BF)).astype(F32)
    total = summed + summed_peer
    w_skip_grad = total[: 2 * rows]
    own = lax.dynamic_slice_in_dim(total[2 * rows :], me * rows, rows, 1)
    b_up_grad = both(
        lax.dynamic_slice_in_dim(summed[2 * rows + 4 : 2 * rows + 6], me * rows, rows, 1),
        lax.dynamic_slice_in_dim(summed_peer[2 * rows + 4 : 2 * rows + 6], me * rows, rows, 1),
    ).reshape(4 * rows)
    w_qkv_grad = qkv_share.astype(F32) + qkv_peer.astype(F32)

    w_up_grad = up_columns(mine, shares[:, : 2 * width], others[:, : 2 * width], blocks)
    shares, others = shares[:, 2 * width :].astype(F32), others[:, 2 * width :].astype(F32)
    w_out_grad = shares + others
    w_down_grad = both(down_share, down_peer).reshape(4 * rows, width).astype(F32)
    return (
        layer_out, frames_grad, skip_grad, w_skip_grad, own[0], own[1], w_qkv_grad, w_out_grad, own[2],
        w_up_grad, b_up_grad, w_down_grad, own[3],
    )


def solution(mesh):
    token_spec = P(("pack", "blk"), None)
    matrix, vector = P("blk", None), P("blk")
    return jax.shard_map(
        local,
        mesh=mesh,
        in_specs=(
            token_spec, token_spec, P("pack", None), matrix, vector, vector, matrix, matrix, vector, matrix, vector,
            matrix, vector, token_spec,
        ),
        out_specs=(
            token_spec, token_spec, token_spec, matrix, vector, vector, matrix, matrix, vector, matrix, vector, matrix,
            vector,
        ),
        check_vma=False,
    )
```

```python
import functools
import math

import jax
import jax.numpy as jnp
from jax import lax
from jax.experimental import pallas as pl
from jax.experimental.pallas import tpu as pltpu
from jax.sharding import PartitionSpec as P

H = 16
HD = 64
EPSILON = 1e-06
MASKED_SCORE = -1e30
SCORES = 2048 * 2048
QKV = 1024
VMEM = 56 * 1024 * 1024
BF = jnp.bfloat16
F32 = jnp.float32


def mm(left, right):
    return jnp.dot(left, right, preferred_element_type=F32)


def mm_nt(left, right):
    return lax.dot_general(left, right, (((1,), (1,)), ((), ())), preferred_element_type=F32)


def mm_tn(left, right):
    return lax.dot_general(left, right, (((0,), (0,)), ((), ())), preferred_element_type=F32)


def whole(shape):
    return pl.BlockSpec(shape, lambda *_: (0,) * len(shape))


def segment_of(position, lengths_row):
    bounds = jnp.cumsum(lengths_row)
    after = position[:, None] >= bounds[None, :]
    segment = jnp.sum(after.astype(jnp.int32), 1, dtype=jnp.int32)
    before = jnp.sum(jnp.where(after, lengths_row[None, :], 0), 1, dtype=jnp.int32)
    return segment, position - before


def angles(offset):
    freq = 10000.0 ** (-(jnp.arange(HD // 2, dtype=F32) * 2.0 / HD))
    angle = offset.astype(F32)[:, None] * freq[None, :]
    return jnp.cos(angle), jnp.sin(angle)


def activation(value):
    return jax.nn.gelu(value, approximate=True)


def pack_pair(block, lane_low):
    half = block.shape[0] // 2
    top, bottom = block[:half], block[half:]
    even = jnp.where(lane_low, top, pltpu.roll(bottom, HD, 1))
    odd = jnp.where(lane_low, pltpu.roll(top, HD, 1), bottom)
    return even, odd


def qkv_kernel(normed_ref, weight_ref, cos_ref, sin_ref, out_ref):
    step = pl.program_id(0)
    projected = mm(normed_ref[...], weight_ref[...])
    rows = projected.shape[0]
    lane = lax.broadcasted_iota(jnp.int32, (rows, 128), 1)
    first = (lane % HD) < HD // 2
    lane_low = lane[: rows // 2] < HD
    per_part = normed_ref.shape[1] // QKV
    scale = jnp.where(step < per_part, 1.0 / math.sqrt(HD), 1.0)
    for pair in range(QKV // 128):
        block = projected[:, pair * 128 : pair * 128 + 128]
        swapped = jnp.where(first, pltpu.roll(block, 128 - HD // 2, 1), pltpu.roll(block, HD // 2, 1))
        block = jnp.where(step < 2 * per_part, block * cos_ref[...] + swapped * sin_ref[...], block)
        even, odd = pack_pair(block.astype(BF).astype(F32) * scale, lane_low)
        out_ref[2 * pair, 0] = even.astype(BF)
        out_ref[2 * pair + 1, 0] = odd.astype(BF)


def qkv_rows(normed, gathered, at, cos_pair, sin_pair):
    rows, width = normed.shape
    return pl.pallas_call(
        qkv_kernel,
        grid=(3 * width // QKV,),
        in_specs=[
            whole(normed.shape), pl.BlockSpec((width, QKV), lambda i: (0, at // QKV + i)), whole((rows, 128)),
            whole((rows, 128)),
        ],
        out_specs=pl.BlockSpec((QKV // HD, 1, rows // 2, 128), lambda i: (i % (width // QKV), i // (width // QKV), 0, 0)),
        out_shape=jax.ShapeDtypeStruct((H, 3, rows // 2, 128), BF),
        compiler_params=pltpu.CompilerParams(vmem_limit_bytes=VMEM),
        name="qkv_rows",
    )(normed, gathered, cos_pair, sin_pair)


def qkv_back_kernel(grad_ref, weight_ref, out_ref, rows_s, total_s):
    half = grad_ref.shape[2]
    lane_low = lax.broadcasted_iota(jnp.int32, (half, 128), 1) < HD
    for pair in range(QKV // 128):
        even, odd = grad_ref[2 * pair, 0].astype(F32), grad_ref[2 * pair + 1, 0].astype(F32)
        at = pair * 128
        rows_s[:half, at : at + 128] = jnp.where(lane_low, even, pltpu.roll(odd, HD, 1)).astype(BF)
        rows_s[half:, at : at + 128] = jnp.where(lane_low, pltpu.roll(even, HD, 1), odd).astype(BF)
    product = mm_nt(weight_ref[...], rows_s[...])

    @pl.when(pl.program_id(0) == 0)
    def _():
        total_s[...] = product

    @pl.when(pl.program_id(0) > 0)
    def _():
        total_s[...] += product

    @pl.when(pl.program_id(0) == pl.num_programs(0) - 1)
    def _():
        out_ref[...] = jnp.transpose(total_s[...])


def qkv_back(grads, gathered, at):
    half = grads.shape[2]
    width = gathered.shape[0]
    return pl.pallas_call(
        qkv_back_kernel,
        grid=(3 * width // QKV,),
        in_specs=[
            pl.BlockSpec((QKV // HD, 1, half, 128), lambda i: (i % (width // QKV), i // (width // QKV), 0, 0)),
            pl.BlockSpec((width, QKV), lambda i: (0, at // QKV + i)),
        ],
        out_specs=whole((2 * half, width)),
        out_shape=jax.ShapeDtypeStruct((2 * half, width), F32),
        scratch_shapes=[pltpu.VMEM((2 * half, QKV), BF), pltpu.VMEM((width, 2 * half), F32)],
        compiler_params=pltpu.CompilerParams(vmem_limit_bytes=VMEM),
        name="qkv_back",
    )(grads, gathered)


def head_grad_kernel(branch_ref, weight_ref, out_ref):
    grad = jnp.transpose(mm_nt(weight_ref[...], branch_ref[...])).astype(BF).astype(F32)
    lane_low = lax.broadcasted_iota(jnp.int32, (grad.shape[0] // 2, 128), 1) < HD
    for pair in range(grad.shape[1] // 128):
        even, odd = pack_pair(grad[:, pair * 128 : pair * 128 + 128], lane_low)
        out_ref[2 * pair] = even.astype(BF)
        out_ref[2 * pair + 1] = odd.astype(BF)


def head_grads(branch, gathered, at):
    rows, width = branch.shape
    step = 8 * HD
    return pl.pallas_call(
        head_grad_kernel,
        grid=(width // step,),
        in_specs=[whole(branch.shape), pl.BlockSpec((step, width), lambda i: (i, at // width))],
        out_specs=pl.BlockSpec((step // HD, rows // 2, 128), lambda i: (i, 0, 0)),
        out_shape=jax.ShapeDtypeStruct((H, rows // 2, 128), BF),
        compiler_params=pltpu.CompilerParams(vmem_limit_bytes=VMEM),
        name="head_grads",
    )(branch, gathered)


def unpack_kernel(in_ref, out_ref):
    parts, half = in_ref.shape[1], in_ref.shape[2]
    lane_low = lax.broadcasted_iota(jnp.int32, (half, 128), 1) < HD
    for part in range(parts):
        for pair in range(H // 2):
            even = in_ref[2 * pair, part].astype(F32)
            odd = in_ref[2 * pair + 1, part].astype(F32)
            top = jnp.where(lane_low, even, pltpu.roll(odd, HD, 1))
            bottom = jnp.where(lane_low, pltpu.roll(even, HD, 1), odd)
            at = (part * H + 2 * pair) * HD
            out_ref[:half, at : at + 128] = top.astype(BF)
            out_ref[half:, at : at + 128] = bottom.astype(BF)


def unpack_heads(packed):
    _, parts, half, _ = packed.shape
    return pl.pallas_call(
        unpack_kernel,
        out_shape=jax.ShapeDtypeStruct((2 * half, parts * H * HD), BF),
        compiler_params=pltpu.CompilerParams(vmem_limit_bytes=VMEM),
        name="unpack_heads",
    )(packed)


def lanes(top, bottom):
    low = lax.broadcasted_iota(jnp.int32, top.shape, 1) < HD
    return jnp.where(low, top, pltpu.roll(bottom, HD, 1)), jnp.where(low, pltpu.roll(top, HD, 1), bottom)


def split_kernel(left_ref, right_ref, out_ref):
    pairs = left_ref.shape[1] // 256
    for half, ref in enumerate((left_ref, right_ref)):
        for pair in range(pairs):
            at = pair * 256
            first, second = lanes(ref[:, at : at + 128].astype(F32), ref[:, at + 128 : at + 256].astype(F32))
            there = (half * pairs + pair) * 128
            out_ref[0, :, there : there + 128] = first.astype(out_ref.dtype)
            out_ref[1, :, there : there + 128] = second.astype(out_ref.dtype)


def split_pieces(left, right, blocks):
    tok, width = left.shape
    if width // blocks != HD:
        by_piece = jnp.concatenate([left, right], 1).reshape(tok, blocks, 2, width // blocks)
        return jnp.transpose(by_piece, (2, 0, 1, 3)).reshape(2, tok, width)
    return pl.pallas_call(
        split_kernel,
        out_shape=jax.ShapeDtypeStruct((2, tok, width), left.dtype),
        compiler_params=pltpu.CompilerParams(vmem_limit_bytes=VMEM),
        name="split_pieces",
    )(left, right)


def merge_kernel(first_ref, second_ref, left_ref, right_ref):
    pairs = left_ref.shape[1] // 256
    for half, ref in enumerate((left_ref, right_ref)):
        for pair in range(pairs):
            there = (half * pairs + pair) * 128
            even, odd = lanes(
                first_ref[:, there : there + 128].astype(F32), second_ref[:, there : there + 128].astype(F32)
            )
            at = pair * 256
            ref[:, at : at + 128] = even.astype(ref.dtype)
            ref[:, at + 128 : at + 256] = odd.astype(ref.dtype)


def merge_pieces(first, second, blocks, dtype):
    tok, width = first.shape
    if width // blocks != HD:
        both = jnp.stack([first.reshape(tok, blocks, -1), second.reshape(tok, blocks, -1)], 2)
        both = both.reshape(tok, 2 * width).astype(dtype)
        return both[:, :width], both[:, width:]
    return pl.pallas_call(
        merge_kernel,
        out_shape=[jax.ShapeDtypeStruct((tok, width), dtype)] * 2,
        compiler_params=pltpu.CompilerParams(vmem_limit_bytes=VMEM),
        name="merge_pieces",
    )(first, second)


def up_kernel(mine_ref, own_ref, other_ref, out_ref):
    width = own_ref.shape[1] // 2
    first = mine_ref[0] == 0
    for piece in range(2):
        for pair in range(width // 128):
            at = pair * 128
            tiles = []
            for s in range(2):
                own = own_ref[:, s * width + at : s * width + at + 128].astype(F32)
                other = other_ref[:, s * width + at : s * width + at + 128].astype(F32)
                tiles.append(jnp.where(first, own, other) if piece == 0 else jnp.where(first, other, own))
            even, odd = lanes(*tiles)
            out_ref[:, (4 * pair + piece) * 128 : (4 * pair + piece + 1) * 128] = even
            out_ref[:, (4 * pair + 2 + piece) * 128 : (4 * pair + 3 + piece) * 128] = odd


def up_columns(mine, own, other, blocks):
    rows, half = own.shape
    if half // 2 // blocks != HD:
        pair = jnp.where(mine == 0, jnp.stack([own, other]), jnp.stack([other, own]))
        pair = jnp.transpose(pair, (1, 0, 2)).reshape(rows, 4, blocks, half // 2 // blocks)
        return jnp.transpose(pair, (0, 2, 1, 3)).reshape(rows, 2 * half).astype(F32)
    return pl.pallas_call(
        up_kernel,
        in_specs=[pl.BlockSpec(memory_space=pltpu.SMEM), whole((rows, half)), whole((rows, half))],
        out_specs=whole((rows, 2 * half)),
        out_shape=jax.ShapeDtypeStruct((rows, 2 * half), F32),
        compiler_params=pltpu.CompilerParams(vmem_limit_bytes=VMEM),
        name="up_columns",
    )(mine.astype(jnp.int32).reshape(1), own, other)


def parts_kernel(planes, inner, core_ref, left_ref, right_ref, keep_ref, send_ref):
    first = core_ref[0] == 0
    step = pl.program_id(0)
    for z in range(planes):
        at = (step // inner * planes * inner + z * inner + step % inner) * 2 * HD
        grad = mm_tn(left_ref[:, pl.ds(pl.multiple_of(at, 2 * HD), 2 * HD)], right_ref[...])
        top, bottom = grad[:HD], grad[HD:]
        keep_ref[0, z] = jnp.where(first, top, bottom).astype(BF)
        send_ref[0, z] = jnp.where(first, bottom, top).astype(BF)


def grad_parts(left, right, me, planes, inner, rows):
    frames, columns = right.shape
    pieces = left.shape[1] // (planes * inner * 2 * rows)
    core, x = me % 2, me // 2 % inner
    if rows != HD:
        grad = mm_tn(left, right).astype(BF).reshape(pieces, planes, inner, 2, rows, columns)
        grad = jnp.stack([lax.dynamic_index_in_dim(grad, (x + k) % inner, 2, keepdims=False) for k in range(inner)])
        both = [lax.dynamic_index_in_dim(grad, c, 3, keepdims=False) for c in (core, 1 - core)]
        return [jnp.transpose(g, (0, 2, 1, 3, 4)).reshape(inner, planes, pieces * rows, columns) for g in both]

    def place(i, scalars):
        return (i % inner - scalars[1] + inner) % inner, 0, i // inner, 0

    shape = (inner, planes, pieces * rows, columns)
    return pl.pallas_call(
        functools.partial(parts_kernel, planes, inner),
        grid_spec=pltpu.PrefetchScalarGridSpec(
            num_scalar_prefetch=1,
            grid=(pieces * inner,),
            in_specs=[whole(left.shape), whole(right.shape)],
            out_specs=[pl.BlockSpec((1, planes, rows, columns), place)] * 2,
        ),
        out_shape=[jax.ShapeDtypeStruct(shape, BF)] * 2,
        compiler_params=pltpu.CompilerParams(vmem_limit_bytes=VMEM),
        name="grad_parts",
    )(jnp.stack([core, x]).astype(jnp.int32), left, right)


def rotated(rows, cosine, sine):
    swapped = jnp.concatenate([rows[:, HD // 2 :], rows[:, : HD // 2]], 1)
    return rows * cosine + swapped * sine


def put_packed(out_ref, step, rows, half, part=None):
    each = rows.shape[0] // (2 * half)
    for i in range(each):
        block = rows[2 * half * i : 2 * half * (i + 1)]
        joined = jnp.concatenate([block[:half], block[half:]], 1).astype(BF)
        if part is None:
            out_ref[step * each + i] = joined
        else:
            out_ref[step * each + i, part] = joined


def attend_kernel(qkv_ref, segc_ref, segr_ref, out_ref, attn_ref, lse_ref, q_ref, k_ref, v_ref, vt_s):
    g = pl.program_id(0)
    step_rows = SCORES // q_ref.shape[0]
    half = qkv_ref.shape[-2]
    tok = 2 * half

    @pl.when(g == 0)
    def _():
        for i in range(qkv_ref.shape[0]):
            for part, ref in enumerate((q_ref, k_ref, v_ref)):
                block = qkv_ref[i, part].astype(F32)
                ref[i * tok : i * tok + half] = block[:, :HD].astype(BF)
                ref[i * tok + half : (i + 1) * tok] = block[:, HD:].astype(BF)
        vt_s[...] = jnp.transpose(v_ref[...].astype(F32)).astype(BF)

    here = pl.ds(pl.multiple_of(g * step_rows, step_rows), step_rows)
    scores = mm_nt(k_ref[...], q_ref[here])
    allowed = segc_ref[...] == segr_ref[:, here]
    scores = jnp.where(allowed, scores, MASKED_SCORE)
    top = jnp.max(scores, 0, keepdims=True)
    weight = jnp.exp(scores - top)
    total = jnp.sum(weight, 0, keepdims=True)
    attn_t = mm(vt_s[...], weight.astype(BF)) / total
    attn_ref[:, here] = attn_t
    lse_ref[:, here] = top + jnp.log(total)
    put_packed(out_ref, g, jnp.transpose(attn_t), tok // 2)


def attend(qkv, seg):
    blocks, _, half, _ = qkv.shape
    total = blocks * half * 2
    return pl.pallas_call(
        attend_kernel,
        grid=(total // (SCORES // total),),
        in_specs=[whole(qkv.shape), whole((total, 1)), whole((1, total))],
        out_specs=[whole((blocks, half, 128)), whole((HD, total)), whole((1, total))] + [whole((total, HD))] * 3,
        out_shape=[
            jax.ShapeDtypeStruct((blocks, half, 128), BF),
            jax.ShapeDtypeStruct((HD, total), F32),
            jax.ShapeDtypeStruct((1, total), F32),
        ]
        + [jax.ShapeDtypeStruct((total, HD), BF)] * 3,
        scratch_shapes=[pltpu.VMEM((HD, total), BF)],
        compiler_params=pltpu.CompilerParams(vmem_limit_bytes=VMEM),
        cost_estimate=pl.CostEstimate(flops=int(1.6e10), bytes_accessed=8 << 20, transcendentals=0),
        name="attend",
    )(qkv, seg[:, None], seg[None, :])


def attend_back_kernel(
    q_ref, k_ref, v_ref, do_ref, attn_ref, lse_ref, segc_ref, segr_ref, cos_ref, sin_ref,
    out_ref, flat_s, do_s, delta_s, dq_s,
):
    g = pl.program_id(0)
    step_rows = SCORES // q_ref.shape[0]
    blocks = do_ref.shape[0]
    half = do_ref.shape[-2]
    tok = 2 * half
    scale = 1.0 / math.sqrt(HD)

    @pl.when(g == 0)
    def _():
        for i in range(blocks):
            block = do_ref[i].astype(F32)
            do_s[i * tok : i * tok + half] = block[:, :HD].astype(BF)
            do_s[i * tok + half : (i + 1) * tok] = block[:, HD:].astype(BF)
        do_t = jnp.transpose(do_s[...].astype(F32))
        delta_s[...] = jnp.sum(do_t * attn_ref[...], 0, keepdims=True)
        dq_s[...] = jnp.zeros_like(dq_s)

    here = pl.ds(pl.multiple_of(g * step_rows, step_rows), step_rows)
    keys = k_ref[here]
    scores = mm_nt(keys, q_ref[...])
    allowed = segc_ref[here] == segr_ref[...]
    probs = jnp.where(allowed, jnp.exp(scores - lse_ref[...]), 0.0)
    prob_grad = mm_nt(v_ref[here], do_s[...])
    score_grad = (probs * (prob_grad - delta_s[...])).astype(BF)
    value_grad = mm(probs.astype(BF), do_s[...])
    key_grad = mm(score_grad, q_ref[...])
    keys_t = jnp.transpose(keys.astype(F32)).astype(BF)
    dq_s[...] += mm(keys_t, score_grad)

    def put(part, step, rows, where):
        flat_s[part * HD : (part + 1) * HD, where] = jnp.transpose(rows).astype(BF)
        put_packed(out_ref, step, rows, half, part)

    put(1, g, rotated(key_grad, cos_ref[here], sin_ref[here]), here)
    put(2, g, value_grad, here)

    @pl.when(g == pl.num_programs(0) - 1)
    def _():
        for step in range(q_ref.shape[0] // step_rows):
            there = slice(step * step_rows, (step + 1) * step_rows)
            rows = jnp.transpose(dq_s[:, there]) * scale
            put(0, step, rotated(rows, cos_ref[there], sin_ref[there]), there)


def qkv_grad_kernel(flat_ref, normed_ref, grad_ref):
    blocks = grad_ref.shape[0]
    grad = jnp.transpose(mm(flat_ref[...], normed_ref[...]))
    rows = grad.shape[0] // blocks
    for i in range(blocks):
        for part in range(3):
            block = grad[i * rows : (i + 1) * rows, part * HD : (part + 1) * HD]
            grad_ref[i, part] = jnp.concatenate([block[: rows // 2], block[rows // 2 :]], 1).astype(BF)


def qkv_grads(flat, normed, blocks):
    rows = normed.shape[1] // blocks
    return pl.pallas_call(
        qkv_grad_kernel,
        out_shape=jax.ShapeDtypeStruct((blocks, 3, rows // 2, 128), BF),
        compiler_params=pltpu.CompilerParams(vmem_limit_bytes=VMEM),
        name="qkv_grads",
    )(flat, normed)


def attend_back(q, k, v, attn_grad, attn_t, lse, seg, cos_rows, sin_rows):
    total = q.shape[0]
    blocks, half, _ = attn_grad.shape
    return pl.pallas_call(
        attend_back_kernel,
        grid=(total // (SCORES // total),),
        in_specs=[whole((total, HD))] * 3
        + [whole((blocks, half, 128)), whole((HD, total)), whole((1, total))]
        + [whole((total, 1)), whole((1, total)), whole((total, HD)), whole((total, HD))],
        out_specs=[whole((blocks, 3, half, 128)), whole((3 * HD, total))],
        out_shape=[
            jax.ShapeDtypeStruct((blocks, 3, half, 128), BF),
            jax.ShapeDtypeStruct((3 * HD, total), BF),
        ],
        scratch_shapes=[
            pltpu.VMEM((total, HD), BF),
            pltpu.VMEM((1, total), F32),
            pltpu.VMEM((HD, total), F32),
        ],
        compiler_params=pltpu.CompilerParams(vmem_limit_bytes=VMEM),
        cost_estimate=pl.CostEstimate(flops=int(2.4e10), bytes_accessed=8 << 20, transcendentals=0),
        name="attend_back",
    )(q, k, v, attn_grad, attn_t, lse, seg[:, None], seg[None, :], cos_rows, sin_rows)


def local(
    frames, skip_input, lengths, w_skip, b_skip, g_attn, w_qkv, w_out, g_ff, w_up, b_up, w_down, b_down, out_grad
):
    tok, width = frames.shape
    blocks = lax.axis_size("blk")
    packs = lax.axis_size("pack")
    me = lax.axis_index("blk")
    mine = lax.axis_index("pack") % 2
    rows = width // blocks
    repeat = blocks // H
    half = tok // 2
    planes = 4
    plane = blocks // planes
    spot = me % plane
    place = me // plane
    plane_groups = [[z * plane + j for j in range(plane)] for z in range(planes)]
    column_groups = [[z * plane + j for z in range(planes)] for j in range(plane)]
    swap = [(i, i ^ 1) for i in range(packs)]

    def to_peer(block):
        return lax.ppermute(block, "pack", swap)

    def over_pairs(block):
        total = block
        for k in range(1, packs // 2):
            total = total + lax.ppermute(block, "pack", [(i, (i + 2 * k) % packs) for i in range(packs)])
        return total

    def all_to_all(block, groups=None):
        return lax.all_to_all(block, "blk", 0, 0, tiled=True, axis_index_groups=groups)

    inner = plane // 2
    core = [(i, i ^ 1) for i in range(blocks)]

    def along_z(k):
        return [(i, (i + plane * k) % blocks) for i in range(blocks)]

    def along_x(k):
        return [(i, (i // plane) * plane + ((i % plane) // 2 + k) % inner * 2 + i % 2) for i in range(blocks)]

    def send(block, route):
        return lax.ppermute(block, "blk", route)

    def plane_blocks(block, beside=()):
        column = [block] + [send(block, along_x(k)) for k in range(1, inner)]
        if inner > 1:
            column = jnp.stack(column)
        else:
            column = column[0][None]
        column, beside = lax.optimization_barrier((column, beside))
        return jnp.concatenate([column, send(column, core)], 0), beside

    def plane_sources():
        return [(spot // 2 - k) % inner * 2 + ((spot % 2) ^ c) for c in range(2) for k in range(inner)]

    def own_half(block, axis):
        size = block.shape[axis] // 2
        return lax.dynamic_slice_in_dim(block, mine * size, size, axis)

    def at_index(block, index, axis=0):
        return lax.dynamic_index_in_dim(block, index, axis, keepdims=False)

    vectors = jnp.stack([b_skip, g_attn, g_ff, b_down] + list(b_up.reshape(4, rows)), 0)
    vectors = jnp.transpose(jnp.pad(vectors, ((0, 120), (0, 0))))
    up_cols = jnp.transpose(w_up.reshape(rows, blocks, 4, rows), (0, 2, 1, 3)).reshape(rows, 2, 2 * width)
    up_mine = at_index(up_cols, mine, 1)
    down_mine = own_half(w_down, 0)
    payload = jnp.concatenate(
        [w_skip[:rows], w_skip[rows:], w_qkv, w_out, up_mine, down_mine[:rows], down_mine[rows:], vectors], 1
    )
    gathered = lax.all_gather(payload, "blk", axis=0, tiled=True)

    pack_lengths = lengths[0]
    seg_all, offset_all = segment_of(jnp.arange(tok * blocks, dtype=jnp.int32), pack_lengths)
    cos_all, sin_all = angles(offset_all)
    cos_rows = jnp.concatenate([cos_all, cos_all], 1)
    sin_rows = jnp.concatenate([sin_all, -sin_all], 1)
    cosine = lax.dynamic_slice_in_dim(cos_all, me * tok, tok, 0)
    sine = lax.dynamic_slice_in_dim(sin_all, me * tok, tok, 0)
    cos_pair = jnp.concatenate([cosine] * 4, 1)
    sin_pair = jnp.concatenate([-sine, sine, -sine, sine], 1)
    pieces = split_pieces(frames, skip_input, blocks)
    gathered, pieces, cos_rows, sin_rows, cos_pair, sin_pair, seg_all = lax.optimization_barrier(
        (gathered, pieces, cos_rows, sin_rows, cos_pair, sin_pair, seg_all)
    )
    skip_a, skip_b = gathered[:, :width], gathered[:, width : 2 * width]
    gathered_more = gathered[:, 5 * width :]
    small = jnp.transpose(gathered[:, 10 * width :].astype(F32))[:8]
    bias_skip, gain_attn, gain_ff, bias_down = small[0], small[1], small[2], small[3]
    bias_up = lax.dynamic_slice_in_dim(small, 4 + 2 * mine, 2, 0).reshape(2 * width)

    def over_core(left, right):
        keep, other = grad_parts(left, right, me, planes, inner, rows)
        return (keep.astype(F32) + send(other, core).astype(F32)).astype(BF)

    def over_x(grad):
        total = grad[0].astype(F32)
        for k in range(1, inner):
            total = total + send(grad[k], along_x(k)).astype(F32)
        return total.astype(BF)

    def x_parts(grad):
        return [grad[0]] + [send(grad[k], along_x(k)) for k in range(1, inner)]

    def added(parts):
        return sum(part.astype(F32) for part in parts).astype(BF)

    def over_z(grad):
        total = lax.psum_scatter(
            grad.reshape(planes * grad.shape[1], grad.shape[2]),
            "blk",
            scatter_dimension=0,
            axis_index_groups=column_groups,
            tiled=True,
        )
        return over_pairs(total.astype(F32)).astype(BF) if packs > 2 else total

    def both(own, other):
        return jnp.where(mine == 0, jnp.stack([own, other]), jnp.stack([other, own]))

    stream_in = mm(pieces[0], skip_a) + mm(pieces[1], skip_b) + bias_skip
    root_in = lax.rsqrt(jnp.mean(stream_in * stream_in, -1, keepdims=True) + EPSILON)
    unit_in = stream_in * root_in
    normed_attn = (unit_in * gain_attn).astype(BF)
    qkv_packed = qkv_rows(normed_attn, gathered, 2 * width, cos_pair, sin_pair)
    if repeat > 1:
        qkv_packed = jnp.repeat(qkv_packed, repeat, 0)
    qkv_packed, grad_sent = lax.optimization_barrier((qkv_packed, out_grad))
    out_grad_two = jnp.concatenate([out_grad, to_peer(grad_sent)], 0)
    qkv_head, frames_late, skip_late = lax.optimization_barrier((all_to_all(qkv_packed), frames, skip_input))
    joined = jnp.concatenate([frames_late, skip_late], 1).reshape(tok, planes, plane, 2 * rows)
    joined = all_to_all(jnp.transpose(joined, (2, 0, 1, 3)).reshape(plane, tok, planes * 2 * rows), plane_groups)
    joined = jnp.concatenate([at_index(joined, source) for source in plane_sources()], 0)
    attn_packed, attn_t, lse, q_all, k_all, v_all = attend(qkv_head, seg_all)
    attn_packed, joined = lax.optimization_barrier((attn_packed, joined))
    attn_back = all_to_all(attn_packed)[::repeat]
    attn_back, normed_late, out_grad_two = lax.optimization_barrier((attn_back, normed_attn, out_grad_two))
    normed_full = lax.all_gather(normed_late, "blk", axis=0, tiled=True)
    attn_low = unpack_heads(attn_back[:, None])
    out_full = gathered_more[:, :width]
    up_half = gathered_more[:, width : 3 * width]
    down_a, down_b = gathered_more[:, 3 * width : 4 * width], gathered_more[:, 4 * width : 5 * width]
    stream_mid = stream_in + mm(attn_low, out_full)
    root_mid = lax.rsqrt(jnp.mean(stream_mid * stream_mid, -1, keepdims=True) + EPSILON)
    unit_mid = stream_mid * root_mid
    normed_ff = (unit_mid * gain_ff).astype(BF)
    normed_two = jnp.concatenate([normed_ff, to_peer(normed_ff)], 0)
    hidden_pre = mm(normed_two, up_half) + bias_up
    act_grad = jnp.concatenate([mm_nt(out_grad_two, down_a), mm_nt(out_grad_two, down_b)], 1)
    hidden, gelu_back = jax.vjp(activation, hidden_pre)
    hidden_act = hidden.astype(BF)
    pre_grad = gelu_back(act_grad)[0].astype(BF)
    ff_grad_two = mm_nt(pre_grad, up_half)
    ff_came = to_peer(ff_grad_two[tok:].astype(BF))
    down_low = [mm_tn(hidden_act[:, i * width : (i + 1) * width], out_grad_two).astype(BF) for i in range(2)]
    down_low = [low.reshape(planes, inner, 2, rows, width) for low in down_low]
    down_low = [
        (at_index(low, me % 2, 2).astype(F32) + send(at_index(low, 1 - me % 2, 2), core).astype(F32)).astype(BF)
        for low in down_low
    ]
    ff_came, down_low = lax.optimization_barrier((ff_came, down_low))
    ff_grad = ff_grad_two[:tok] + ff_came.astype(F32)

    scaled = ff_grad * gain_ff
    grad_gff = jnp.sum(ff_grad * unit_mid, 0)
    mid_grad = out_grad.astype(F32) + root_mid * (scaled - unit_mid * jnp.mean(scaled * unit_mid, -1, keepdims=True))
    branch_grad = mid_grad.astype(BF)
    attn_grad = head_grads(branch_grad, gathered, 5 * width)
    if repeat > 1:
        attn_grad = jnp.repeat(attn_grad, repeat, 0)

    hidden_act, normed_two, pre_grad, attn_grad = lax.optimization_barrier(
        (hidden_act, normed_two, pre_grad, attn_grad)
    )
    attn_grad_head = all_to_all(attn_grad)
    grad_bup = jnp.sum(pre_grad.astype(F32), 0)
    up_low, out_low = over_core(normed_two, pre_grad), over_core(attn_low, branch_grad)
    ff_two = mm(hidden_act[:, :width], down_a) + mm(hidden_act[:, width:], down_b)
    layer_out = (
        stream_mid + (ff_two[:tok] + to_peer(ff_two[tok:].astype(BF)).astype(F32)) + bias_down
    ).astype(BF)
    down_low = jnp.concatenate(down_low, 2)
    down_sum = over_x(jnp.stack([at_index(down_low, (spot // 2 + k) % inner, 1) for k in range(inner)]))
    attn_grad_head, down_sum, up_low, out_low, normed_full = lax.optimization_barrier(
        (attn_grad_head, down_sum, up_low, out_low, normed_full)
    )
    down_share = over_z(down_sum)
    up_came, out_came = x_parts(up_low), x_parts(out_low)

    dqkv_packed, flat = attend_back(
        q_all, k_all, v_all, attn_grad_head, attn_t, lse, seg_all, cos_rows, sin_rows
    )
    dqkv_packed, out_came = lax.optimization_barrier((dqkv_packed, out_came))
    down_peer = to_peer(down_share)
    dqkv_back, up_came, down_share, down_peer, layer_out, folded = lax.optimization_barrier(
        (all_to_all(dqkv_packed)[::repeat], up_came, down_share, down_peer, layer_out, qkv_grads(flat, normed_full, blocks))
    )
    shares = over_z(jnp.concatenate([added(up_came), added(out_came)], 2))
    normed_grad = qkv_back(dqkv_back, gathered, 2 * width)
    scaled_in = normed_grad * gain_attn
    grad_gattn = jnp.sum(normed_grad * unit_in, 0)
    in_grad = mid_grad + root_in * (scaled_in - unit_in * jnp.mean(scaled_in * unit_in, -1, keepdims=True))
    in_low = in_grad.astype(BF)
    folded, in_low = lax.optimization_barrier((all_to_all(folded)[::repeat], in_low))
    frames_grad, skip_grad = merge_pieces(mm_nt(in_low, skip_a), mm_nt(in_low, skip_b), blocks, BF)
    extra = [grad_gattn, grad_gff, jnp.sum(out_grad.astype(F32), 0)] + list(grad_bup.reshape(2, width))
    extra = jnp.pad(jnp.stack(extra).astype(BF), ((0, 11), (0, 0)))
    tail = jnp.concatenate([in_low, extra], 0)
    tails, (frames_grad, skip_grad, folded) = plane_blocks(tail[None], (frames_grad, skip_grad, folded))
    qkv_share = unpack_heads(folded)
    if packs > 2:
        qkv_share = over_pairs(qkv_share.astype(F32)).astype(BF)
    qkv_peer = to_peer(qkv_share)
    tails = tails.reshape(plane, tok + 16, width)
    low_all = tails[:, :tok].reshape(plane * tok, width)
    skip_part = mm_tn(joined, low_all).astype(BF).reshape(planes, 2 * rows, width)
    vec = jnp.sum(tails[:, tok : tok + 5].astype(F32), 0)
    vec = jnp.concatenate([jnp.sum(low_all.astype(F32), 0)[None], vec], 0)
    vec = jnp.pad(vec.astype(BF), ((0, 10), (0, 0)))
    payload = jnp.concatenate([skip_part, jnp.broadcast_to(vec[None], (planes, 16, width))], 1)
    payload, shares = lax.optimization_barrier((payload, shares))
    others = to_peer(shares)
    summed = at_index(payload, place).astype(F32)
    came = [send(at_index(payload, (place + k) % planes), along_z(k)) for k in range(1, planes)]
    came, qkv_peer, others = lax.optimization_barrier((came, qkv_peer, others))
    for block in came:
        summed = summed + block.astype(F32)
    if packs > 2:
        summed = over_pairs(summed)
    summed_peer = to_peer(summed.astype(BF)).astype(F32)
    total = summed + summed_peer
    w_skip_grad = total[: 2 * rows]
    own = lax.dynamic_slice_in_dim(total[2 * rows :], me * rows, rows, 1)
    b_up_grad = both(
        lax.dynamic_slice_in_dim(summed[2 * rows + 4 : 2 * rows + 6], me * rows, rows, 1),
        lax.dynamic_slice_in_dim(summed_peer[2 * rows + 4 : 2 * rows + 6], me * rows, rows, 1),
    ).reshape(4 * rows)
    w_qkv_grad = qkv_share.astype(F32) + qkv_peer.astype(F32)

    w_up_grad = up_columns(mine, shares[:, : 2 * width], others[:, : 2 * width], blocks)
    shares, others = shares[:, 2 * width :].astype(F32), others[:, 2 * width :].astype(F32)
    w_out_grad = shares + others
    w_down_grad = both(down_share, down_peer).reshape(4 * rows, width).astype(F32)
    return (
        layer_out, frames_grad, skip_grad, w_skip_grad, own[0], own[1], w_qkv_grad, w_out_grad, own[2],
        w_up_grad, b_up_grad, w_down_grad, own[3],
    )


def solution(mesh):
    token_spec = P(("pack", "blk"), None)
    matrix, vector = P("blk", None), P("blk")
    return jax.shard_map(
        local,
        mesh=mesh,
        in_specs=(
            token_spec, token_spec, P("pack", None), matrix, vector, vector, matrix, matrix, vector, matrix, vector,
            matrix, vector, token_spec,
        ),
        out_specs=(
            token_spec, token_spec, token_spec, matrix, vector, vector, matrix, matrix, vector, matrix, vector, matrix,
            vector,
        ),
        check_vma=False,
    )
```
